32 devices in a mesh: groups: 2 (over x), nodes: 16 (over z, y, core).
Axes of the slice: x: 2, y: 2, z: 4, core: 2. Of those that a mesh axis runs over, the one named last changes fastest.
Arguments:
- grid_in: bfloat16 [131072, 227], P(('groups', 'nodes')), parts along dimension 0, may hold values from -6 to 6
- w_embed: bfloat16 [227, 512], replicated, may hold values from -0.375 to 0.375
- enc_coef: bfloat16 [6144, 32, 128], P('nodes'), may hold values from -0.125 to 0.125
- enc_owner: int32 [6144], P('nodes'), may hold values from 0 to 15, as said below
- slot_block: int32 [256], P('nodes'), may hold values from 0 to 3
- mesh_in: bfloat16 [4096, 512], P(('groups', 'nodes')), parts along dimension 0, may hold values from -6 to 6
- w_enc: bfloat16 [512, 512], replicated, may hold values from -0.25 to 0.25
- proc_adj: int32 [64, 6], P('nodes'), may hold values from -1 to 63, as said below
- proc_coef: bfloat16 [64, 6, 32, 32], P('nodes'), may hold values from -0.4375 to 0.4375
- proc_gain: float32 [512], replicated, may hold values from 0.1 to 1.9
- w_proc: bfloat16 [512, 512], replicated, may hold values from -0.25 to 0.25
- dec_coef: bfloat16 [6144, 128, 32], P('nodes'), may hold values from -0.3125 to 0.3125
- w_out: bfloat16 [512, 227], replicated, may hold values from -0.25 to 0.25
Outputs:
- grid_pred: bfloat16 [131072, 227], P(('groups', 'nodes')), parts along dimension 0
- mesh_out: bfloat16 [4096, 512], P(('groups', 'nodes')), parts along dimension 0
The draws below stay inside these ranges and needn't reach their ends.
There are 2 independent parts, one for each index of `groups`. The reference program is written for one: setup_inputs(seed, part) draws one part's arguments, and reference() takes and returns one part's arrays. A program takes and returns all parts, laid end to end along the dimension named above; an argument that names none is the same for every part. Nothing has to cross between parts.
Inputs may be any that keep to these rules, and one draw needn't show every extreme that they name: `proc_adj`: each row lists between 2 and 6 neighbour blocks first, then -1 padding; a listed block belongs to the row's own partition or to one of the two partitions beside it, the first and last partition being beside each other. `enc_owner`: A tile of partition p feeds partition (p + d) mod 16 for some d of -2 to 2, or d = 8.
All inputs are finite; a program needn't handle non-finite values.
Results may differ from the reference program's by a relative error of at most 0.0075.
Values may be sent and summed in bfloat16 or wider, within the bound.
No kernel may reach another device: no remote copies, remote signals or barrier semaphores. Data moves between devices by JAX's collectives and lax.ppermute only.
A program may use at most 128 MiB of HBM per device.

```python
import jax
import jax.numpy as jnp
from jax import lax

L = 512
C = 227
GP_DEV = 4096
BG = 128
BM = 32
TPG = 12
ADJ = 6
GB_DEV = 32
TE_DEV = 384
BPD = 4
GRID = 65536
MESH = 2048
MB_TOTAL = 64
TILES = 6144
N_NODES = 16


def draw_proc_adj(key, part):
    key = jax.random.fold_in(key, 7)
    key_step, key_block, key_live = jax.random.split(key, 3)
    block_rows = jnp.arange(MB_TOTAL, dtype=jnp.int32)
    owners = block_rows // BPD
    offsets = jax.random.randint(key_step, (MB_TOTAL, ADJ), -1, 2)
    within = jax.random.randint(key_block, (MB_TOTAL, ADJ), 0, BPD)
    targets = (owners[:, None] + offsets) % N_NODES * BPD + within
    live_count = jax.random.randint(key_live, (MB_TOTAL, 1), 2, ADJ + 1)
    positions = jnp.arange(ADJ, dtype=jnp.int32)[None, :]
    return jnp.where(positions < live_count, targets, -1).astype(jnp.int32)


def draw_enc_owner(key, part):
    key = jax.random.fold_in(key, 11)
    tile_rows = jnp.arange(TILES, dtype=jnp.int32)
    home = tile_rows // TE_DEV
    local_tile = tile_rows % TE_DEV
    offsets = jax.random.randint(key, (TILES,), -2, 3)
    offsets = jnp.where(local_tile < TPG, N_NODES // 2, offsets)
    return ((home + offsets) % N_NODES).astype(jnp.int32)


def touch_ends(result, rng, low, top_value):
    longest = result.shape.index(max(result.shape))
    spots = []
    for shift in (0, 1):
        where = [jax.random.randint(jax.random.fold_in(rng, axis), (), 0, length) for axis, length in enumerate(result.shape)]
        where[longest] = (where[longest] + shift) % result.shape[longest]
        spots.append(tuple(where))
    return result.at[spots[0]].set(low).at[spots[1]].set(top_value)


def steps_of(own_key, extent, cuts, least, high):
    gain = 1.0
    for axis_at, blocks in cuts:
        heights = jax.random.uniform(jax.random.fold_in(jax.random.fold_in(own_key, 6), axis_at), (blocks,), jnp.float32, least / len(cuts), high / len(cuts))
        gain = gain * jnp.repeat(jnp.exp(heights), extent[axis_at] // blocks).reshape((-1,) + (1,) * (len(extent) - 1 - axis_at))
    return gain


def gaussian(stream_key, extent, deviation, reach, pieces=(), held_as=jnp.bfloat16):
    values = jax.random.normal(stream_key, extent, jnp.float32) * deviation
    if len(pieces) > 0:
        values = steps_of(stream_key, extent, pieces, -0.22, 0.18) * values
    return jnp.clip(values, min=-reach, max=reach).astype(held_as)


def setup_inputs(seed: int = 0, part: int = 0) -> dict:
    splits = jax.random.split(jax.random.key(seed), 14)
    part_splits = jax.random.split(jax.random.fold_in(splits[13], part), 14)
    grid_in = gaussian(part_splits[0], (GRID, C), 1.0, 6.0, ((0, 16),))
    w_embed = gaussian(splits[1], (C, L), C ** -0.5, 0.375)
    enc_coef = gaussian(splits[2], (TILES, BM, BG), (BG * TE_DEV // (5 * BPD)) ** -0.5, 0.125, ((0, 16),))
    enc_owner = draw_enc_owner(jax.random.fold_in(splits[13], 71), part)
    slot_block = touch_ends(jax.random.randint(splits[4], (N_NODES * N_NODES,), 0, BPD), jax.random.fold_in(splits[4], 1), 0, BPD - 1).astype(jnp.int32)
    mesh_in = gaussian(part_splits[5], (MESH, L), 1.0, 6.0, ((0, 16),))
    w_enc = gaussian(splits[6], (L, L), L ** -0.5, 0.25)
    proc_adj = draw_proc_adj(jax.random.fold_in(splits[13], 71), part)
    proc_coef = gaussian(splits[8], (MB_TOTAL, ADJ, BM, BM), (BM * ADJ) ** -0.5, 0.4375, ((0, 16),))
    proc_gain = jnp.clip(1.0 + 0.18 * jax.random.normal(splits[9], (L,), jnp.float32), 0.1, 1.9)
    w_proc = gaussian(splits[10], (L, L), L ** -0.5, 0.25)
    dec_coef = gaussian(splits[11], (TILES, BG, BM), (BM * TPG) ** -0.5, 0.3125, ((0, 16),))
    w_out = gaussian(splits[12], (L, C), L ** -0.5, 0.25)
    return {"grid_in": grid_in, "w_embed": w_embed, "enc_coef": enc_coef, "enc_owner": enc_owner, "slot_block": slot_block, "mesh_in": mesh_in, "w_enc": w_enc, "proc_adj": proc_adj, "proc_coef": proc_coef, "proc_gain": proc_gain, "w_proc": w_proc, "dec_coef": dec_coef, "w_out": w_out}


def reference(grid_in, w_embed, enc_coef, enc_owner, slot_block, mesh_in, w_enc, proc_adj, proc_coef, proc_gain, w_proc, dec_coef, w_out):
    parts = N_NODES
    grid_parts = grid_in.reshape(parts, GP_DEV, C)
    enc_parts = enc_coef.reshape(parts, GB_DEV, TPG, BM, BG)
    dec_parts = dec_coef.reshape(parts, GB_DEV, TPG, BG, BM)
    owner_parts = enc_owner.reshape(parts, TE_DEV)
    table = slot_block.reshape(parts, parts)
    owner_base = jnp.arange(parts, dtype=jnp.int32) * BPD

    def embed(grid_rows):
        return jax.nn.silu(jnp.dot(grid_rows, w_embed, preferred_element_type=jnp.float32)).astype(jnp.bfloat16)

    def encode(aggregate, inputs):
        grid_rows, coef_part, owners, blocks_row = inputs
        latent_grid = embed(grid_rows).reshape(GB_DEV, BG, L)
        products = jnp.einsum('gkij,gjl->gkil', coef_part.astype(jnp.float32), latent_grid.astype(jnp.float32))
        slot_sums = jnp.zeros((parts, BM, L), jnp.float32).at[owners].add(products.reshape(TE_DEV, BM, L))
        rounded = lax.optimization_barrier(slot_sums.astype(jnp.bfloat16)).astype(jnp.float32)
        targets = (owner_base + blocks_row).astype(jnp.int32)
        return (aggregate.at[targets].add(rounded), None)
    aggregate, _ = lax.scan(encode, jnp.zeros((MB_TOTAL, BM, L), jnp.float32), (grid_parts, enc_parts, owner_parts, table))
    aggregate = aggregate.reshape(MESH, L).astype(jnp.bfloat16)
    mesh_mid = (mesh_in.astype(jnp.float32) + jax.nn.silu(jnp.dot(aggregate, w_enc, preferred_element_type=jnp.float32))).astype(jnp.bfloat16)
    mid_blocks = mesh_mid.reshape(MB_TOTAL, BM, L)

    def passing(inputs):
        adj_rows, coef_rows = inputs
        picked = mid_blocks[jnp.clip(adj_rows, 0, MB_TOTAL - 1)]
        picked = jnp.where((adj_rows >= 0)[:, :, None, None], picked, jnp.zeros_like(picked))
        return jnp.einsum('bakj,bajl->bkl', coef_rows.astype(jnp.float32), picked.astype(jnp.float32))
    message = lax.map(passing, (proc_adj.reshape(parts, BPD, ADJ), proc_coef.reshape(parts, BPD, ADJ, BM, BM)))
    message = message.reshape(MESH, L)
    scale_inv = lax.rsqrt(lax.optimization_barrier(jnp.mean(message * message, axis=-1, keepdims=True)) + 1e-05)
    normed = (message * scale_inv * proc_gain).astype(jnp.bfloat16)
    mesh_out = (mesh_mid.astype(jnp.float32) + jax.nn.silu(jnp.dot(normed, w_proc, preferred_element_type=jnp.float32))).astype(jnp.bfloat16)
    out_blocks = mesh_out.reshape(MB_TOTAL, BM, L)

    def decode(inputs):
        grid_rows, coef_part, owners, blocks_row = inputs
        latent_grid = embed(grid_rows)
        fetched = out_blocks[(owner_base + blocks_row).astype(jnp.int32)]
        per_tile = fetched[owners].reshape(GB_DEV, TPG, BM, L)
        decoded = jnp.einsum('gkij,gkjl->gil', coef_part.astype(jnp.float32), per_tile.astype(jnp.float32))
        hidden_grid = jax.nn.silu(latent_grid.astype(jnp.float32) + decoded.reshape(GP_DEV, L)).astype(jnp.bfloat16)
        return (grid_rows.astype(jnp.float32) + jnp.dot(hidden_grid, w_out, preferred_element_type=jnp.float32)).astype(jnp.bfloat16)
    grid_pred = lax.map(decode, (grid_parts, dec_parts, owner_parts, table)).reshape(GRID, C)
    return (grid_pred, mesh_out)
```

```python
import functools

import jax
import jax.numpy as jnp
from jax import lax
from jax.experimental import pallas as pl
from jax.experimental.pallas import tpu as pltpu
from jax.sharding import PartitionSpec as P

F32 = jnp.float32
BF16 = jnp.bfloat16
SLOTS = 6
MIB = 1 << 20


def offsets_of(parts):
    return (0, 1, 2, -2, -1, parts // 2)


def silu(x):
    half = 0.5 * x
    return half + half * jnp.tanh(half)


def encode_kernel(
    parts, per_block, owner_ref, grid_ref, w_ref, enc_ref, dec_ref,
    lat_ref, dsum_ref, *rest,
):
    slot_refs = rest[:SLOTS]
    wt_ref, tgt_ref, msum_ref, acc_ref = rest[SLOTS:]
    step = pl.program_id(0)
    block_mesh, block_grid = enc_ref.shape[1:]
    blocks = enc_ref.shape[0] // per_block
    wide = per_block * block_mesh
    rows = SLOTS * block_mesh

    @pl.when(step == 0)
    def _():
        channels, latent = w_ref.shape
        wt_ref[:, :channels] = w_ref[...].astype(F32).T.astype(BF16)
        me = lax.axis_index("nodes")
        off = owner_ref[...] - me
        off = jnp.where(off < 0, off + parts, off)
        slot = jnp.where(off == parts // 2, 5, jnp.where(off > 2, off - parts + 5, off))
        slot = slot.astype(F32)
        total = jnp.zeros(tgt_ref.shape, F32)
        groups, lanes = owner_ref.shape
        all_blocks = tgt_ref.shape[0]
        for r in range(groups):
            tile = lax.broadcasted_iota(jnp.int32, (all_blocks, lanes), 1) + r * lanes
            first = lax.broadcasted_iota(jnp.int32, (all_blocks, lanes), 0) * per_block
            mine = (tile >= first) & (tile < first + per_block)
            picked = jnp.where(mine, slot[r : r + 1, :], 0.0).astype(BF16)
            row = lax.broadcasted_iota(jnp.int32, (lanes, wide), 0) + r * lanes
            col = lax.broadcasted_iota(jnp.int32, (lanes, wide), 1)
            place = row - per_block * ((row * (2**19 // per_block + 1)) >> 19)
            spread = jnp.where(place == col // block_mesh, 1.0, 0.0).astype(BF16)
            total += jnp.dot(picked, spread, preferred_element_type=F32)
        col = lax.broadcasted_iota(jnp.int32, tgt_ref.shape, 1)
        tgt_ref[...] = total.astype(jnp.int32) * block_mesh + col % block_mesh
        acc_ref[...] = jnp.zeros_like(acc_ref)

    row_ids = lax.broadcasted_iota(jnp.int32, (rows, wide), 0)
    for b in range(blocks):
        target = tgt_ref[pl.ds(step * blocks + b, 1), :]
        hot = jnp.where(row_ids == target, 1.0, 0.0).astype(BF16)
        span = slice(b * per_block, (b + 1) * per_block)
        both = jnp.concatenate(
            [
                enc_ref[span].reshape(wide, block_grid),
                dec_ref[span].reshape(wide, block_grid),
            ],
            axis=1,
        )
        sums = jnp.dot(hot, both, preferred_element_type=F32).astype(BF16)
        cols = slice(b * block_grid, (b + 1) * block_grid)
        msum_ref[:, cols] = sums[:, :block_grid]
        dsum_ref[:, cols] = sums[:, block_grid:]
    channels = grid_ref.shape[0]
    lat = silu(
        jnp.dot(wt_ref[:, :channels], grid_ref[...], preferred_element_type=F32)
    ).astype(BF16)
    lat_ref[...] = lat
    acc_ref[...] += lax.dot_general(
        lat, msum_ref[...], (((1,), (1,)), ((), ())), preferred_element_type=F32
    )

    @pl.when(step == pl.num_programs(0) - 1)
    def _():
        flipped = acc_ref[...].T.astype(BF16)
        for s in range(SLOTS):
            slot_refs[s][...] = flipped[s * block_mesh : (s + 1) * block_mesh, :]


def encode(parts, grid_t, w_embed, enc_coef, dec_t, owners):
    channels, points = grid_t.shape
    latent = w_embed.shape[1]
    tiles, block_mesh, block_grid = enc_coef.shape
    grid_blocks = points // block_grid
    per_block = tiles // grid_blocks
    blocks = 4
    steps = grid_blocks // blocks
    width = blocks * block_grid
    rows = SLOTS * block_mesh
    wide = per_block * block_mesh
    return pl.pallas_call(
        functools.partial(encode_kernel, parts, per_block),
        grid=(steps,),
        in_specs=[
            pl.BlockSpec(owners.shape, lambda i: (0, 0)),
            pl.BlockSpec((channels, width), lambda i: (0, i)),
            pl.BlockSpec((channels, latent), lambda i: (0, 0)),
            pl.BlockSpec((blocks * per_block, block_mesh, block_grid), lambda i: (i, 0, 0)),
            pl.BlockSpec((blocks * per_block, block_mesh, block_grid), lambda i: (i, 0, 0)),
        ],
        out_specs=[
            pl.BlockSpec((latent, width), lambda i: (0, i)),
            pl.BlockSpec((rows, width), lambda i: (0, i)),
        ]
        + [pl.BlockSpec((block_mesh, latent), lambda i: (0, 0))] * SLOTS,
        out_shape=[
            jax.ShapeDtypeStruct((latent, points), BF16),
            jax.ShapeDtypeStruct((rows, points), BF16),
        ]
        + [jax.ShapeDtypeStruct((block_mesh, latent), BF16)] * SLOTS,
        scratch_shapes=[
            pltpu.VMEM((latent, 256), BF16),
            pltpu.VMEM((grid_blocks, wide), jnp.int32),
            pltpu.VMEM((rows, width), BF16),
            pltpu.VMEM((latent, rows), F32),
        ],
        compiler_params=pltpu.CompilerParams(vmem_limit_bytes=24 * MIB),
        name="encode",
    )(owners, grid_t, w_embed, enc_coef, dec_t)


def update_kernel(parts, ids_ref, *refs):
    slots = refs[:SLOTS]
    mesh_ref, w_ref, mid_ref, agg_ref = refs[SLOTS:]
    block_mesh = slots[0].shape[0]
    me = lax.axis_index("nodes")
    agg_ref[...] = jnp.zeros_like(agg_ref)
    for s, off in enumerate(offsets_of(parts)):
        block = ids_ref[lax.rem(me - off + parts, parts) * parts + me]
        span = pl.ds(pl.multiple_of(block * block_mesh, block_mesh), block_mesh)
        agg_ref[span, :] += slots[s][...].astype(F32)
    grown = jnp.dot(agg_ref[...].astype(BF16), w_ref[...], preferred_element_type=F32)
    mid_ref[...] = (mesh_ref[...].astype(F32) + silu(grown)).astype(BF16)


def update(parts, ids, slots, mesh_in, w_enc):
    vmem = pl.BlockSpec(memory_space=pltpu.VMEM)
    return pl.pallas_call(
        functools.partial(update_kernel, parts),
        in_specs=[pl.BlockSpec(memory_space=pltpu.SMEM)] + [vmem] * (SLOTS + 2),
        out_specs=vmem,
        out_shape=jax.ShapeDtypeStruct(mesh_in.shape, BF16),
        scratch_shapes=[pltpu.VMEM(mesh_in.shape, F32)],
        compiler_params=pltpu.CompilerParams(vmem_limit_bytes=8 * MIB),
        name="mesh_update",
    )(ids, *slots, mesh_in, w_enc)


def process_kernel(
    parts, ids_ref, adj_ref, mid_ref, left_ref, right_ref, coef_ref, gain_ref, w_ref,
    out_ref, *rest,
):
    sends = rest[:SLOTS]
    ext_ref, pick_ref, norm_ref = rest[SLOTS:]
    mesh_blocks, block_mesh, wide = coef_ref.shape
    adj_width = wide // block_mesh
    mesh_count = mid_ref.shape[0]
    me = lax.axis_index("nodes")
    ext_ref[0:mesh_count, :] = left_ref[...]
    ext_ref[mesh_count : 2 * mesh_count, :] = mid_ref[...]
    ext_ref[2 * mesh_count : 3 * mesh_count, :] = right_ref[...]
    for b in range(mesh_blocks):
        for a in range(adj_width):
            near = jnp.maximum(adj_ref[b, a], 0)
            side = lax.rem(near // mesh_blocks - me + 1 + parts, parts)
            place = side * mesh_blocks + lax.rem(near, mesh_blocks)
            place = jnp.minimum(place, 3 * mesh_blocks - 1)
            span = pl.ds(pl.multiple_of(place * block_mesh, block_mesh), block_mesh)
            pick_ref[b, a * block_mesh : (a + 1) * block_mesh, :] = ext_ref[span, :]
        message = jnp.dot(coef_ref[b], pick_ref[b], preferred_element_type=F32)
        power = jnp.mean(message * message, axis=-1, keepdims=True)
        normed = message * lax.rsqrt(power + 1e-05) * gain_ref[...]
        norm_ref[b * block_mesh : (b + 1) * block_mesh, :] = normed.astype(BF16)
    grown = jnp.dot(norm_ref[...], w_ref[...], preferred_element_type=F32)
    out_ref[...] = (mid_ref[...].astype(F32) + silu(grown)).astype(BF16)
    for s, off in enumerate(offsets_of(parts)):
        block = ids_ref[lax.rem(me - off + parts, parts) * parts + me]
        span = pl.ds(pl.multiple_of(block * block_mesh, block_mesh), block_mesh)
        sends[s][...] = out_ref[span, :]


def process(parts, ids, adj, mid, left, right, coef, gain, w_proc):
    vmem = pl.BlockSpec(memory_space=pltpu.VMEM)
    smem = pl.BlockSpec(memory_space=pltpu.SMEM)
    mesh_blocks, block_mesh, wide = coef.shape
    mesh_count, latent = mid.shape
    return pl.pallas_call(
        functools.partial(process_kernel, parts),
        in_specs=[smem] * 2 + [vmem] * 6,
        out_specs=[vmem] * (1 + SLOTS),
        out_shape=[jax.ShapeDtypeStruct(mid.shape, BF16)]
        + [jax.ShapeDtypeStruct((block_mesh, latent), BF16)] * SLOTS,
        scratch_shapes=[
            pltpu.VMEM((3 * mesh_count, latent), BF16),
            pltpu.VMEM((mesh_blocks, wide, latent), BF16),
            pltpu.VMEM((mesh_count, latent), BF16),
        ],
        compiler_params=pltpu.CompilerParams(vmem_limit_bytes=8 * MIB),
        name="mesh_process",
    )(ids, adj, mid, left, right, coef, gain, w_proc)


def decode_kernel(grid_ref, lat_ref, dsum_ref, w_ref, *rest):
    slots = rest[:SLOTS]
    out_ref, back_ref = rest[SLOTS:]

    @pl.when(pl.program_id(0) == 0)
    def _():
        joined = jnp.concatenate([slot[...] for slot in slots], axis=0)
        back_ref[...] = joined.astype(F32).T.astype(BF16)

    decoded = jnp.dot(back_ref[...], dsum_ref[...], preferred_element_type=F32)
    hidden = silu(lat_ref[...].astype(F32) + decoded).astype(BF16)
    out_ref[...] = (
        grid_ref[...].astype(F32)
        + jnp.dot(w_ref[...], hidden, preferred_element_type=F32)
    ).astype(BF16)


def decode(grid_t, lat_t, dsum, w_out_t, slots):
    channels, points = grid_t.shape
    latent = lat_t.shape[0]
    rows = dsum.shape[0]
    block_mesh = slots[0].shape[0]
    width = 512
    return pl.pallas_call(
        decode_kernel,
        grid=(points // width,),
        in_specs=[
            pl.BlockSpec((channels, width), lambda i: (0, i)),
            pl.BlockSpec((latent, width), lambda i: (0, i)),
            pl.BlockSpec((rows, width), lambda i: (0, i)),
            pl.BlockSpec((channels, latent), lambda i: (0, 0)),
        ]
        + [pl.BlockSpec((block_mesh, latent), lambda i: (0, 0))] * SLOTS,
        out_specs=pl.BlockSpec((channels, width), lambda i: (0, i)),
        out_shape=jax.ShapeDtypeStruct((channels, points), BF16),
        scratch_shapes=[pltpu.VMEM((latent, rows), BF16)],
        compiler_params=pltpu.CompilerParams(vmem_limit_bytes=24 * MIB),
        name="decode",
    )(grid_t, lat_t, dsum, w_out_t, *slots)


def local(
    grid_in, w_embed, enc_coef, enc_owner, slot_block, mesh_in, w_enc,
    proc_adj, proc_coef, proc_gain, w_proc, dec_coef, w_out,
):
    parts = lax.axis_size("nodes")
    offsets = offsets_of(parts)
    mesh_blocks, adj_width, block_mesh, _ = proc_coef.shape

    def shift(x, off):
        if off == 0:
            return x
        return lax.ppermute(x, "nodes", [(i, (i + off) % parts) for i in range(parts)])

    ids = lax.all_gather(slot_block, "nodes", axis=0, tiled=True)
    grid_t = grid_in.T
    lat_t, dsum, *sums = encode(
        parts, grid_t, w_embed, enc_coef, jnp.swapaxes(dec_coef, 1, 2),
        enc_owner.reshape(-1, 128),
    )
    received = [shift(x, off) for x, off in zip(sums, offsets)]
    mid = update(parts, ids, received, mesh_in, w_enc)
    left, right = shift(mid, 1), shift(mid, -1)
    live = (proc_adj >= 0)[:, :, None, None]
    coef = jnp.where(live, proc_coef, jnp.zeros_like(proc_coef))
    coef = coef.transpose(0, 2, 1, 3).reshape(mesh_blocks, block_mesh, adj_width * block_mesh)
    mesh_out, *sends = process(
        parts, ids, proc_adj, mid, left, right, coef, proc_gain.reshape(1, -1), w_proc
    )
    returned = [shift(x, -off) for x, off in zip(sends, offsets)]
    pred_t = decode(grid_t, lat_t, dsum, w_out.T, returned)
    return (pred_t.T, mesh_out)


def solution(mesh):
    return jax.shard_map(
        local,
        mesh=mesh,
        in_specs=(
            P(("groups", "nodes"), None),
            P(),
            P("nodes", None, None),
            P("nodes"),
            P("nodes"),
            P(("groups", "nodes"), None),
            P(),
            P("nodes", None),
            P("nodes", None, None, None),
            P(),
            P(),
            P("nodes", None, None),
            P(),
        ),
        out_specs=(P(("groups", "nodes"), None), P(("groups", "nodes"), None)),
        check_vma=False,
    )
```

```python
import functools

import jax
import jax.numpy as jnp
from jax import lax
from jax.experimental import pallas as pl
from jax.experimental.pallas import tpu as pltpu
from jax.sharding import PartitionSpec as P

F32 = jnp.float32
BF16 = jnp.bfloat16
MIB = 1 << 20
OWN, HALF, ODD, FAR, EVEN, NEAR = range(6)
SLOTS = 6
PAD = 16


def partner(slot, me, parts):
    chip = me // 2 % 2
    core = me % 2
    step = {
        OWN: 0,
        HALF: parts // 2,
        ODD: 4 * chip - 2,
        EVEN: 2 - 4 * chip,
        FAR: 2 * core - 1,
        NEAR: 1 - 2 * core,
    }[slot]
    return (me + step + parts) % parts


def scalar_partner(slot, me, parts):
    chip = lax.rem(lax.div(me, 2), 2)
    core = lax.rem(me, 2)
    step = {
        OWN: 0,
        HALF: parts // 2,
        ODD: 4 * chip - 2,
        EVEN: 2 - 4 * chip,
        FAR: 2 * core - 1,
        NEAR: 1 - 2 * core,
    }[slot]
    return lax.rem(me + step + parts, parts)


def silu(x):
    half = 0.5 * x
    return half + half * jnp.tanh(half)


def hot_rows(target, rows):
    ids = lax.broadcasted_iota(jnp.int32, (rows, target.shape[1]), 0)
    return jnp.where(ids == target, 1.0, 0.0).astype(BF16)


def fill_targets(parts, per_block, block_mesh, owner_ref, tgt_ref):
    wide = tgt_ref.shape[1]
    me = lax.axis_index("nodes")
    chip = lax.rem(lax.div(me, 2), 2)
    core = lax.rem(me, 2)
    up2 = EVEN + (ODD - EVEN) * chip
    up1 = NEAR + (FAR - NEAR) * core
    off = owner_ref[...] - me
    off = jnp.where(off < 0, off + parts, off)
    slot = jnp.where(off == parts // 2, HALF, OWN)
    slot = jnp.where(off == 2, up2, slot)
    slot = jnp.where(off == parts - 2, ODD + EVEN - up2, slot)
    slot = jnp.where(off == 1, up1, slot)
    slot = jnp.where(off == parts - 1, NEAR + FAR - up1, slot)
    slot = slot.astype(F32)
    groups, lanes = owner_ref.shape
    all_blocks = tgt_ref.shape[0]
    total = jnp.zeros(tgt_ref.shape, F32)
    for r in range(groups):
        tile = lax.broadcasted_iota(jnp.int32, (all_blocks, lanes), 1) + r * lanes
        first = lax.broadcasted_iota(jnp.int32, (all_blocks, lanes), 0) * per_block
        mine = (tile >= first) & (tile < first + per_block)
        picked = jnp.where(mine, slot[r : r + 1, :], 0.0).astype(BF16)
        row = lax.broadcasted_iota(jnp.int32, (lanes, wide), 0) + r * lanes
        col = lax.broadcasted_iota(jnp.int32, (lanes, wide), 1)
        place = row - per_block * ((row * (2**19 // per_block + 1)) >> 19)
        spread = jnp.where(place == col // block_mesh, 1.0, 0.0).astype(BF16)
        total += jnp.dot(picked, spread, preferred_element_type=F32)
    col = lax.broadcasted_iota(jnp.int32, tgt_ref.shape, 1)
    tgt_ref[...] = total.astype(jnp.int32) * block_mesh + col % block_mesh


def encode_kernel(
    parts, per_block, slot_ref, owner_ref, grid_ref, w_ref, enc_ref, lat_ref, tgt_ref, *rest
):
    send_refs = rest[:SLOTS]
    wt_ref, msum_ref, acc_ref = rest[SLOTS:]
    step = pl.program_id(0)
    block_mesh, block_grid = enc_ref.shape[1:]
    blocks = enc_ref.shape[0] // per_block
    wide = per_block * block_mesh
    rows = SLOTS * block_mesh
    channels, latent = w_ref.shape

    @pl.when(step == 0)
    def _():
        wt_ref[:, :channels] = w_ref[...].astype(F32).T.astype(BF16)
        fill_targets(parts, per_block, block_mesh, owner_ref, tgt_ref)
        acc_ref[...] = jnp.zeros_like(acc_ref)

    for b in range(blocks):
        hot = hot_rows(tgt_ref[pl.ds(step * blocks + b, 1), :], rows)
        tiles = enc_ref[b * per_block : (b + 1) * per_block].reshape(wide, block_grid)
        sums = jnp.dot(hot, tiles, preferred_element_type=F32)
        msum_ref[:, b * block_grid : (b + 1) * block_grid] = sums.astype(BF16)
    lat = silu(
        jnp.dot(wt_ref[:, :channels], grid_ref[...], preferred_element_type=F32)
    ).astype(BF16)
    lat_ref[...] = lat
    acc_ref[...] += lax.dot_general(
        lat, msum_ref[...], (((1,), (1,)), ((), ())), preferred_element_type=F32
    )

    @pl.when(step == pl.num_programs(0) - 1)
    def _():
        me = lax.axis_index("nodes")
        flipped = acc_ref[...].T.astype(BF16)
        for s in range(SLOTS):
            send_refs[s][:block_mesh, :] = flipped[s * block_mesh : (s + 1) * block_mesh, :]
            block = slot_ref[scalar_partner(s, me, parts)].astype(F32)
            send_refs[s][block_mesh:, :] = jnp.full((PAD, latent), block, F32).astype(BF16)


def encode(parts, slot_block, owners, grid_t, w_embed, enc_coef):
    channels, points = grid_t.shape
    latent = w_embed.shape[1]
    tiles, block_mesh, block_grid = enc_coef.shape
    grid_blocks = points // block_grid
    per_block = tiles // grid_blocks
    blocks = 4
    steps = grid_blocks // blocks
    width = blocks * block_grid
    rows = SLOTS * block_mesh
    wide = per_block * block_mesh
    return pl.pallas_call(
        functools.partial(encode_kernel, parts, per_block),
        grid=(steps,),
        in_specs=[
            pl.BlockSpec(memory_space=pltpu.SMEM),
            pl.BlockSpec(owners.shape, lambda i: (0, 0)),
            pl.BlockSpec((channels, width), lambda i: (0, i)),
            pl.BlockSpec((channels, latent), lambda i: (0, 0)),
            pl.BlockSpec((blocks * per_block, block_mesh, block_grid), lambda i: (i, 0, 0)),
        ],
        out_specs=[
            pl.BlockSpec((latent, width), lambda i: (0, i)),
            pl.BlockSpec((grid_blocks, wide), lambda i: (0, 0)),
        ]
        + [pl.BlockSpec((block_mesh + PAD, latent), lambda i: (0, 0))] * SLOTS,
        out_shape=[
            jax.ShapeDtypeStruct((latent, points), BF16),
            jax.ShapeDtypeStruct((grid_blocks, wide), jnp.int32),
        ]
        + [jax.ShapeDtypeStruct((block_mesh + PAD, latent), BF16)] * SLOTS,
        scratch_shapes=[
            pltpu.VMEM((latent, 256), BF16),
            pltpu.VMEM((rows, width), BF16),
            pltpu.VMEM((latent, rows), F32),
        ],
        compiler_params=pltpu.CompilerParams(vmem_limit_bytes=56 * MIB),
        name="encode",
    )(slot_block, owners, grid_t, w_embed, enc_coef)


def prepare_kernel(parts, per_block, adj_ref, coef_ref, tgt_ref, dec_ref, near_ref, dsum_ref):
    step = pl.program_id(0)
    block_mesh, block_grid = dec_ref.shape[1:]
    blocks = dec_ref.shape[0] // per_block
    wide = per_block * block_mesh
    rows = SLOTS * block_mesh
    for b in range(blocks):
        hot = hot_rows(tgt_ref[pl.ds(step * blocks + b, 1), :], rows)
        tiles = dec_ref[b * per_block : (b + 1) * per_block].reshape(wide, block_grid)
        sums = jnp.dot(hot, tiles, preferred_element_type=F32)
        dsum_ref[:, b * block_grid : (b + 1) * block_grid] = sums.astype(BF16)

    @pl.when(step == 0)
    def _():
        mesh_blocks, adj_width = adj_ref.shape
        me = lax.axis_index("nodes")
        core = lax.rem(me, 2)
        columns = near_ref.shape[1]
        row = lax.broadcasted_iota(jnp.int32, (block_mesh, columns), 0)
        col = lax.broadcasted_iota(jnp.int32, (block_mesh, columns), 1)
        for b in range(mesh_blocks):
            total = jnp.zeros((block_mesh, columns), F32)
            for a in range(adj_width):
                which = adj_ref[b, a]
                listed = jnp.maximum(which, 0)
                side = lax.rem(lax.div(listed, mesh_blocks) - me + 1 + parts, parts)
                side = jnp.where(core == 0, 2 - side, side)
                place = side * mesh_blocks + lax.rem(listed, mesh_blocks)
                place = jnp.where(which >= 0, place, -1)
                spot = jnp.where(col == place * block_mesh + row, 1.0, 0.0).astype(BF16)
                total += jnp.dot(coef_ref[b, a], spot, preferred_element_type=F32)
            near_ref[b * block_mesh : (b + 1) * block_mesh, :] = total.astype(BF16)


def prepare(parts, adj, coef, tgt, dec_t):
    tiles, block_mesh, block_grid = dec_t.shape
    grid_blocks, wide = tgt.shape
    per_block = tiles // grid_blocks
    mesh_blocks = adj.shape[0]
    blocks = 4
    width = blocks * block_grid
    rows = SLOTS * block_mesh
    count = mesh_blocks * block_mesh
    return pl.pallas_call(
        functools.partial(prepare_kernel, parts, per_block),
        grid=(grid_blocks // blocks,),
        in_specs=[
            pl.BlockSpec(memory_space=pltpu.SMEM),
            pl.BlockSpec(coef.shape, lambda i: (0, 0, 0, 0)),
            pl.BlockSpec(tgt.shape, lambda i: (0, 0)),
            pl.BlockSpec((blocks * per_block, block_mesh, block_grid), lambda i: (i, 0, 0)),
        ],
        out_specs=[
            pl.BlockSpec((count, 3 * count), lambda i: (0, 0)),
            pl.BlockSpec((rows, width), lambda i: (0, i)),
        ],
        out_shape=[
            jax.ShapeDtypeStruct((count, 3 * count), BF16),
            jax.ShapeDtypeStruct((rows, grid_blocks * block_grid), BF16),
        ],
        compiler_params=pltpu.CompilerParams(vmem_limit_bytes=56 * MIB),
        cost_estimate=pl.CostEstimate(
            flops=2 * rows * wide * block_grid * grid_blocks,
            bytes_accessed=2 * (tiles * block_mesh * block_grid + rows * width * 8),
            transcendentals=0,
        ),
        name="prepare",
    )(adj, coef, tgt, dec_t)


def update_kernel(*refs):
    slots = refs[:SLOTS]
    mesh_ref, w_ref, mid_ref, ids_ref = refs[SLOTS:]
    count, latent = mesh_ref.shape
    block_mesh = slots[0].shape[0] - PAD
    sums = [slot[:block_mesh, :].astype(F32) for slot in slots]
    ids = [slot[block_mesh:, :].astype(F32)[:1, :] for slot in slots]
    for s in range(SLOTS):
        ids_ref[s : s + 1, :] = ids[s]
    parts = []
    for b in range(count // block_mesh):
        total = jnp.zeros((block_mesh, latent), F32)
        for s in range(SLOTS):
            total += jnp.where(ids[s] == b, sums[s], 0.0)
        parts.append(total.astype(BF16))
    grown = jnp.dot(jnp.concatenate(parts, axis=0), w_ref[...], preferred_element_type=F32)
    mid_ref[...] = (mesh_ref[...].astype(F32) + silu(grown)).astype(BF16)


def update(slots, mesh_in, w_enc):
    vmem = pl.BlockSpec(memory_space=pltpu.VMEM)
    return pl.pallas_call(
        update_kernel,
        in_specs=[vmem] * (SLOTS + 2),
        out_specs=[vmem] * 2,
        out_shape=[
            jax.ShapeDtypeStruct(mesh_in.shape, BF16),
            jax.ShapeDtypeStruct((8, mesh_in.shape[1]), F32),
        ],
        compiler_params=pltpu.CompilerParams(vmem_limit_bytes=8 * MIB),
        name="mesh_update",
    )(*slots, mesh_in, w_enc)


def process_kernel(ids_ref, mid_ref, near_mid_ref, far_mid_ref, near_ref, gain_ref, w_ref, out_ref, *sends):
    count, latent = mid_ref.shape
    block_mesh = sends[0].shape[0]
    around = jnp.concatenate([near_mid_ref[...], mid_ref[...], far_mid_ref[...]], axis=0)
    message = jnp.dot(near_ref[...], around, preferred_element_type=F32)
    power = jnp.mean(message * message, axis=-1, keepdims=True)
    normed = (message * lax.rsqrt(power + 1e-05) * gain_ref[...]).astype(BF16)
    grown = jnp.dot(normed, w_ref[...], preferred_element_type=F32)
    grown = mid_ref[...].astype(F32) + silu(grown)
    out_ref[...] = grown.astype(BF16)
    for s in range(SLOTS):
        chosen = grown[:block_mesh, :]
        for b in range(1, count // block_mesh):
            block = grown[b * block_mesh : (b + 1) * block_mesh, :]
            chosen = jnp.where(ids_ref[s : s + 1, :] == b, block, chosen)
        sends[s][...] = chosen.astype(BF16)


def process(block_mesh, ids, mid, near_mid, far_mid, near, gain, w_proc):
    vmem = pl.BlockSpec(memory_space=pltpu.VMEM)
    latent = mid.shape[1]
    return pl.pallas_call(
        process_kernel,
        in_specs=[vmem] * 7,
        out_specs=[vmem] * (1 + SLOTS),
        out_shape=[jax.ShapeDtypeStruct(mid.shape, BF16)]
        + [jax.ShapeDtypeStruct((block_mesh, latent), BF16)] * SLOTS,
        compiler_params=pltpu.CompilerParams(vmem_limit_bytes=8 * MIB),
        name="mesh_process",
    )(ids, mid, near_mid, far_mid, near, gain, w_proc)


def decode_kernel(grid_ref, lat_ref, dsum_ref, w_ref, *rest):
    slots = rest[:SLOTS]
    out_ref, back_ref = rest[SLOTS:]

    @pl.when(pl.program_id(0) == 0)
    def _():
        joined = jnp.concatenate([slot[...] for slot in slots], axis=0)
        back_ref[...] = joined.astype(F32).T.astype(BF16)

    decoded = jnp.dot(back_ref[...], dsum_ref[...], preferred_element_type=F32)
    hidden = silu(lat_ref[...].astype(F32) + decoded).astype(BF16)
    out_ref[...] = (
        grid_ref[...].astype(F32)
        + jnp.dot(w_ref[...], hidden, preferred_element_type=F32)
    ).astype(BF16)


def decode(grid_t, lat_t, dsum, w_out_t, slots):
    channels, points = grid_t.shape
    latent = lat_t.shape[0]
    rows = dsum.shape[0]
    block_mesh = slots[0].shape[0]
    width = 512
    return pl.pallas_call(
        decode_kernel,
        grid=(points // width,),
        in_specs=[
            pl.BlockSpec((channels, width), lambda i: (0, i)),
            pl.BlockSpec((latent, width), lambda i: (0, i)),
            pl.BlockSpec((rows, width), lambda i: (0, i)),
            pl.BlockSpec((channels, latent), lambda i: (0, 0)),
        ]
        + [pl.BlockSpec((block_mesh, latent), lambda i: (0, 0))] * SLOTS,
        out_specs=pl.BlockSpec((channels, width), lambda i: (0, i)),
        out_shape=jax.ShapeDtypeStruct((channels, points), BF16),
        scratch_shapes=[pltpu.VMEM((latent, rows), BF16)],
        compiler_params=pltpu.CompilerParams(vmem_limit_bytes=56 * MIB),
        name="decode",
    )(grid_t, lat_t, dsum, w_out_t, *slots)


def local(
    grid_in, w_embed, enc_coef, enc_owner, slot_block, mesh_in, w_enc,
    proc_adj, proc_coef, proc_gain, w_proc, dec_coef, w_out,
):
    parts = lax.axis_size("nodes")
    block_mesh = enc_coef.shape[1]

    def swap(x, slot):
        pairs = [(i, partner(slot, i, parts)) for i in range(parts)]
        return lax.ppermute(x, "nodes", pairs)

    def swap_all(xs):
        return [xs[OWN]] + [swap(xs[s], s) for s in range(1, SLOTS)]

    grid_t = grid_in.T
    lat_t, tgt, *sums = encode(
        parts, slot_block, enc_owner.reshape(-1, 128), grid_t, w_embed, enc_coef
    )
    received = swap_all(sums)
    near, dsum = prepare(parts, proc_adj, proc_coef, tgt, jnp.swapaxes(dec_coef, 1, 2))
    mid, ids = update(received, mesh_in, w_enc)
    far_mid = swap(mid, FAR)
    near_mid = swap(mid, NEAR)
    mesh_out, *sends = process(
        block_mesh, ids, mid, near_mid, far_mid, near, proc_gain.reshape(1, -1), w_proc
    )
    returned = swap_all(sends)
    pred_t = decode(grid_t, lat_t, dsum, w_out.T, returned)
    return (pred_t.T, mesh_out)


def solution(mesh):
    return jax.shard_map(
        local,
        mesh=mesh,
        in_specs=(
            P(("groups", "nodes"), None),
            P(),
            P("nodes", None, None),
            P("nodes"),
            P("nodes"),
            P(("groups", "nodes"), None),
            P(),
            P("nodes", None),
            P("nodes", None, None, None),
            P(),
            P(),
            P("nodes", None, None),
            P(),
        ),
        out_specs=(P(("groups", "nodes"), None), P(("groups", "nodes"), None)),
        check_vma=False,
    )
```

```python
import functools

import jax
import jax.numpy as jnp
from jax import lax
from jax.experimental import pallas as pl
from jax.experimental.pallas import tpu as pltpu
from jax.sharding import PartitionSpec as P

F32 = jnp.float32
BF16 = jnp.bfloat16
MIB = 1 << 20
OWN, HALF, ODD, FAR, EVEN, NEAR = range(6)
SLOTS = 6
PAD = 128


def partner(slot, me, parts):
    chip = me // 2 % 2
    core = me % 2
    step = {
        OWN: 0,
        HALF: parts // 2,
        ODD: 4 * chip - 2,
        EVEN: 2 - 4 * chip,
        FAR: 2 * core - 1,
        NEAR: 1 - 2 * core,
    }[slot]
    return (me + step + parts) % parts


def scalar_partner(slot, me, parts):
    chip = lax.rem(lax.div(me, 2), 2)
    core = lax.rem(me, 2)
    step = {
        OWN: 0,
        HALF: parts // 2,
        ODD: 4 * chip - 2,
        EVEN: 2 - 4 * chip,
        FAR: 2 * core - 1,
        NEAR: 1 - 2 * core,
    }[slot]
    return lax.rem(me + step + parts, parts)


def silu(x):
    half = 0.5 * x
    return half + half * jnp.tanh(half)


def hot_rows(ids, target):
    lanes = ids.shape[1]
    target = target.astype(BF16)
    one, zero = jnp.ones((), BF16), jnp.zeros((), BF16)
    return jnp.concatenate(
        [
            jnp.where(ids == target[:, at : at + lanes], one, zero)
            for at in range(0, target.shape[1], lanes)
        ],
        axis=1,
    )


def fill_targets(parts, per_block, block_mesh, owner_ref, tgt_ref):
    wide = tgt_ref.shape[1]
    me = lax.axis_index("nodes")
    chip = lax.rem(lax.div(me, 2), 2)
    core = lax.rem(me, 2)
    up2 = EVEN + (ODD - EVEN) * chip
    up1 = NEAR + (FAR - NEAR) * core
    off = owner_ref[...] - me
    off = jnp.where(off < 0, off + parts, off)
    slot = jnp.where(off == parts // 2, HALF, OWN)
    slot = jnp.where(off == 2, up2, slot)
    slot = jnp.where(off == parts - 2, ODD + EVEN - up2, slot)
    slot = jnp.where(off == 1, up1, slot)
    slot = jnp.where(off == parts - 1, NEAR + FAR - up1, slot)
    slot = slot.astype(F32)
    groups, lanes = owner_ref.shape
    all_blocks = tgt_ref.shape[0]
    total = jnp.zeros(tgt_ref.shape, F32)
    for r in range(groups):
        tile = lax.broadcasted_iota(jnp.int32, (all_blocks, lanes), 1) + r * lanes
        first = lax.broadcasted_iota(jnp.int32, (all_blocks, lanes), 0) * per_block
        mine = (tile >= first) & (tile < first + per_block)
        picked = jnp.where(mine, slot[r : r + 1, :], 0.0).astype(BF16)
        row = lax.broadcasted_iota(jnp.int32, (lanes, wide), 0) + r * lanes
        col = lax.broadcasted_iota(jnp.int32, (lanes, wide), 1)
        place = row - per_block * ((row * (2**19 // per_block + 1)) >> 19)
        spread = jnp.where(place == col // block_mesh, 1.0, 0.0).astype(BF16)
        total += jnp.dot(picked, spread, preferred_element_type=F32)
    col = lax.broadcasted_iota(jnp.int32, tgt_ref.shape, 1)
    tgt_ref[...] = total * block_mesh + (col % block_mesh).astype(F32)


def encode_kernel(
    parts, width, slot_hbm, owner_hbm, w_hbm, grid_hbm, enc_hbm, dec_hbm,
    lat_ref, dsum_ref, grid_ref, *rest,
):
    send_refs = rest[:SLOTS]
    (
        slot_ref, owner_ref, w_ref, enc_ref, dec_ref, wt_ref, tgt_ref, ids_ref, msum_ref,
        acc_ref, small_sems, sems,
    ) = rest[SLOTS:]
    tiles, block_mesh, block_grid = enc_ref.shape
    channels, points = grid_ref.shape
    latent = w_ref.shape[1]
    per_block = tiles * block_grid // points
    blocks = width // block_grid
    chunk = blocks * per_block
    steps = points // width
    wide = per_block * block_mesh
    rows = SLOTS * block_mesh

    def copies(step):
        cols = pl.ds(pl.multiple_of(step * width, width), width)
        some = pl.ds(step * chunk, chunk)
        return (
            pltpu.make_async_copy(grid_hbm.at[:, cols], grid_ref.at[:, cols], sems.at[0, step]),
            pltpu.make_async_copy(enc_hbm.at[some], enc_ref.at[some], sems.at[1, step]),
            pltpu.make_async_copy(dec_hbm.at[some], dec_ref.at[some], sems.at[2, step]),
        )

    small = [
        pltpu.make_async_copy(source, target, small_sems.at[i])
        for i, (source, target) in enumerate(
            ((owner_hbm, owner_ref), (w_hbm, w_ref), (slot_hbm, slot_ref))
        )
    ]
    for copy in small:
        copy.start()
    for step in range(steps):
        for copy in copies(step):
            copy.start()
    for copy in small:
        copy.wait()
    wt_ref[:, :channels] = w_ref[...].astype(F32).T.astype(BF16)
    fill_targets(parts, per_block, block_mesh, owner_ref, tgt_ref)
    ids_ref[...] = lax.broadcasted_iota(jnp.int32, ids_ref.shape, 0).astype(BF16)
    acc_ref[...] = jnp.zeros_like(acc_ref)

    @pl.loop(0, steps)
    def _(step):
        for copy in copies(step):
            copy.wait()
        cols = pl.ds(pl.multiple_of(step * width, width), width)
        for b in range(blocks):
            hot = hot_rows(ids_ref[...], tgt_ref[pl.ds(step * blocks + b, 1), :])
            some = pl.ds(step * chunk + b * per_block, per_block)
            both = jnp.concatenate(
                [
                    enc_ref[some].reshape(wide, block_grid),
                    dec_ref[some].reshape(wide, block_grid),
                ],
                axis=1,
            )
            sums = jnp.dot(hot, both, preferred_element_type=F32).astype(BF16)
            msum_ref[:, b * block_grid : (b + 1) * block_grid] = sums[:, :block_grid]
            first = pl.multiple_of((step * blocks + b) * block_grid, block_grid)
            dsum_ref[:, pl.ds(first, block_grid)] = sums[:, block_grid:]
        lat = silu(
            jnp.dot(wt_ref[:, :channels], grid_ref[:, cols], preferred_element_type=F32)
        ).astype(BF16)
        lat_ref[:, cols] = lat
        acc_ref[...] += lax.dot_general(
            lat, msum_ref[...], (((1,), (1,)), ((), ())), preferred_element_type=F32
        )

    me = lax.axis_index("nodes")
    flipped = acc_ref[...].T.astype(BF16)
    for s in range(SLOTS):
        send_refs[s][:, :latent] = flipped[s * block_mesh : (s + 1) * block_mesh, :]
        block = slot_ref[scalar_partner(s, me, parts)].astype(F32)
        send_refs[s][:, latent:] = jnp.full((block_mesh, PAD), block, F32).astype(BF16)


def encode(parts, slot_block, owners, grid_t, w_embed, enc_coef, dec_t):
    channels, points = grid_t.shape
    latent = w_embed.shape[1]
    tiles, block_mesh, block_grid = enc_coef.shape
    grid_blocks = points // block_grid
    width = 512
    steps = points // width
    rows = SLOTS * block_mesh
    wide = tiles // grid_blocks * block_mesh
    vmem = pl.BlockSpec(memory_space=pltpu.VMEM)
    hbm = pl.BlockSpec(memory_space=pl.ANY)
    return pl.pallas_call(
        functools.partial(encode_kernel, parts, width),
        in_specs=[hbm] * 6,
        out_specs=[vmem] * (3 + SLOTS),
        out_shape=[
            pltpu.VMEM((latent, points), BF16),
            pltpu.VMEM((rows, points), BF16),
            pltpu.VMEM((channels, points), BF16),
        ]
        + [jax.ShapeDtypeStruct((block_mesh, latent + PAD), BF16)] * SLOTS,
        scratch_shapes=[
            pltpu.SMEM(slot_block.shape, jnp.int32),
            pltpu.VMEM(owners.shape, jnp.int32),
            pltpu.VMEM(w_embed.shape, BF16),
            pltpu.VMEM(enc_coef.shape, BF16),
            pltpu.VMEM(dec_t.shape, BF16),
            pltpu.VMEM((latent, 256), BF16),
            pltpu.VMEM((grid_blocks, wide), F32),
            pltpu.VMEM((rows, 128), BF16),
            pltpu.VMEM((rows, width), BF16),
            pltpu.VMEM((latent, rows), F32),
            pltpu.SemaphoreType.DMA((3,)),
            pltpu.SemaphoreType.DMA((3, steps)),
        ],
        compiler_params=pltpu.CompilerParams(vmem_limit_bytes=24 * MIB),
        name="encode",
    )(
        *(
            pltpu.with_memory_space_constraint(x, pltpu.HBM)
            for x in (slot_block, owners, w_embed, grid_t, enc_coef, dec_t)
        )
    )


def prepare_kernel(parts, adj_ref, coef_ref, after_ref, near_ref):
    mesh_blocks, adj_width = adj_ref.shape
    block_mesh = coef_ref.shape[2]
    me = lax.axis_index("nodes")
    core = lax.rem(me, 2)
    columns = near_ref.shape[1]
    row = lax.broadcasted_iota(jnp.int32, (block_mesh, columns), 0)
    col = lax.broadcasted_iota(jnp.int32, (block_mesh, columns), 1)
    for b in range(mesh_blocks):
        total = jnp.zeros((block_mesh, columns), F32)
        for a in range(adj_width):
            which = adj_ref[b, a]
            listed = jnp.maximum(which, 0)
            side = lax.rem(lax.div(listed, mesh_blocks) - me + 1 + parts, parts)
            side = jnp.where(core == 0, 2 - side, side)
            place = side * mesh_blocks + lax.rem(listed, mesh_blocks)
            place = jnp.where(which >= 0, place, -columns)
            spot = jnp.where(col == place * block_mesh + row, 1.0, 0.0).astype(BF16)
            total += jnp.dot(coef_ref[b, a], spot, preferred_element_type=F32)
        near_ref[b * block_mesh : (b + 1) * block_mesh, :] = total.astype(BF16)


def prepare(parts, adj, coef, after):
    mesh_blocks, adj_width, block_mesh, _ = coef.shape
    count = mesh_blocks * block_mesh
    vmem = pl.BlockSpec(memory_space=pltpu.VMEM)
    return pl.pallas_call(
        functools.partial(prepare_kernel, parts),
        in_specs=[pl.BlockSpec(memory_space=pltpu.SMEM), vmem, vmem],
        out_specs=vmem,
        out_shape=jax.ShapeDtypeStruct((count, 3 * count), BF16),
        compiler_params=pltpu.CompilerParams(vmem_limit_bytes=8 * MIB),
        cost_estimate=pl.CostEstimate(
            flops=2 * adj_width * count * block_mesh * 3 * count,
            bytes_accessed=8 * count * 3 * count,
            transcendentals=0,
        ),
        name="prepare",
    )(adj, coef, after)


def update_kernel(*refs):
    slots = refs[:SLOTS]
    mesh_ref, w_ref, mid_ref, ids_ref = refs[SLOTS:]
    count, latent = mesh_ref.shape
    block_mesh = slots[0].shape[0]
    sums = [slot[:, :latent].astype(F32) for slot in slots]
    ids = [slot[:, latent:].astype(F32)[:1, :1] for slot in slots]
    for s in range(SLOTS):
        ids_ref[s : s + 1, :] = jnp.broadcast_to(ids[s], (1, latent))
    parts = []
    for b in range(count // block_mesh):
        total = jnp.zeros((block_mesh, latent), F32)
        for s in range(SLOTS):
            total += jnp.where(ids[s] == b, sums[s], 0.0)
        parts.append(total.astype(BF16))
    grown = jnp.dot(jnp.concatenate(parts, axis=0), w_ref[...], preferred_element_type=F32)
    mid_ref[...] = (mesh_ref[...].astype(F32) + silu(grown)).astype(BF16)


def update(slots, mesh_in, w_enc):
    vmem = pl.BlockSpec(memory_space=pltpu.VMEM)
    return pl.pallas_call(
        update_kernel,
        in_specs=[vmem] * (SLOTS + 2),
        out_specs=[vmem] * 2,
        out_shape=[
            jax.ShapeDtypeStruct(mesh_in.shape, BF16),
            jax.ShapeDtypeStruct((8, mesh_in.shape[1]), F32),
        ],
        compiler_params=pltpu.CompilerParams(vmem_limit_bytes=8 * MIB),
        name="mesh_update",
    )(*slots, mesh_in, w_enc)


def process_kernel(ids_ref, mid_ref, near_mid_ref, far_mid_ref, near_ref, gain_ref, w_ref, out_ref, *sends):
    count, latent = mid_ref.shape
    block_mesh = sends[0].shape[0]
    around = jnp.concatenate([near_mid_ref[...], mid_ref[...], far_mid_ref[...]], axis=0)
    message = jnp.dot(near_ref[...], around, preferred_element_type=F32)
    power = jnp.mean(message * message, axis=-1, keepdims=True)
    normed = (message * lax.rsqrt(power + 1e-05) * gain_ref[...]).astype(BF16)
    grown = jnp.dot(normed, w_ref[...], preferred_element_type=F32)
    grown = mid_ref[...].astype(F32) + silu(grown)
    out_ref[...] = grown.astype(BF16)
    for s in range(SLOTS):
        chosen = grown[:block_mesh, :]
        for b in range(1, count // block_mesh):
            block = grown[b * block_mesh : (b + 1) * block_mesh, :]
            chosen = jnp.where(ids_ref[s : s + 1, :] == b, block, chosen)
        sends[s][...] = chosen.astype(BF16)


def process(block_mesh, ids, mid, near_mid, far_mid, near, gain, w_proc):
    vmem = pl.BlockSpec(memory_space=pltpu.VMEM)
    latent = mid.shape[1]
    return pl.pallas_call(
        process_kernel,
        in_specs=[vmem] * 7,
        out_specs=[vmem] * (1 + SLOTS),
        out_shape=[jax.ShapeDtypeStruct(mid.shape, BF16)]
        + [jax.ShapeDtypeStruct((block_mesh, latent), BF16)] * SLOTS,
        compiler_params=pltpu.CompilerParams(vmem_limit_bytes=8 * MIB),
        name="mesh_process",
    )(ids, mid, near_mid, far_mid, near, gain, w_proc)


def decode_kernel(width, grid_ref, lat_ref, dsum_ref, w_ref, *rest):
    slots = rest[:SLOTS]
    out_hbm, back_ref, pred_ref, sems = rest[SLOTS:]
    steps = grid_ref.shape[1] // width

    def copy_out(step):
        cols = pl.ds(pl.multiple_of(step * width, width), width)
        return pltpu.make_async_copy(pred_ref.at[:, cols], out_hbm.at[:, cols], sems.at[step])

    joined = jnp.concatenate([slot[...] for slot in slots], axis=0)
    back_ref[...] = joined.astype(F32).T.astype(BF16)

    @pl.loop(0, steps)
    def _(step):
        cols = pl.ds(pl.multiple_of(step * width, width), width)
        decoded = jnp.dot(back_ref[...], dsum_ref[:, cols], preferred_element_type=F32)
        hidden = silu(lat_ref[:, cols].astype(F32) + decoded).astype(BF16)
        pred_ref[:, cols] = (
            grid_ref[:, cols].astype(F32)
            + jnp.dot(w_ref[...], hidden, preferred_element_type=F32)
        ).astype(BF16)
        copy_out(step).start()

    for step in range(steps):
        copy_out(step).wait()


def decode(grid_t, lat_t, dsum, w_out_t, slots):
    channels, points = grid_t.shape
    latent = lat_t.shape[0]
    rows = dsum.shape[0]
    width = 512
    vmem = pl.BlockSpec(memory_space=pltpu.VMEM)
    return pl.pallas_call(
        functools.partial(decode_kernel, width),
        in_specs=[vmem] * (4 + SLOTS),
        out_specs=pl.BlockSpec(memory_space=pl.ANY),
        out_shape=jax.ShapeDtypeStruct((channels, points), BF16),
        scratch_shapes=[
            pltpu.VMEM((latent, rows), BF16),
            pltpu.VMEM((channels, points), BF16),
            pltpu.SemaphoreType.DMA((points // width,)),
        ],
        compiler_params=pltpu.CompilerParams(vmem_limit_bytes=24 * MIB),
        name="decode",
    )(grid_t, lat_t, dsum, w_out_t, *slots)


def local(
    grid_in, w_embed, enc_coef, enc_owner, slot_block, mesh_in, w_enc,
    proc_adj, proc_coef, proc_gain, w_proc, dec_coef, w_out,
):
    parts = lax.axis_size("nodes")
    block_mesh = enc_coef.shape[1]

    def swap(x, slot):
        pairs = [(i, partner(slot, i, parts)) for i in range(parts)]
        return lax.ppermute(x, "nodes", pairs)

    def swap_all(xs):
        return [xs[OWN]] + [swap(xs[s], s) for s in range(1, SLOTS)]

    lat_t, dsum, grid_t, *sums = encode(
        parts, slot_block, enc_owner.reshape(-1, 128), grid_in.T, w_embed, enc_coef,
        jnp.swapaxes(dec_coef, 1, 2),
    )
    received = swap_all(sums)
    near = prepare(parts, proc_adj, proc_coef, sums[OWN])
    mid, ids = update(received, mesh_in, w_enc)
    far_mid = swap(mid, FAR)
    near_mid = swap(mid, NEAR)
    mesh_out, *sends = process(
        block_mesh, ids, mid, near_mid, far_mid, near, proc_gain.reshape(1, -1), w_proc
    )
    returned = swap_all(sends)
    pred_t = decode(grid_t, lat_t, dsum, w_out.T, returned)
    return (pred_t.T, mesh_out)


def solution(mesh):
    return jax.shard_map(
        local,
        mesh=mesh,
        in_specs=(
            P(("groups", "nodes"), None),
            P(),
            P("nodes", None, None),
            P("nodes"),
            P("nodes"),
            P(("groups", "nodes"), None),
            P(),
            P("nodes", None),
            P("nodes", None, None, None),
            P(),
            P(),
            P("nodes", None, None),
            P(),
        ),
        out_specs=(P(("groups", "nodes"), None), P(("groups", "nodes"), None)),
        check_vma=False,
    )
```

```python
import functools

import jax
import jax.numpy as jnp
from jax import lax
from jax.experimental import pallas as pl
from jax.experimental.pallas import tpu as pltpu
from jax.sharding import PartitionSpec as P

F32 = jnp.float32
BF16 = jnp.bfloat16
MIB = 1 << 20
SLOTS = 6
HALF = 5
SQUAD = 4
LANES = 128


def offsets_of(parts):
    return (0, 1, 2, -2, -1, parts // 2)


def squads_of(parts, first):
    return [
        [(at + first + i) % parts for i in range(SQUAD)] for at in range(0, parts, SQUAD)
    ]


def seat(me, offset):
    even = lax.rem(me, SQUAD) + offset
    inside = (even >= 0) & (even < SQUAD)
    odd = jnp.clip(lax.rem(me + 2, SQUAD) + offset, 0, SQUAD - 1)
    return jnp.clip(even, 0, SQUAD - 1), inside, odd


def silu(x):
    half = 0.5 * x
    return half + half * jnp.tanh(half)


def hot_rows(ids, target):
    lanes = ids.shape[1]
    target = target.astype(BF16)
    one, zero = jnp.ones((), BF16), jnp.zeros((), BF16)
    return jnp.concatenate(
        [
            jnp.where(ids == target[:, at : at + lanes], one, zero)
            for at in range(0, target.shape[1], lanes)
        ],
        axis=1,
    )


def fill_targets(parts, per_block, block_mesh, owner_ref, tgt_ref):
    wide = tgt_ref.shape[1]
    me = lax.axis_index("nodes")
    off = owner_ref[...] - me
    off = jnp.where(off < 0, off + parts, off)
    slot = jnp.where(off == parts // 2, HALF, jnp.where(off > 2, off - parts + HALF, off))
    slot = slot.astype(F32)
    groups, lanes = owner_ref.shape
    all_blocks = tgt_ref.shape[0]
    total = jnp.zeros(tgt_ref.shape, F32)
    for r in range(groups):
        tile = lax.broadcasted_iota(jnp.int32, (all_blocks, lanes), 1) + r * lanes
        first = lax.broadcasted_iota(jnp.int32, (all_blocks, lanes), 0) * per_block
        mine = (tile >= first) & (tile < first + per_block)
        picked = jnp.where(mine, slot[r : r + 1, :], 0.0).astype(BF16)
        row = lax.broadcasted_iota(jnp.int32, (lanes, wide), 0) + r * lanes
        col = lax.broadcasted_iota(jnp.int32, (lanes, wide), 1)
        place = row - per_block * ((row * (2**19 // per_block + 1)) >> 19)
        spread = jnp.where(place == col // block_mesh, 1.0, 0.0).astype(BF16)
        total += jnp.dot(picked, spread, preferred_element_type=F32)
    col = lax.broadcasted_iota(jnp.int32, tgt_ref.shape, 1)
    tgt_ref[...] = total * block_mesh + (col % block_mesh).astype(F32)


def encode_kernel(
    parts, width, slot_hbm, owner_hbm, w_hbm, grid_hbm, enc_hbm, dec_hbm,
    lat_ref, dsum_ref, grid_ref, *rest,
):
    even_ref, odd_ref, half_ref = rest[:3]
    (
        slot_ref, owner_ref, w_ref, enc_ref, dec_ref, wt_ref, tgt_ref, ids_ref, msum_ref,
        acc_ref, small_sems, sems,
    ) = rest[3:]
    tiles, block_mesh, block_grid = enc_ref.shape
    channels, points = grid_ref.shape
    latent = w_ref.shape[1]
    per_block = tiles * block_grid // points
    blocks = width // block_grid
    chunk = blocks * per_block
    steps = points // width
    wide = per_block * block_mesh
    rows = SLOTS * block_mesh

    def copies(step):
        cols = pl.ds(pl.multiple_of(step * width, width), width)
        some = pl.ds(step * chunk, chunk)
        return (
            pltpu.make_async_copy(grid_hbm.at[:, cols], grid_ref.at[:, cols], sems.at[0, step]),
            pltpu.make_async_copy(enc_hbm.at[some], enc_ref.at[some], sems.at[1, step]),
            pltpu.make_async_copy(dec_hbm.at[some], dec_ref.at[some], sems.at[2, step]),
        )

    small = [
        pltpu.make_async_copy(source, target, small_sems.at[i])
        for i, (source, target) in enumerate(
            ((owner_hbm, owner_ref), (w_hbm, w_ref), (slot_hbm, slot_ref))
        )
    ]
    for copy in small:
        copy.start()
    for step in range(steps):
        for copy in copies(step):
            copy.start()
    for ref in (even_ref, odd_ref):
        ref[:, :, :latent] = jnp.zeros((SQUAD, block_mesh, latent), BF16)
        ref[:, :, latent:] = jnp.full((SQUAD, block_mesh, LANES), -1.0, BF16)
    ids_ref[...] = lax.broadcasted_iota(jnp.int32, ids_ref.shape, 0).astype(BF16)
    acc_ref[...] = jnp.zeros_like(acc_ref)
    for copy in small:
        copy.wait()
    wt_ref[:, :channels] = w_ref[...].astype(F32).T.astype(BF16)
    fill_targets(parts, per_block, block_mesh, owner_ref, tgt_ref)

    @pl.loop(0, steps)
    def _(step):
        for copy in copies(step):
            copy.wait()
        cols = pl.ds(pl.multiple_of(step * width, width), width)
        for b in range(blocks):
            hot = hot_rows(ids_ref[...], tgt_ref[pl.ds(step * blocks + b, 1), :])
            some = pl.ds(step * chunk + b * per_block, per_block)
            both = jnp.concatenate(
                [
                    enc_ref[some].reshape(wide, block_grid),
                    dec_ref[some].reshape(wide, block_grid),
                ],
                axis=1,
            )
            sums = jnp.dot(hot, both, preferred_element_type=F32).astype(BF16)
            msum_ref[:, b * block_grid : (b + 1) * block_grid] = sums[:, :block_grid]
            first = pl.multiple_of((step * blocks + b) * block_grid, block_grid)
            dsum_ref[:, pl.ds(first, block_grid)] = sums[:, block_grid:]
        lat = silu(
            jnp.dot(wt_ref[:, :channels], grid_ref[:, cols], preferred_element_type=F32)
        ).astype(BF16)
        lat_ref[:, cols] = lat
        acc_ref[...] += lax.dot_general(
            lat, msum_ref[...], (((1,), (1,)), ((), ())), preferred_element_type=F32
        )

    me = lax.axis_index("nodes")
    flipped = acc_ref[...].T.astype(BF16)
    for s, offset in enumerate(offsets_of(parts)):
        block = slot_ref[lax.rem(me + offset + parts, parts)].astype(F32)
        block = jnp.full((block_mesh, LANES), block, F32).astype(BF16)
        mine = jnp.concatenate([flipped[s * block_mesh : (s + 1) * block_mesh, :], block], axis=1)
        if s == HALF:
            half_ref[...] = mine
            continue
        even, inside, odd = seat(me, offset)

        @pl.when(inside)
        def _():
            even_ref[even] = mine

        if offset != 0:

            @pl.when(jnp.logical_not(inside))
            def _():
                odd_ref[odd] = mine


def encode(parts, slot_block, owners, grid_t, w_embed, enc_coef, dec_t):
    channels, points = grid_t.shape
    latent = w_embed.shape[1]
    tiles, block_mesh, block_grid = enc_coef.shape
    grid_blocks = points // block_grid
    width = 512
    steps = points // width
    rows = SLOTS * block_mesh
    wide = tiles // grid_blocks * block_mesh
    vmem = pl.BlockSpec(memory_space=pltpu.VMEM)
    hbm = pl.BlockSpec(memory_space=pl.ANY)
    return pl.pallas_call(
        functools.partial(encode_kernel, parts, width),
        in_specs=[hbm] * 6,
        out_specs=[vmem] * 6,
        out_shape=[
            pltpu.VMEM((latent, points), BF16),
            pltpu.VMEM((rows, points), BF16),
            pltpu.VMEM((channels, points), BF16),
        ]
        + [jax.ShapeDtypeStruct((SQUAD, block_mesh, latent + LANES), BF16)] * 2
        + [jax.ShapeDtypeStruct((block_mesh, latent + LANES), BF16)],
        scratch_shapes=[
            pltpu.SMEM(slot_block.shape, jnp.int32),
            pltpu.VMEM(owners.shape, jnp.int32),
            pltpu.VMEM(w_embed.shape, BF16),
            pltpu.VMEM(enc_coef.shape, BF16),
            pltpu.VMEM(dec_t.shape, BF16),
            pltpu.VMEM((latent, 256), BF16),
            pltpu.VMEM((grid_blocks, wide), F32),
            pltpu.VMEM((rows, 128), BF16),
            pltpu.VMEM((rows, width), BF16),
            pltpu.VMEM((latent, rows), F32),
            pltpu.SemaphoreType.DMA((3,)),
            pltpu.SemaphoreType.DMA((3, steps)),
        ],
        compiler_params=pltpu.CompilerParams(vmem_limit_bytes=24 * MIB),
        name="encode",
    )(
        *(
            pltpu.with_memory_space_constraint(x, pltpu.HBM)
            for x in (slot_block, owners, w_embed, grid_t, enc_coef, dec_t)
        )
    )


def prepare_kernel(parts, adj_ref, coef_ref, after_ref, near_ref):
    mesh_blocks, adj_width = adj_ref.shape
    block_mesh = coef_ref.shape[2]
    me = lax.axis_index("nodes")
    core = lax.rem(me, 2)
    columns = near_ref.shape[1]
    row = lax.broadcasted_iota(jnp.int32, (block_mesh, columns), 0)
    col = lax.broadcasted_iota(jnp.int32, (block_mesh, columns), 1)
    for b in range(mesh_blocks):
        total = jnp.zeros((block_mesh, columns), F32)
        for a in range(adj_width):
            which = adj_ref[b, a]
            listed = jnp.maximum(which, 0)
            side = lax.rem(lax.div(listed, mesh_blocks) - me + 1 + parts, parts)
            side = jnp.where(core == 0, 2 - side, side)
            place = side * mesh_blocks + lax.rem(listed, mesh_blocks)
            place = jnp.where(which >= 0, place, -columns)
            spot = jnp.where(col == place * block_mesh + row, 1.0, 0.0).astype(BF16)
            total += jnp.dot(coef_ref[b, a], spot, preferred_element_type=F32)
        near_ref[b * block_mesh : (b + 1) * block_mesh, :] = total.astype(BF16)


def prepare(parts, adj, coef, after):
    mesh_blocks, adj_width, block_mesh, _ = coef.shape
    count = mesh_blocks * block_mesh
    vmem = pl.BlockSpec(memory_space=pltpu.VMEM)
    return pl.pallas_call(
        functools.partial(prepare_kernel, parts),
        in_specs=[pl.BlockSpec(memory_space=pltpu.SMEM), vmem, vmem],
        out_specs=vmem,
        out_shape=jax.ShapeDtypeStruct((count, 3 * count), BF16),
        compiler_params=pltpu.CompilerParams(vmem_limit_bytes=8 * MIB),
        cost_estimate=pl.CostEstimate(
            flops=2 * adj_width * count * block_mesh * 3 * count,
            bytes_accessed=8 * count * 3 * count,
            transcendentals=0,
        ),
        name="prepare",
    )(adj, coef, after)


def update_kernel(even_ref, odd_ref, half_ref, mesh_ref, w_ref, mid_ref, ids_ref):
    count, latent = mesh_ref.shape
    block_mesh = half_ref.shape[0]
    chunks = [ref[i] for ref in (even_ref, odd_ref) for i in range(SQUAD)] + [half_ref[...]]
    sums = [chunk[:, :latent].astype(F32) for chunk in chunks]
    ids = [chunk[:, latent:].astype(F32)[:1, :1] for chunk in chunks]
    for i, block in enumerate(ids):
        ids_ref[i : i + 1, :] = jnp.broadcast_to(block, (1, latent))
    blocks = []
    for b in range(count // block_mesh):
        total = jnp.zeros((block_mesh, latent), F32)
        for block, part in zip(ids, sums):
            total += jnp.where(block == b, part, 0.0)
        blocks.append(total.astype(BF16))
    grown = jnp.dot(jnp.concatenate(blocks, axis=0), w_ref[...], preferred_element_type=F32)
    mid_ref[...] = (mesh_ref[...].astype(F32) + silu(grown)).astype(BF16)


def update(even, odd, half, mesh_in, w_enc):
    vmem = pl.BlockSpec(memory_space=pltpu.VMEM)
    return pl.pallas_call(
        update_kernel,
        in_specs=[vmem] * 5,
        out_specs=[vmem] * 2,
        out_shape=[
            jax.ShapeDtypeStruct(mesh_in.shape, BF16),
            jax.ShapeDtypeStruct((16, mesh_in.shape[1]), F32),
        ],
        compiler_params=pltpu.CompilerParams(vmem_limit_bytes=8 * MIB),
        name="mesh_update",
    )(even, odd, half, mesh_in, w_enc)


def process_kernel(
    ids_ref, mid_ref, near_mid_ref, far_mid_ref, near_ref, gain_ref, w_ref,
    out_ref, even_ref, odd_ref, half_ref,
):
    count, latent = mid_ref.shape
    block_mesh = half_ref.shape[0]
    around = jnp.concatenate([near_mid_ref[...], mid_ref[...], far_mid_ref[...]], axis=0)
    message = jnp.dot(near_ref[...], around, preferred_element_type=F32)
    power = jnp.mean(message * message, axis=-1, keepdims=True)
    normed = (message * lax.rsqrt(power + 1e-05) * gain_ref[...]).astype(BF16)
    grown = jnp.dot(normed, w_ref[...], preferred_element_type=F32)
    grown = mid_ref[...].astype(F32) + silu(grown)
    out_ref[...] = grown.astype(BF16)
    for i in range(2 * SQUAD + 1):
        chosen = grown[:block_mesh, :]
        for b in range(1, count // block_mesh):
            block = grown[b * block_mesh : (b + 1) * block_mesh, :]
            chosen = jnp.where(ids_ref[i : i + 1, :] == b, block, chosen)
        if i < SQUAD:
            even_ref[i] = chosen.astype(BF16)
        elif i < 2 * SQUAD:
            odd_ref[i - SQUAD] = chosen.astype(BF16)
        else:
            half_ref[...] = chosen.astype(BF16)


def process(block_mesh, ids, mid, near_mid, far_mid, near, gain, w_proc):
    vmem = pl.BlockSpec(memory_space=pltpu.VMEM)
    latent = mid.shape[1]
    return pl.pallas_call(
        process_kernel,
        in_specs=[vmem] * 7,
        out_specs=[vmem] * 4,
        out_shape=[jax.ShapeDtypeStruct(mid.shape, BF16)]
        + [jax.ShapeDtypeStruct((SQUAD, block_mesh, latent), BF16)] * 2
        + [jax.ShapeDtypeStruct((block_mesh, latent), BF16)],
        compiler_params=pltpu.CompilerParams(vmem_limit_bytes=8 * MIB),
        name="mesh_process",
    )(ids, mid, near_mid, far_mid, near, gain, w_proc)


def decode_kernel(
    parts, width, grid_ref, lat_ref, dsum_ref, w_ref, even_ref, odd_ref, half_ref,
    out_hbm, join_ref, back_ref, pred_ref, sems,
):
    steps = grid_ref.shape[1] // width

    def copy_out(step):
        cols = pl.ds(pl.multiple_of(step * width, width), width)
        return pltpu.make_async_copy(pred_ref.at[:, cols], out_hbm.at[:, cols], sems.at[step])

    me = lax.axis_index("nodes")
    block_mesh = half_ref.shape[0]
    for s, offset in enumerate(offsets_of(parts)):
        rows = slice(s * block_mesh, (s + 1) * block_mesh)
        if s == HALF:
            join_ref[rows, :] = half_ref[...].astype(F32)
            continue
        even, inside, odd = seat(me, offset)

        @pl.when(inside)
        def _():
            join_ref[rows, :] = even_ref[even].astype(F32)

        if offset != 0:

            @pl.when(jnp.logical_not(inside))
            def _():
                join_ref[rows, :] = odd_ref[odd].astype(F32)

    back_ref[...] = join_ref[...].T.astype(BF16)

    @pl.loop(0, steps)
    def _(step):
        cols = pl.ds(pl.multiple_of(step * width, width), width)
        decoded = jnp.dot(back_ref[...], dsum_ref[:, cols], preferred_element_type=F32)
        hidden = silu(lat_ref[:, cols].astype(F32) + decoded).astype(BF16)
        pred_ref[:, cols] = (
            grid_ref[:, cols].astype(F32)
            + jnp.dot(w_ref[...], hidden, preferred_element_type=F32)
        ).astype(BF16)
        copy_out(step).start()

    for step in range(steps):
        copy_out(step).wait()


def decode(parts, grid_t, lat_t, dsum, w_out_t, even, odd, half):
    channels, points = grid_t.shape
    latent = lat_t.shape[0]
    rows = dsum.shape[0]
    width = 512
    vmem = pl.BlockSpec(memory_space=pltpu.VMEM)
    return pl.pallas_call(
        functools.partial(decode_kernel, parts, width),
        in_specs=[vmem] * 7,
        out_specs=pl.BlockSpec(memory_space=pl.ANY),
        out_shape=jax.ShapeDtypeStruct((channels, points), BF16),
        scratch_shapes=[
            pltpu.VMEM((rows, latent), F32),
            pltpu.VMEM((latent, rows), BF16),
            pltpu.VMEM((channels, points), BF16),
            pltpu.SemaphoreType.DMA((points // width,)),
        ],
        compiler_params=pltpu.CompilerParams(vmem_limit_bytes=24 * MIB),
        name="decode",
    )(grid_t, lat_t, dsum, w_out_t, even, odd, half)


def local(
    grid_in, w_embed, enc_coef, enc_owner, slot_block, mesh_in, w_enc,
    proc_adj, proc_coef, proc_gain, w_proc, dec_coef, w_out,
):
    parts = lax.axis_size("nodes")
    block_mesh = enc_coef.shape[1]

    def swap(x, to):
        return lax.ppermute(x, "nodes", [(i, to(i) % parts) for i in range(parts)])

    def exchange(even, odd, half):
        half = swap(half, lambda i: i + parts // 2)
        odd, even = (
            lax.all_to_all(
                x, "nodes", split_axis=0, concat_axis=0, tiled=True,
                axis_index_groups=squads_of(parts, first),
            )
            for x, first in ((odd, 2), (even, 0))
        )
        return even, odd, half

    lat_t, dsum, grid_t, *sums = encode(
        parts, slot_block, enc_owner.reshape(-1, 128), grid_in.T, w_embed, enc_coef,
        jnp.swapaxes(dec_coef, 1, 2),
    )
    near = prepare(parts, proc_adj, proc_coef, sums[-1])
    mid, ids = update(*exchange(*sums), mesh_in, w_enc)
    far_mid = swap(mid, lambda i: i + 2 * (i % 2) - 1)
    near_mid = swap(mid, lambda i: i + 1 - 2 * (i % 2))
    mesh_out, *sends = process(
        block_mesh, ids, mid, near_mid, far_mid, near, proc_gain.reshape(1, -1), w_proc
    )
    pred_t = decode(parts, grid_t, lat_t, dsum, w_out.T, *exchange(*sends))
    return (pred_t.T, mesh_out)


def solution(mesh):
    return jax.shard_map(
        local,
        mesh=mesh,
        in_specs=(
            P(("groups", "nodes"), None),
            P(),
            P("nodes", None, None),
            P("nodes"),
            P("nodes"),
            P(("groups", "nodes"), None),
            P(),
            P("nodes", None),
            P("nodes", None, None, None),
            P(),
            P(),
            P("nodes", None, None),
            P(),
        ),
        out_specs=(P(("groups", "nodes"), None), P(("groups", "nodes"), None)),
        check_vma=False,
    )
```

```python
import functools

import jax
import jax.numpy as jnp
from jax import lax
from jax.experimental import pallas as pl
from jax.experimental.pallas import tpu as pltpu
from jax.sharding import PartitionSpec as P

F32 = jnp.float32
BF16 = jnp.bfloat16
MIB = 1 << 20
OWN, HALF, ODD, FAR, EVEN, NEAR = range(6)
SLOTS = 6
PAD = 128
AHEAD = 3


def partner(slot, me, parts):
    chip = me // 2 % 2
    core = me % 2
    step = {
        OWN: 0,
        HALF: parts // 2,
        ODD: 4 * chip - 2,
        EVEN: 2 - 4 * chip,
        FAR: 2 * core - 1,
        NEAR: 1 - 2 * core,
    }[slot]
    return (me + step + parts) % parts


def scalar_partner(slot, me, parts):
    chip = lax.rem(lax.div(me, 2), 2)
    core = lax.rem(me, 2)
    step = {
        OWN: 0,
        HALF: parts // 2,
        ODD: 4 * chip - 2,
        EVEN: 2 - 4 * chip,
        FAR: 2 * core - 1,
        NEAR: 1 - 2 * core,
    }[slot]
    return lax.rem(me + step + parts, parts)


def silu(x):
    half = 0.5 * x
    return half + half * jnp.tanh(half)


def hot_rows(ids, target):
    lanes = ids.shape[1]
    target = target.astype(BF16)
    one, zero = jnp.ones((), BF16), jnp.zeros((), BF16)
    return jnp.concatenate(
        [
            jnp.where(ids == target[:, at : at + lanes], one, zero)
            for at in range(0, target.shape[1], lanes)
        ],
        axis=1,
    )


def fill_targets(parts, per_block, block_mesh, owner_ref, tgt_ref):
    wide = tgt_ref.shape[1]
    me = lax.axis_index("nodes")
    chip = lax.rem(lax.div(me, 2), 2)
    core = lax.rem(me, 2)
    up2 = EVEN + (ODD - EVEN) * chip
    up1 = NEAR + (FAR - NEAR) * core
    off = owner_ref[...] - me
    off = jnp.where(off < 0, off + parts, off)
    slot = jnp.where(off == parts // 2, HALF, OWN)
    slot = jnp.where(off == 2, up2, slot)
    slot = jnp.where(off == parts - 2, ODD + EVEN - up2, slot)
    slot = jnp.where(off == 1, up1, slot)
    slot = jnp.where(off == parts - 1, NEAR + FAR - up1, slot)
    slot = slot.astype(F32)
    groups, lanes = owner_ref.shape
    all_blocks = tgt_ref.shape[0]
    total = jnp.zeros(tgt_ref.shape, F32)
    for r in range(groups):
        tile = lax.broadcasted_iota(jnp.int32, (all_blocks, lanes), 1) + r * lanes
        first = lax.broadcasted_iota(jnp.int32, (all_blocks, lanes), 0) * per_block
        mine = (tile >= first) & (tile < first + per_block)
        picked = jnp.where(mine, slot[r : r + 1, :], 0.0).astype(BF16)
        row = lax.broadcasted_iota(jnp.int32, (lanes, wide), 0) + r * lanes
        col = lax.broadcasted_iota(jnp.int32, (lanes, wide), 1)
        place = row - per_block * ((row * (2**19 // per_block + 1)) >> 19)
        spread = jnp.where(place == col // block_mesh, 1.0, 0.0).astype(BF16)
        total += jnp.dot(picked, spread, preferred_element_type=F32)
    col = lax.broadcasted_iota(jnp.int32, tgt_ref.shape, 1)
    tgt_ref[...] = total * block_mesh + (col % block_mesh).astype(F32)


def encode_kernel(
    parts, width, slot_hbm, owner_hbm, w_hbm, grid_hbm, enc_hbm, dec_hbm,
    lat_ref, dsum_ref, grid_ref, *rest,
):
    send_refs = rest[:SLOTS]
    (
        slot_ref, owner_ref, w_ref, enc_ref, dec_ref, wt_ref, tgt_ref, ids_ref, msum_ref,
        hold_ref, acc_ref, small_sems, sems,
    ) = rest[SLOTS:]
    tiles, block_mesh, block_grid = enc_ref.shape
    channels, points = grid_ref.shape
    latent = w_ref.shape[1]
    per_block = tiles * block_grid // points
    blocks = width // block_grid
    chunk = blocks * per_block
    steps = points // width
    wide = per_block * block_mesh
    rows = SLOTS * block_mesh

    def copies(step):
        cols = pl.ds(pl.multiple_of(step * width, width), width)
        some = pl.ds(step * chunk, chunk)
        return (
            pltpu.make_async_copy(grid_hbm.at[:, cols], grid_ref.at[:, cols], sems.at[0, step]),
            pltpu.make_async_copy(enc_hbm.at[some], enc_ref.at[some], sems.at[1, step]),
            pltpu.make_async_copy(dec_hbm.at[some], dec_ref.at[some], sems.at[2, step]),
        )

    small = [
        pltpu.make_async_copy(source, target, small_sems.at[i])
        for i, (source, target) in enumerate(
            ((owner_hbm, owner_ref), (w_hbm, w_ref), (slot_hbm, slot_ref))
        )
    ]
    for copy in small:
        copy.start()
    def start(step):
        for copy in copies(step):
            copy.start()

    for step in range(AHEAD):
        start(step)
    ids_ref[...] = lax.broadcasted_iota(jnp.int32, ids_ref.shape, 0).astype(BF16)
    acc_ref[...] = jnp.zeros_like(acc_ref)
    msum_ref[1] = jnp.zeros(msum_ref.shape[1:], BF16)
    hold_ref[1] = jnp.zeros(hold_ref.shape[1:], BF16)
    for copy in small:
        copy.wait()
    wt_ref[:, :channels] = w_ref[...].astype(F32).T.astype(BF16)
    fill_targets(parts, per_block, block_mesh, owner_ref, tgt_ref)

    def collect(slot):
        acc_ref[...] += lax.dot_general(
            hold_ref[slot], msum_ref[slot], (((1,), (1,)), ((), ())), preferred_element_type=F32
        )

    @pl.loop(0, steps // 2)
    def _(pair):
        for slot in range(2):
            step = 2 * pair + slot

            @pl.when(step + AHEAD < steps)
            def _():
                start(step + AHEAD)

            for copy in copies(step):
                copy.wait()
            collect(1 - slot)
            cols = pl.ds(pl.multiple_of(step * width, width), width)
            for b in range(blocks):
                hot = hot_rows(ids_ref[...], tgt_ref[pl.ds(step * blocks + b, 1), :])
                some = pl.ds(step * chunk + b * per_block, per_block)
                both = jnp.concatenate(
                    [
                        enc_ref[some].reshape(wide, block_grid),
                        dec_ref[some].reshape(wide, block_grid),
                    ],
                    axis=1,
                )
                sums = jnp.dot(hot, both, preferred_element_type=F32).astype(BF16)
                msum_ref[slot, :, b * block_grid : (b + 1) * block_grid] = sums[:, :block_grid]
                first = pl.multiple_of((step * blocks + b) * block_grid, block_grid)
                dsum_ref[:, pl.ds(first, block_grid)] = sums[:, block_grid:]
            for half in range(0, width, 256):
                part = pl.ds(pl.multiple_of(step * width + half, 256), 256)
                lat = silu(
                    jnp.dot(
                        wt_ref[:, :channels], grid_ref[:, part], preferred_element_type=F32
                    )
                ).astype(BF16)
                lat_ref[:, part] = lat
                hold_ref[slot, :, half : half + 256] = lat

    collect(1)
    me = lax.axis_index("nodes")
    flipped = acc_ref[...].T.astype(BF16)
    for s in range(SLOTS):
        send_refs[s][:, :latent] = flipped[s * block_mesh : (s + 1) * block_mesh, :]
        block = slot_ref[scalar_partner(s, me, parts)].astype(F32)
        send_refs[s][:, latent:] = jnp.full((block_mesh, PAD), block, F32).astype(BF16)


def encode(parts, slot_block, owners, grid_t, w_embed, enc_coef, dec_t):
    channels, points = grid_t.shape
    latent = w_embed.shape[1]
    tiles, block_mesh, block_grid = enc_coef.shape
    grid_blocks = points // block_grid
    width = 512
    steps = points // width
    rows = SLOTS * block_mesh
    wide = tiles // grid_blocks * block_mesh
    vmem = pl.BlockSpec(memory_space=pltpu.VMEM)
    hbm = pl.BlockSpec(memory_space=pl.ANY)
    return pl.pallas_call(
        functools.partial(encode_kernel, parts, width),
        in_specs=[hbm] * 6,
        out_specs=[vmem] * (3 + SLOTS),
        out_shape=[
            pltpu.VMEM((latent, points), BF16),
            pltpu.VMEM((rows, points), BF16),
            pltpu.VMEM((channels, points), BF16),
        ]
        + [jax.ShapeDtypeStruct((block_mesh, latent + PAD), BF16)] * SLOTS,
        scratch_shapes=[
            pltpu.SMEM(slot_block.shape, jnp.int32),
            pltpu.VMEM(owners.shape, jnp.int32),
            pltpu.VMEM(w_embed.shape, BF16),
            pltpu.VMEM(enc_coef.shape, BF16),
            pltpu.VMEM(dec_t.shape, BF16),
            pltpu.VMEM((latent, 256), BF16),
            pltpu.VMEM((grid_blocks, wide), F32),
            pltpu.VMEM((rows, 128), BF16),
            pltpu.VMEM((2, rows, width), BF16),
            pltpu.VMEM((2, latent, width), BF16),
            pltpu.VMEM((latent, rows), F32),
            pltpu.SemaphoreType.DMA((3,)),
            pltpu.SemaphoreType.DMA((3, steps)),
        ],
        compiler_params=pltpu.CompilerParams(vmem_limit_bytes=24 * MIB),
        name="encode",
    )(
        *(
            pltpu.with_memory_space_constraint(x, pltpu.HBM)
            for x in (slot_block, owners, w_embed, grid_t, enc_coef, dec_t)
        )
    )


def prepare_kernel(parts, adj_ref, coef_ref, after_ref, near_ref):
    mesh_blocks, adj_width = adj_ref.shape
    block_mesh = coef_ref.shape[2]
    me = lax.axis_index("nodes")
    core = lax.rem(me, 2)
    columns = near_ref.shape[1]
    row = lax.broadcasted_iota(jnp.int32, (block_mesh, columns), 0)
    col = lax.broadcasted_iota(jnp.int32, (block_mesh, columns), 1)
    for b in range(mesh_blocks):
        total = jnp.zeros((block_mesh, columns), F32)
        for a in range(adj_width):
            which = adj_ref[b, a]
            listed = jnp.maximum(which, 0)
            side = lax.rem(lax.div(listed, mesh_blocks) - me + 1 + parts, parts)
            side = jnp.where(core == 0, 2 - side, side)
            place = side * mesh_blocks + lax.rem(listed, mesh_blocks)
            place = jnp.where(which >= 0, place, -columns)
            spot = jnp.where(col == place * block_mesh + row, 1.0, 0.0).astype(BF16)
            total += jnp.dot(coef_ref[b, a], spot, preferred_element_type=F32)
        near_ref[b * block_mesh : (b + 1) * block_mesh, :] = total.astype(BF16)


def prepare(parts, adj, coef, after):
    mesh_blocks, adj_width, block_mesh, _ = coef.shape
    count = mesh_blocks * block_mesh
    vmem = pl.BlockSpec(memory_space=pltpu.VMEM)
    return pl.pallas_call(
        functools.partial(prepare_kernel, parts),
        in_specs=[pl.BlockSpec(memory_space=pltpu.SMEM), vmem, vmem],
        out_specs=vmem,
        out_shape=jax.ShapeDtypeStruct((count, 3 * count), BF16),
        compiler_params=pltpu.CompilerParams(vmem_limit_bytes=8 * MIB),
        cost_estimate=pl.CostEstimate(
            flops=2 * adj_width * count * block_mesh * 3 * count,
            bytes_accessed=8 * count * 3 * count,
            transcendentals=0,
        ),
        name="prepare",
    )(adj, coef, after)


def update_kernel(*refs):
    slots = refs[:SLOTS]
    mesh_ref, w_ref, mid_ref, ids_ref = refs[SLOTS:]
    count, latent = mesh_ref.shape
    block_mesh = slots[0].shape[0]
    sums = [slot[:, :latent].astype(F32) for slot in slots]
    ids = [slot[:, latent:].astype(F32)[:1, :1] for slot in slots]
    for s in range(SLOTS):
        ids_ref[s : s + 1, :] = jnp.broadcast_to(ids[s], (1, latent))
    parts = []
    for b in range(count // block_mesh):
        total = jnp.zeros((block_mesh, latent), F32)
        for s in range(SLOTS):
            total += jnp.where(ids[s] == b, sums[s], 0.0)
        parts.append(total.astype(BF16))
    grown = jnp.dot(jnp.concatenate(parts, axis=0), w_ref[...], preferred_element_type=F32)
    mid_ref[...] = (mesh_ref[...].astype(F32) + silu(grown)).astype(BF16)


def update(slots, mesh_in, w_enc):
    vmem = pl.BlockSpec(memory_space=pltpu.VMEM)
    return pl.pallas_call(
        update_kernel,
        in_specs=[vmem] * (SLOTS + 2),
        out_specs=[vmem] * 2,
        out_shape=[
            jax.ShapeDtypeStruct(mesh_in.shape, BF16),
            jax.ShapeDtypeStruct((8, mesh_in.shape[1]), F32),
        ],
        compiler_params=pltpu.CompilerParams(vmem_limit_bytes=8 * MIB),
        name="mesh_update",
    )(*slots, mesh_in, w_enc)


def process_kernel(ids_ref, mid_ref, near_mid_ref, far_mid_ref, near_ref, gain_ref, w_ref, out_ref, *sends):
    count, latent = mid_ref.shape
    block_mesh = sends[0].shape[0]
    around = jnp.concatenate([near_mid_ref[...], mid_ref[...], far_mid_ref[...]], axis=0)
    message = jnp.dot(near_ref[...], around, preferred_element_type=F32)
    power = jnp.mean(message * message, axis=-1, keepdims=True)
    normed = (message * lax.rsqrt(power + 1e-05) * gain_ref[...]).astype(BF16)
    grown = jnp.dot(normed, w_ref[...], preferred_element_type=F32)
    grown = mid_ref[...].astype(F32) + silu(grown)
    out_ref[...] = grown.astype(BF16)
    for s in range(SLOTS):
        chosen = grown[:block_mesh, :]
        for b in range(1, count // block_mesh):
            block = grown[b * block_mesh : (b + 1) * block_mesh, :]
            chosen = jnp.where(ids_ref[s : s + 1, :] == b, block, chosen)
        sends[s][...] = chosen.astype(BF16)


def process(block_mesh, ids, mid, near_mid, far_mid, near, gain, w_proc):
    vmem = pl.BlockSpec(memory_space=pltpu.VMEM)
    latent = mid.shape[1]
    return pl.pallas_call(
        process_kernel,
        in_specs=[vmem] * 7,
        out_specs=[vmem] * (1 + SLOTS),
        out_shape=[jax.ShapeDtypeStruct(mid.shape, BF16)]
        + [jax.ShapeDtypeStruct((block_mesh, latent), BF16)] * SLOTS,
        compiler_params=pltpu.CompilerParams(vmem_limit_bytes=8 * MIB),
        name="mesh_process",
    )(ids, mid, near_mid, far_mid, near, gain, w_proc)


def decode_kernel(width, grid_ref, lat_ref, dsum_ref, w_ref, *rest):
    slots = rest[:SLOTS]
    out_hbm, back_ref, pred_ref, hold_ref, sems = rest[SLOTS:]
    steps = grid_ref.shape[1] // width

    def copy_out(step):
        cols = pl.ds(pl.multiple_of(step * width, width), width)
        return pltpu.make_async_copy(pred_ref.at[:, cols], out_hbm.at[:, cols], sems.at[step])

    joined = jnp.concatenate([slot[...] for slot in slots], axis=0)
    back_ref[...] = joined.astype(F32).T.astype(BF16)

    hold_ref[1] = jnp.zeros(hold_ref.shape[1:], BF16)

    def predict(step, slot):
        cols = pl.ds(pl.multiple_of(step * width, width), width)
        pred_ref[:, cols] = (
            grid_ref[:, cols].astype(F32)
            + jnp.dot(w_ref[...], hold_ref[slot], preferred_element_type=F32)
        ).astype(BF16)

    @pl.loop(0, steps // 2)
    def _(pair):
        for slot in range(2):
            step = 2 * pair + slot
            before = jnp.maximum(step - 1, 0)
            predict(before, 1 - slot)
            for half in range(0, width, 256):
                part = pl.ds(pl.multiple_of(step * width + half, 256), 256)
                decoded = jnp.dot(back_ref[...], dsum_ref[:, part], preferred_element_type=F32)
                hidden = silu(lat_ref[:, part].astype(F32) + decoded)
                hold_ref[slot, :, half : half + 256] = hidden.astype(BF16)

            @pl.when(step > 0)
            def _():
                copy_out(before).start()

    predict(steps - 1, 1)
    copy_out(steps - 1).start()
    for step in range(steps):
        copy_out(step).wait()


def decode(grid_t, lat_t, dsum, w_out_t, slots):
    channels, points = grid_t.shape
    latent = lat_t.shape[0]
    rows = dsum.shape[0]
    width = 512
    vmem = pl.BlockSpec(memory_space=pltpu.VMEM)
    return pl.pallas_call(
        functools.partial(decode_kernel, width),
        in_specs=[vmem] * (4 + SLOTS),
        out_specs=pl.BlockSpec(memory_space=pl.ANY),
        out_shape=jax.ShapeDtypeStruct((channels, points), BF16),
        scratch_shapes=[
            pltpu.VMEM((latent, rows), BF16),
            pltpu.VMEM((channels, points), BF16),
            pltpu.VMEM((2, latent, width), BF16),
            pltpu.SemaphoreType.DMA((points // width,)),
        ],
        compiler_params=pltpu.CompilerParams(vmem_limit_bytes=24 * MIB),
        name="decode",
    )(grid_t, lat_t, dsum, w_out_t, *slots)


def local(
    grid_in, w_embed, enc_coef, enc_owner, slot_block, mesh_in, w_enc,
    proc_adj, proc_coef, proc_gain, w_proc, dec_coef, w_out,
):
    parts = lax.axis_size("nodes")
    block_mesh = enc_coef.shape[1]

    def swap(x, slot):
        pairs = [(i, partner(slot, i, parts)) for i in range(parts)]
        return lax.ppermute(x, "nodes", pairs)

    def swap_all(xs):
        return [xs[OWN]] + [swap(xs[s], s) for s in range(1, SLOTS)]

    lat_t, dsum, grid_t, *sums = encode(
        parts, slot_block, enc_owner.reshape(-1, 128), grid_in.T, w_embed, enc_coef,
        jnp.swapaxes(dec_coef, 1, 2),
    )
    received = swap_all(sums)
    near = prepare(parts, proc_adj, proc_coef, sums[OWN])
    mid, ids = update(received, mesh_in, w_enc)
    far_mid = swap(mid, FAR)
    near_mid = swap(mid, NEAR)
    mesh_out, *sends = process(
        block_mesh, ids, mid, near_mid, far_mid, near, proc_gain.reshape(1, -1), w_proc
    )
    returned = swap_all(sends)
    pred_t = decode(grid_t, lat_t, dsum, w_out.T, returned)
    return (pred_t.T, mesh_out)


def solution(mesh):
    return jax.shard_map(
        local,
        mesh=mesh,
        in_specs=(
            P(("groups", "nodes"), None),
            P(),
            P("nodes", None, None),
            P("nodes"),
            P("nodes"),
            P(("groups", "nodes"), None),
            P(),
            P("nodes", None),
            P("nodes", None, None, None),
            P(),
            P(),
            P("nodes", None, None),
            P(),
        ),
        out_specs=(P(("groups", "nodes"), None), P(("groups", "nodes"), None)),
        check_vma=False,
    )
```

```python
import functools

import jax
import jax.numpy as jnp
from jax import lax
from jax.experimental import pallas as pl
from jax.experimental.pallas import tpu as pltpu
from jax.sharding import PartitionSpec as P

F32 = jnp.float32
BF16 = jnp.bfloat16
MIB = 1 << 20
OWN, HALF, ODD, FAR, EVEN, NEAR = range(6)
SLOTS = 6
PAD = 128
AHEAD = 3
TALL = 128


def partner(slot, me, parts):
    chip = me // 2 % 2
    core = me % 2
    step = {
        OWN: 0,
        HALF: parts // 2,
        ODD: 4 * chip - 2,
        EVEN: 2 - 4 * chip,
        FAR: 2 * core - 1,
        NEAR: 1 - 2 * core,
    }[slot]
    return (me + step + parts) % parts


def scalar_partner(slot, me, parts):
    chip = lax.rem(lax.div(me, 2), 2)
    core = lax.rem(me, 2)
    step = {
        OWN: 0,
        HALF: parts // 2,
        ODD: 4 * chip - 2,
        EVEN: 2 - 4 * chip,
        FAR: 2 * core - 1,
        NEAR: 1 - 2 * core,
    }[slot]
    return lax.rem(me + step + parts, parts)


def silu(x):
    half = 0.5 * x
    return half + half * jnp.tanh(half)


def hot_rows(ids, target):
    lanes = ids.shape[1]
    target = target.astype(BF16)
    one, zero = jnp.ones((), BF16), jnp.zeros((), BF16)
    return jnp.concatenate(
        [
            jnp.where(ids == target[:, at : at + lanes], one, zero)
            for at in range(0, target.shape[1], lanes)
        ],
        axis=1,
    )


def fill_targets(parts, per_block, block_mesh, owner_ref, tgt_ref):
    wide = tgt_ref.shape[1]
    me = lax.axis_index("nodes")
    chip = lax.rem(lax.div(me, 2), 2)
    core = lax.rem(me, 2)
    up2 = EVEN + (ODD - EVEN) * chip
    up1 = NEAR + (FAR - NEAR) * core
    off = owner_ref[...] - me
    off = jnp.where(off < 0, off + parts, off)
    slot = jnp.where(off == parts // 2, HALF, OWN)
    slot = jnp.where(off == 2, up2, slot)
    slot = jnp.where(off == parts - 2, ODD + EVEN - up2, slot)
    slot = jnp.where(off == 1, up1, slot)
    slot = jnp.where(off == parts - 1, NEAR + FAR - up1, slot)
    slot = slot.astype(F32)
    groups, lanes = owner_ref.shape
    all_blocks = tgt_ref.shape[0]
    total = jnp.zeros(tgt_ref.shape, F32)
    for r in range(groups):
        tile = lax.broadcasted_iota(jnp.int32, (all_blocks, lanes), 1) + r * lanes
        first = lax.broadcasted_iota(jnp.int32, (all_blocks, lanes), 0) * per_block
        mine = (tile >= first) & (tile < first + per_block)
        picked = jnp.where(mine, slot[r : r + 1, :], 0.0).astype(BF16)
        row = lax.broadcasted_iota(jnp.int32, (lanes, wide), 0) + r * lanes
        col = lax.broadcasted_iota(jnp.int32, (lanes, wide), 1)
        place = row - per_block * ((row * (2**19 // per_block + 1)) >> 19)
        spread = jnp.where(place == col // block_mesh, 1.0, 0.0).astype(BF16)
        total += jnp.dot(picked, spread, preferred_element_type=F32)
    col = lax.broadcasted_iota(jnp.int32, tgt_ref.shape, 1)
    tgt_ref[...] = total * block_mesh + (col % block_mesh).astype(F32)


def encode_kernel(
    parts, width, slot_hbm, owner_hbm, w_hbm, grid_hbm, enc_hbm, dec_hbm,
    lat_ref, dsum_ref, grid_ref, *rest,
):
    send_refs = rest[:SLOTS]
    (
        slot_ref, owner_ref, w_ref, enc_ref, dec_ref, wt_ref, tgt_ref, ids_ref, msum_ref,
        hold_ref, acc_ref, small_sems, sems,
    ) = rest[SLOTS:]
    tiles, block_mesh, block_grid = enc_ref.shape
    channels, points = grid_ref.shape
    latent = w_ref.shape[1]
    per_block = tiles * block_grid // points
    blocks = width // block_grid
    chunk = blocks * per_block
    steps = points // width
    wide = per_block * block_mesh
    rows = SLOTS * block_mesh

    def copies(step):
        cols = pl.ds(pl.multiple_of(step * width, width), width)
        some = pl.ds(step * chunk, chunk)
        return (
            pltpu.make_async_copy(grid_hbm.at[:, cols], grid_ref.at[:, cols], sems.at[0, step]),
            pltpu.make_async_copy(enc_hbm.at[some], enc_ref.at[some], sems.at[1, step]),
            pltpu.make_async_copy(dec_hbm.at[some], dec_ref.at[some], sems.at[2, step]),
        )

    small = [
        pltpu.make_async_copy(source, target, small_sems.at[i])
        for i, (source, target) in enumerate(
            ((owner_hbm, owner_ref), (w_hbm, w_ref), (slot_hbm, slot_ref))
        )
    ]
    for copy in small:
        copy.start()
    def start(step):
        for copy in copies(step):
            copy.start()

    for step in range(AHEAD):
        start(step)
    ids_ref[...] = lax.broadcasted_iota(jnp.int32, ids_ref.shape, 0).astype(BF16)
    acc_ref[...] = jnp.zeros_like(acc_ref)
    msum_ref[1] = jnp.zeros(msum_ref.shape[1:], BF16)
    hold_ref[1] = jnp.zeros(hold_ref.shape[1:], BF16)
    for copy in small:
        copy.wait()
    wt_ref[:, :channels] = w_ref[...].astype(F32).T.astype(BF16)
    fill_targets(parts, per_block, block_mesh, owner_ref, tgt_ref)

    def collect(slot):
        for top in range(0, latent, TALL):
            acc_ref[top : top + TALL, :] += lax.dot_general(
                hold_ref[slot, top : top + TALL, :], msum_ref[slot], (((1,), (1,)), ((), ())),
                preferred_element_type=F32,
            )

    @pl.loop(0, steps // 2)
    def _(pair):
        for slot in range(2):
            step = 2 * pair + slot

            @pl.when(step + AHEAD < steps)
            def _():
                start(step + AHEAD)

            for copy in copies(step):
                copy.wait()
            collect(1 - slot)
            cols = pl.ds(pl.multiple_of(step * width, width), width)
            for b in range(blocks):
                hot = hot_rows(ids_ref[...], tgt_ref[pl.ds(step * blocks + b, 1), :])
                some = pl.ds(step * chunk + b * per_block, per_block)
                both = jnp.concatenate(
                    [
                        enc_ref[some].reshape(wide, block_grid),
                        dec_ref[some].reshape(wide, block_grid),
                    ],
                    axis=1,
                )
                sums = jnp.dot(hot, both, preferred_element_type=F32).astype(BF16)
                msum_ref[slot, :, b * block_grid : (b + 1) * block_grid] = sums[:, :block_grid]
                first = pl.multiple_of((step * blocks + b) * block_grid, block_grid)
                dsum_ref[:, pl.ds(first, block_grid)] = sums[:, block_grid:]
            for half in range(0, width, 256):
                part = pl.ds(pl.multiple_of(step * width + half, 256), 256)
                for top in range(0, latent, TALL):
                    lat = jnp.dot(
                        wt_ref[top : top + TALL, :channels], grid_ref[:, part],
                        preferred_element_type=F32,
                    )
                    lat = silu(lat).astype(BF16)
                    lat_ref[top : top + TALL, part] = lat
                    hold_ref[slot, top : top + TALL, half : half + 256] = lat

    collect(1)
    me = lax.axis_index("nodes")
    flipped = acc_ref[...].T.astype(BF16)
    for s in range(SLOTS):
        send_refs[s][:, :latent] = flipped[s * block_mesh : (s + 1) * block_mesh, :]
        block = slot_ref[scalar_partner(s, me, parts)].astype(F32)
        send_refs[s][:, latent:] = jnp.full((block_mesh, PAD), block, F32).astype(BF16)


def encode(parts, slot_block, owners, grid_t, w_embed, enc_coef, dec_t):
    channels, points = grid_t.shape
    latent = w_embed.shape[1]
    tiles, block_mesh, block_grid = enc_coef.shape
    grid_blocks = points // block_grid
    width = 512
    steps = points // width
    rows = SLOTS * block_mesh
    wide = tiles // grid_blocks * block_mesh
    vmem = pl.BlockSpec(memory_space=pltpu.VMEM)
    hbm = pl.BlockSpec(memory_space=pl.ANY)
    return pl.pallas_call(
        functools.partial(encode_kernel, parts, width),
        in_specs=[hbm] * 6,
        out_specs=[vmem] * (3 + SLOTS),
        out_shape=[
            pltpu.VMEM((latent, points), BF16),
            pltpu.VMEM((rows, points), BF16),
            pltpu.VMEM((channels, points), BF16),
        ]
        + [jax.ShapeDtypeStruct((block_mesh, latent + PAD), BF16)] * SLOTS,
        scratch_shapes=[
            pltpu.SMEM(slot_block.shape, jnp.int32),
            pltpu.VMEM(owners.shape, jnp.int32),
            pltpu.VMEM(w_embed.shape, BF16),
            pltpu.VMEM(enc_coef.shape, BF16),
            pltpu.VMEM(dec_t.shape, BF16),
            pltpu.VMEM((latent, 256), BF16),
            pltpu.VMEM((grid_blocks, wide), F32),
            pltpu.VMEM((rows, 128), BF16),
            pltpu.VMEM((2, rows, width), BF16),
            pltpu.VMEM((2, latent, width), BF16),
            pltpu.VMEM((latent, rows), F32),
            pltpu.SemaphoreType.DMA((3,)),
            pltpu.SemaphoreType.DMA((3, steps)),
        ],
        compiler_params=pltpu.CompilerParams(vmem_limit_bytes=24 * MIB),
        name="encode",
    )(
        *(
            pltpu.with_memory_space_constraint(x, pltpu.HBM)
            for x in (slot_block, owners, w_embed, grid_t, enc_coef, dec_t)
        )
    )


def prepare_kernel(parts, adj_ref, coef_ref, after_ref, near_ref):
    mesh_blocks, adj_width = adj_ref.shape
    block_mesh = coef_ref.shape[2]
    me = lax.axis_index("nodes")
    core = lax.rem(me, 2)
    columns = near_ref.shape[1]
    row = lax.broadcasted_iota(jnp.int32, (block_mesh, columns), 0)
    col = lax.broadcasted_iota(jnp.int32, (block_mesh, columns), 1)
    for b in range(mesh_blocks):
        total = jnp.zeros((block_mesh, columns), F32)
        for a in range(adj_width):
            which = adj_ref[b, a]
            listed = jnp.maximum(which, 0)
            side = lax.rem(lax.div(listed, mesh_blocks) - me + 1 + parts, parts)
            side = jnp.where(core == 0, 2 - side, side)
            place = side * mesh_blocks + lax.rem(listed, mesh_blocks)
            place = jnp.where(which >= 0, place, -columns)
            spot = jnp.where(col == place * block_mesh + row, 1.0, 0.0).astype(BF16)
            total += jnp.dot(coef_ref[b, a], spot, preferred_element_type=F32)
        near_ref[b * block_mesh : (b + 1) * block_mesh, :] = total.astype(BF16)


def prepare(parts, adj, coef, after):
    mesh_blocks, adj_width, block_mesh, _ = coef.shape
    count = mesh_blocks * block_mesh
    vmem = pl.BlockSpec(memory_space=pltpu.VMEM)
    return pl.pallas_call(
        functools.partial(prepare_kernel, parts),
        in_specs=[pl.BlockSpec(memory_space=pltpu.SMEM), vmem, vmem],
        out_specs=vmem,
        out_shape=jax.ShapeDtypeStruct((count, 3 * count), BF16),
        compiler_params=pltpu.CompilerParams(vmem_limit_bytes=8 * MIB),
        cost_estimate=pl.CostEstimate(
            flops=2 * adj_width * count * block_mesh * 3 * count,
            bytes_accessed=8 * count * 3 * count,
            transcendentals=0,
        ),
        name="prepare",
    )(adj, coef, after)


def update_kernel(*refs):
    slots = refs[:SLOTS]
    mesh_ref, w_ref, mid_ref, ids_ref = refs[SLOTS:]
    count, latent = mesh_ref.shape
    block_mesh = slots[0].shape[0]
    sums = [slot[:, :latent].astype(F32) for slot in slots]
    ids = [slot[:, latent:].astype(F32)[:1, :1] for slot in slots]
    for s in range(SLOTS):
        ids_ref[s : s + 1, :] = jnp.broadcast_to(ids[s], (1, latent))
    parts = []
    for b in range(count // block_mesh):
        total = jnp.zeros((block_mesh, latent), F32)
        for s in range(SLOTS):
            total += jnp.where(ids[s] == b, sums[s], 0.0)
        parts.append(total.astype(BF16))
    grown = jnp.dot(jnp.concatenate(parts, axis=0), w_ref[...], preferred_element_type=F32)
    mid_ref[...] = (mesh_ref[...].astype(F32) + silu(grown)).astype(BF16)


def update(slots, mesh_in, w_enc):
    vmem = pl.BlockSpec(memory_space=pltpu.VMEM)
    return pl.pallas_call(
        update_kernel,
        in_specs=[vmem] * (SLOTS + 2),
        out_specs=[vmem] * 2,
        out_shape=[
            jax.ShapeDtypeStruct(mesh_in.shape, BF16),
            jax.ShapeDtypeStruct((8, mesh_in.shape[1]), F32),
        ],
        compiler_params=pltpu.CompilerParams(vmem_limit_bytes=8 * MIB),
        name="mesh_update",
    )(*slots, mesh_in, w_enc)


def process_kernel(ids_ref, mid_ref, near_mid_ref, far_mid_ref, near_ref, gain_ref, w_ref, out_ref, *sends):
    count, latent = mid_ref.shape
    block_mesh = sends[0].shape[0]
    around = jnp.concatenate([near_mid_ref[...], mid_ref[...], far_mid_ref[...]], axis=0)
    message = jnp.dot(near_ref[...], around, preferred_element_type=F32)
    power = jnp.mean(message * message, axis=-1, keepdims=True)
    normed = (message * lax.rsqrt(power + 1e-05) * gain_ref[...]).astype(BF16)
    grown = jnp.dot(normed, w_ref[...], preferred_element_type=F32)
    grown = mid_ref[...].astype(F32) + silu(grown)
    out_ref[...] = grown.astype(BF16)
    for s in range(SLOTS):
        chosen = grown[:block_mesh, :]
        for b in range(1, count // block_mesh):
            block = grown[b * block_mesh : (b + 1) * block_mesh, :]
            chosen = jnp.where(ids_ref[s : s + 1, :] == b, block, chosen)
        sends[s][...] = chosen.astype(BF16)


def process(block_mesh, ids, mid, near_mid, far_mid, near, gain, w_proc):
    vmem = pl.BlockSpec(memory_space=pltpu.VMEM)
    latent = mid.shape[1]
    return pl.pallas_call(
        process_kernel,
        in_specs=[vmem] * 7,
        out_specs=[vmem] * (1 + SLOTS),
        out_shape=[jax.ShapeDtypeStruct(mid.shape, BF16)]
        + [jax.ShapeDtypeStruct((block_mesh, latent), BF16)] * SLOTS,
        compiler_params=pltpu.CompilerParams(vmem_limit_bytes=8 * MIB),
        name="mesh_process",
    )(ids, mid, near_mid, far_mid, near, gain, w_proc)


def decode_kernel(width, grid_ref, lat_ref, dsum_ref, w_ref, *rest):
    slots = rest[:SLOTS]
    out_hbm, back_ref, pred_ref, hold_ref, sems = rest[SLOTS:]
    steps = grid_ref.shape[1] // width
    channels = grid_ref.shape[0]
    latent = lat_ref.shape[0]

    def copy_out(step):
        cols = pl.ds(pl.multiple_of(step * width, width), width)
        return pltpu.make_async_copy(pred_ref.at[:, cols], out_hbm.at[:, cols], sems.at[step])

    joined = jnp.concatenate([slot[...] for slot in slots], axis=0)
    back_ref[...] = joined.astype(F32).T.astype(BF16)

    hold_ref[1] = jnp.zeros(hold_ref.shape[1:], BF16)

    def predict(step, slot):
        for half in range(0, width, 256):
            part = pl.ds(pl.multiple_of(step * width + half, 256), 256)
            for top in range(0, channels, TALL):
                rows = slice(top, min(top + TALL, channels))
                pred = jnp.dot(
                    w_ref[rows, :], hold_ref[slot, :, half : half + 256],
                    preferred_element_type=F32,
                )
                pred_ref[rows, part] = (grid_ref[rows, part].astype(F32) + pred).astype(BF16)

    @pl.loop(0, steps // 2)
    def _(pair):
        for slot in range(2):
            step = 2 * pair + slot
            before = jnp.maximum(step - 1, 0)
            predict(before, 1 - slot)
            for half in range(0, width, 256):
                part = pl.ds(pl.multiple_of(step * width + half, 256), 256)
                for top in range(0, latent, TALL):
                    rows = slice(top, top + TALL)
                    decoded = jnp.dot(
                        back_ref[rows, :], dsum_ref[:, part], preferred_element_type=F32
                    )
                    hidden = silu(lat_ref[rows, part].astype(F32) + decoded)
                    hold_ref[slot, rows, half : half + 256] = hidden.astype(BF16)

            @pl.when(step > 0)
            def _():
                copy_out(before).start()

    predict(steps - 1, 1)
    copy_out(steps - 1).start()
    for step in range(steps):
        copy_out(step).wait()


def decode(grid_t, lat_t, dsum, w_out_t, slots):
    channels, points = grid_t.shape
    latent = lat_t.shape[0]
    rows = dsum.shape[0]
    width = 512
    vmem = pl.BlockSpec(memory_space=pltpu.VMEM)
    return pl.pallas_call(
        functools.partial(decode_kernel, width),
        in_specs=[vmem] * (4 + SLOTS),
        out_specs=pl.BlockSpec(memory_space=pl.ANY),
        out_shape=jax.ShapeDtypeStruct((channels, points), BF16),
        scratch_shapes=[
            pltpu.VMEM((latent, rows), BF16),
            pltpu.VMEM((channels, points), BF16),
            pltpu.VMEM((2, latent, width), BF16),
            pltpu.SemaphoreType.DMA((points // width,)),
        ],
        compiler_params=pltpu.CompilerParams(vmem_limit_bytes=24 * MIB),
        name="decode",
    )(grid_t, lat_t, dsum, w_out_t, *slots)


def local(
    grid_in, w_embed, enc_coef, enc_owner, slot_block, mesh_in, w_enc,
    proc_adj, proc_coef, proc_gain, w_proc, dec_coef, w_out,
):
    parts = lax.axis_size("nodes")
    block_mesh = enc_coef.shape[1]

    def swap(x, slot):
        pairs = [(i, partner(slot, i, parts)) for i in range(parts)]
        return lax.ppermute(x, "nodes", pairs)

    def swap_all(xs):
        return [xs[OWN]] + [swap(xs[s], s) for s in range(1, SLOTS)]

    lat_t, dsum, grid_t, *sums = encode(
        parts, slot_block, enc_owner.reshape(-1, 128), grid_in.T, w_embed, enc_coef,
        jnp.swapaxes(dec_coef, 1, 2),
    )
    received = swap_all(sums)
    near = prepare(parts, proc_adj, proc_coef, sums[OWN])
    mid, ids = update(received, mesh_in, w_enc)
    far_mid = swap(mid, FAR)
    near_mid = swap(mid, NEAR)
    mesh_out, *sends = process(
        block_mesh, ids, mid, near_mid, far_mid, near, proc_gain.reshape(1, -1), w_proc
    )
    returned = swap_all(sends)
    pred_t = decode(grid_t, lat_t, dsum, w_out.T, returned)
    return (pred_t.T, mesh_out)


def solution(mesh):
    return jax.shard_map(
        local,
        mesh=mesh,
        in_specs=(
            P(("groups", "nodes"), None),
            P(),
            P("nodes", None, None),
            P("nodes"),
            P("nodes"),
            P(("groups", "nodes"), None),
            P(),
            P("nodes", None),
            P("nodes", None, None, None),
            P(),
            P(),
            P("nodes", None, None),
            P(),
        ),
        out_specs=(P(("groups", "nodes"), None), P(("groups", "nodes"), None)),
        check_vma=False,
    )
```

```python
import functools

import jax
import jax.numpy as jnp
from jax import lax
from jax.experimental import pallas as pl
from jax.experimental.pallas import tpu as pltpu
from jax.sharding import PartitionSpec as P

F32 = jnp.float32
BF16 = jnp.bfloat16
MIB = 1 << 20
OWN, HALF, ODD, FAR, EVEN, NEAR = range(6)
SLOTS = 6
PAD = 128
AHEAD = 3


def partner(slot, me, parts):
    chip = me // 2 % 2
    core = me % 2
    step = {
        OWN: 0,
        HALF: parts // 2,
        ODD: 4 * chip - 2,
        EVEN: 2 - 4 * chip,
        FAR: 2 * core - 1,
        NEAR: 1 - 2 * core,
    }[slot]
    return (me + step + parts) % parts


def scalar_partner(slot, me, parts):
    chip = lax.rem(lax.div(me, 2), 2)
    core = lax.rem(me, 2)
    step = {
        OWN: 0,
        HALF: parts // 2,
        ODD: 4 * chip - 2,
        EVEN: 2 - 4 * chip,
        FAR: 2 * core - 1,
        NEAR: 1 - 2 * core,
    }[slot]
    return lax.rem(me + step + parts, parts)


def silu(x):
    return x * pl.reciprocal(1.0 + jnp.exp(-x), approx=True)


def hot_rows(ids, target):
    lanes = ids.shape[1]
    target = target.astype(BF16)
    one, zero = jnp.ones((), BF16), jnp.zeros((), BF16)
    return jnp.concatenate(
        [
            jnp.where(ids == target[:, at : at + lanes], one, zero)
            for at in range(0, target.shape[1], lanes)
        ],
        axis=1,
    )


def fill_targets(parts, per_block, block_mesh, owner_ref, tgt_ref):
    wide = tgt_ref.shape[1]
    me = lax.axis_index("nodes")
    chip = lax.rem(lax.div(me, 2), 2)
    core = lax.rem(me, 2)
    up2 = EVEN + (ODD - EVEN) * chip
    up1 = NEAR + (FAR - NEAR) * core
    off = owner_ref[...] - me
    off = jnp.where(off < 0, off + parts, off)
    slot = jnp.where(off == parts // 2, HALF, OWN)
    slot = jnp.where(off == 2, up2, slot)
    slot = jnp.where(off == parts - 2, ODD + EVEN - up2, slot)
    slot = jnp.where(off == 1, up1, slot)
    slot = jnp.where(off == parts - 1, NEAR + FAR - up1, slot)
    slot = slot.astype(F32)
    groups, lanes = owner_ref.shape
    all_blocks = tgt_ref.shape[0]
    total = jnp.zeros(tgt_ref.shape, F32)
    for r in range(groups):
        tile = lax.broadcasted_iota(jnp.int32, (all_blocks, lanes), 1) + r * lanes
        first = lax.broadcasted_iota(jnp.int32, (all_blocks, lanes), 0) * per_block
        mine = (tile >= first) & (tile < first + per_block)
        picked = jnp.where(mine, slot[r : r + 1, :], 0.0).astype(BF16)
        row = lax.broadcasted_iota(jnp.int32, (lanes, wide), 0) + r * lanes
        col = lax.broadcasted_iota(jnp.int32, (lanes, wide), 1)
        place = row - per_block * ((row * (2**19 // per_block + 1)) >> 19)
        spread = jnp.where(place == col // block_mesh, 1.0, 0.0).astype(BF16)
        total += jnp.dot(picked, spread, preferred_element_type=F32)
    col = lax.broadcasted_iota(jnp.int32, tgt_ref.shape, 1)
    tgt_ref[...] = total * block_mesh + (col % block_mesh).astype(F32)


def encode_kernel(
    parts, width, slot_hbm, owner_hbm, w_hbm, grid_hbm, enc_hbm, dec_hbm,
    lat_ref, dsum_ref, grid_ref, *rest,
):
    send_refs = rest[:SLOTS]
    (
        slot_ref, owner_ref, w_ref, enc_ref, dec_ref, wt_ref, tgt_ref, ids_ref, msum_ref,
        hold_ref, acc_ref, small_sems, sems,
    ) = rest[SLOTS:]
    tiles, block_mesh, block_grid = enc_ref.shape
    channels, points = grid_ref.shape
    latent = w_ref.shape[1]
    per_block = tiles * block_grid // points
    blocks = width // block_grid
    chunk = blocks * per_block
    steps = points // width
    wide = per_block * block_mesh
    rows = SLOTS * block_mesh

    def copies(step):
        cols = pl.ds(pl.multiple_of(step * width, width), width)
        some = pl.ds(step * chunk, chunk)
        return (
            pltpu.make_async_copy(grid_hbm.at[:, cols], grid_ref.at[:, cols], sems.at[0, step]),
            pltpu.make_async_copy(enc_hbm.at[some], enc_ref.at[some], sems.at[1, step]),
            pltpu.make_async_copy(dec_hbm.at[some], dec_ref.at[some], sems.at[2, step]),
        )

    small = [
        pltpu.make_async_copy(source, target, small_sems.at[i])
        for i, (source, target) in enumerate(
            ((owner_hbm, owner_ref), (w_hbm, w_ref), (slot_hbm, slot_ref))
        )
    ]
    for copy in small:
        copy.start()
    def start(step):
        for copy in copies(step):
            copy.start()

    for step in range(AHEAD):
        start(step)
    ids_ref[...] = lax.broadcasted_iota(jnp.int32, ids_ref.shape, 0).astype(BF16)
    acc_ref[...] = jnp.zeros_like(acc_ref)
    msum_ref[1] = jnp.zeros(msum_ref.shape[1:], BF16)
    hold_ref[1] = jnp.zeros(hold_ref.shape[1:], BF16)
    for copy in small:
        copy.wait()
    wt_ref[:, :channels] = w_ref[...].astype(F32).T.astype(BF16)
    fill_targets(parts, per_block, block_mesh, owner_ref, tgt_ref)

    def collect(slot):
        acc_ref[...] += lax.dot_general(
            hold_ref[slot], msum_ref[slot], (((1,), (1,)), ((), ())), preferred_element_type=F32
        )

    @pl.loop(0, steps // 2)
    def _(pair):
        for slot in range(2):
            step = 2 * pair + slot

            @pl.when(step + AHEAD < steps)
            def _():
                start(step + AHEAD)

            for copy in copies(step):
                copy.wait()
            collect(1 - slot)
            cols = pl.ds(pl.multiple_of(step * width, width), width)
            for b in range(blocks):
                hot = hot_rows(ids_ref[...], tgt_ref[pl.ds(step * blocks + b, 1), :])
                some = pl.ds(step * chunk + b * per_block, per_block)
                both = jnp.concatenate(
                    [
                        enc_ref[some].reshape(wide, block_grid),
                        dec_ref[some].reshape(wide, block_grid),
                    ],
                    axis=1,
                )
                sums = jnp.dot(hot, both, preferred_element_type=F32).astype(BF16)
                msum_ref[slot, :, b * block_grid : (b + 1) * block_grid] = sums[:, :block_grid]
                first = pl.multiple_of((step * blocks + b) * block_grid, block_grid)
                dsum_ref[:, pl.ds(first, block_grid)] = sums[:, block_grid:]
            for half in range(0, width, 256):
                part = pl.ds(pl.multiple_of(step * width + half, 256), 256)
                lat = silu(
                    jnp.dot(
                        wt_ref[:, :channels], grid_ref[:, part], preferred_element_type=F32
                    )
                ).astype(BF16)
                lat_ref[:, part] = lat
                hold_ref[slot, :, half : half + 256] = lat

    collect(1)
    me = lax.axis_index("nodes")
    flipped = acc_ref[...].T.astype(BF16)
    for s in range(SLOTS):
        send_refs[s][:, :latent] = flipped[s * block_mesh : (s + 1) * block_mesh, :]
        block = slot_ref[scalar_partner(s, me, parts)].astype(F32)
        send_refs[s][:, latent:] = jnp.full((block_mesh, PAD), block, F32).astype(BF16)


def encode(parts, slot_block, owners, grid_t, w_embed, enc_coef, dec_t):
    channels, points = grid_t.shape
    latent = w_embed.shape[1]
    tiles, block_mesh, block_grid = enc_coef.shape
    grid_blocks = points // block_grid
    width = 512
    steps = points // width
    rows = SLOTS * block_mesh
    wide = tiles // grid_blocks * block_mesh
    vmem = pl.BlockSpec(memory_space=pltpu.VMEM)
    hbm = pl.BlockSpec(memory_space=pl.ANY)
    return pl.pallas_call(
        functools.partial(encode_kernel, parts, width),
        in_specs=[hbm] * 6,
        out_specs=[vmem] * (3 + SLOTS),
        out_shape=[
            pltpu.VMEM((latent, points), BF16),
            pltpu.VMEM((rows, points), BF16),
            pltpu.VMEM((channels, points), BF16),
        ]
        + [jax.ShapeDtypeStruct((block_mesh, latent + PAD), BF16)] * SLOTS,
        scratch_shapes=[
            pltpu.SMEM(slot_block.shape, jnp.int32),
            pltpu.VMEM(owners.shape, jnp.int32),
            pltpu.VMEM(w_embed.shape, BF16),
            pltpu.VMEM(enc_coef.shape, BF16),
            pltpu.VMEM(dec_t.shape, BF16),
            pltpu.VMEM((latent, 256), BF16),
            pltpu.VMEM((grid_blocks, wide), F32),
            pltpu.VMEM((rows, 128), BF16),
            pltpu.VMEM((2, rows, width), BF16),
            pltpu.VMEM((2, latent, width), BF16),
            pltpu.VMEM((latent, rows), F32),
            pltpu.SemaphoreType.DMA((3,)),
            pltpu.SemaphoreType.DMA((3, steps)),
        ],
        compiler_params=pltpu.CompilerParams(vmem_limit_bytes=24 * MIB),
        name="encode",
    )(
        *(
            pltpu.with_memory_space_constraint(x, pltpu.HBM)
            for x in (slot_block, owners, w_embed, grid_t, enc_coef, dec_t)
        )
    )


def prepare_kernel(parts, adj_ref, coef_ref, after_ref, near_ref):
    mesh_blocks, adj_width = adj_ref.shape
    block_mesh = coef_ref.shape[2]
    me = lax.axis_index("nodes")
    core = lax.rem(me, 2)
    columns = near_ref.shape[1]
    row = lax.broadcasted_iota(jnp.int32, (block_mesh, columns), 0)
    col = lax.broadcasted_iota(jnp.int32, (block_mesh, columns), 1)
    for b in range(mesh_blocks):
        total = jnp.zeros((block_mesh, columns), F32)
        for a in range(adj_width):
            which = adj_ref[b, a]
            listed = jnp.maximum(which, 0)
            side = lax.rem(lax.div(listed, mesh_blocks) - me + 1 + parts, parts)
            side = jnp.where(core == 0, 2 - side, side)
            place = side * mesh_blocks + lax.rem(listed, mesh_blocks)
            place = jnp.where(which >= 0, place, -columns)
            spot = jnp.where(col == place * block_mesh + row, 1.0, 0.0).astype(BF16)
            total += jnp.dot(coef_ref[b, a], spot, preferred_element_type=F32)
        near_ref[b * block_mesh : (b + 1) * block_mesh, :] = total.astype(BF16)


def prepare(parts, adj, coef, after):
    mesh_blocks, adj_width, block_mesh, _ = coef.shape
    count = mesh_blocks * block_mesh
    vmem = pl.BlockSpec(memory_space=pltpu.VMEM)
    return pl.pallas_call(
        functools.partial(prepare_kernel, parts),
        in_specs=[pl.BlockSpec(memory_space=pltpu.SMEM), vmem, vmem],
        out_specs=vmem,
        out_shape=jax.ShapeDtypeStruct((count, 3 * count), BF16),
        compiler_params=pltpu.CompilerParams(vmem_limit_bytes=8 * MIB),
        cost_estimate=pl.CostEstimate(
            flops=2 * adj_width * count * block_mesh * 3 * count,
            bytes_accessed=8 * count * 3 * count,
            transcendentals=0,
        ),
        name="prepare",
    )(adj, coef, after)


def update_kernel(*refs):
    slots = refs[:SLOTS]
    mesh_ref, w_ref, mid_ref, ids_ref = refs[SLOTS:]
    count, latent = mesh_ref.shape
    block_mesh = slots[0].shape[0]
    sums = [slot[:, :latent].astype(F32) for slot in slots]
    ids = [slot[:, latent:].astype(F32)[:1, :1] for slot in slots]
    for s in range(SLOTS):
        ids_ref[s : s + 1, :] = jnp.broadcast_to(ids[s], (1, latent))
    parts = []
    for b in range(count // block_mesh):
        total = jnp.zeros((block_mesh, latent), F32)
        for s in range(SLOTS):
            total += jnp.where(ids[s] == b, sums[s], 0.0)
        parts.append(total.astype(BF16))
    grown = jnp.dot(jnp.concatenate(parts, axis=0), w_ref[...], preferred_element_type=F32)
    mid_ref[...] = (mesh_ref[...].astype(F32) + silu(grown)).astype(BF16)


def update(slots, mesh_in, w_enc):
    vmem = pl.BlockSpec(memory_space=pltpu.VMEM)
    return pl.pallas_call(
        update_kernel,
        in_specs=[vmem] * (SLOTS + 2),
        out_specs=[vmem] * 2,
        out_shape=[
            jax.ShapeDtypeStruct(mesh_in.shape, BF16),
            jax.ShapeDtypeStruct((8, mesh_in.shape[1]), F32),
        ],
        compiler_params=pltpu.CompilerParams(vmem_limit_bytes=8 * MIB),
        name="mesh_update",
    )(*slots, mesh_in, w_enc)


def process_kernel(ids_ref, mid_ref, near_mid_ref, far_mid_ref, near_ref, gain_ref, w_ref, out_ref, *sends):
    count, latent = mid_ref.shape
    block_mesh = sends[0].shape[0]
    around = jnp.concatenate([near_mid_ref[...], mid_ref[...], far_mid_ref[...]], axis=0)
    message = jnp.dot(near_ref[...], around, preferred_element_type=F32)
    power = jnp.mean(message * message, axis=-1, keepdims=True)
    normed = (message * lax.rsqrt(power + 1e-05) * gain_ref[...]).astype(BF16)
    grown = jnp.dot(normed, w_ref[...], preferred_element_type=F32)
    grown = mid_ref[...].astype(F32) + silu(grown)
    out_ref[...] = grown.astype(BF16)
    for s in range(SLOTS):
        chosen = grown[:block_mesh, :]
        for b in range(1, count // block_mesh):
            block = grown[b * block_mesh : (b + 1) * block_mesh, :]
            chosen = jnp.where(ids_ref[s : s + 1, :] == b, block, chosen)
        sends[s][...] = chosen.astype(BF16)


def process(block_mesh, ids, mid, near_mid, far_mid, near, gain, w_proc):
    vmem = pl.BlockSpec(memory_space=pltpu.VMEM)
    latent = mid.shape[1]
    return pl.pallas_call(
        process_kernel,
        in_specs=[vmem] * 7,
        out_specs=[vmem] * (1 + SLOTS),
        out_shape=[jax.ShapeDtypeStruct(mid.shape, BF16)]
        + [jax.ShapeDtypeStruct((block_mesh, latent), BF16)] * SLOTS,
        compiler_params=pltpu.CompilerParams(vmem_limit_bytes=8 * MIB),
        name="mesh_process",
    )(ids, mid, near_mid, far_mid, near, gain, w_proc)


def decode_kernel(width, grid_ref, lat_ref, dsum_ref, w_ref, *rest):
    slots = rest[:SLOTS]
    out_hbm, back_ref, pred_ref, hold_ref, sems = rest[SLOTS:]
    steps = grid_ref.shape[1] // width

    def copy_out(step):
        cols = pl.ds(pl.multiple_of(step * width, width), width)
        return pltpu.make_async_copy(pred_ref.at[:, cols], out_hbm.at[:, cols], sems.at[step])

    joined = jnp.concatenate([slot[...] for slot in slots], axis=0)
    back_ref[...] = joined.astype(F32).T.astype(BF16)

    hold_ref[1] = jnp.zeros(hold_ref.shape[1:], BF16)

    def predict(step, slot):
        cols = pl.ds(pl.multiple_of(step * width, width), width)
        pred_ref[:, cols] = (
            grid_ref[:, cols].astype(F32)
            + jnp.dot(w_ref[...], hold_ref[slot], preferred_element_type=F32)
        ).astype(BF16)

    @pl.loop(0, steps // 2)
    def _(pair):
        for slot in range(2):
            step = 2 * pair + slot
            before = jnp.maximum(step - 1, 0)
            predict(before, 1 - slot)
            for half in range(0, width, 256):
                part = pl.ds(pl.multiple_of(step * width + half, 256), 256)
                decoded = jnp.dot(back_ref[...], dsum_ref[:, part], preferred_element_type=F32)
                hidden = silu(lat_ref[:, part].astype(F32) + decoded)
                hold_ref[slot, :, half : half + 256] = hidden.astype(BF16)

            @pl.when(step > 0)
            def _():
                copy_out(before).start()

    predict(steps - 1, 1)
    copy_out(steps - 1).start()
    for step in range(steps):
        copy_out(step).wait()


def decode(grid_t, lat_t, dsum, w_out_t, slots):
    channels, points = grid_t.shape
    latent = lat_t.shape[0]
    rows = dsum.shape[0]
    width = 512
    vmem = pl.BlockSpec(memory_space=pltpu.VMEM)
    return pl.pallas_call(
        functools.partial(decode_kernel, width),
        in_specs=[vmem] * (4 + SLOTS),
        out_specs=pl.BlockSpec(memory_space=pl.ANY),
        out_shape=jax.ShapeDtypeStruct((channels, points), BF16),
        scratch_shapes=[
            pltpu.VMEM((latent, rows), BF16),
            pltpu.VMEM((channels, points), BF16),
            pltpu.VMEM((2, latent, width), BF16),
            pltpu.SemaphoreType.DMA((points // width,)),
        ],
        compiler_params=pltpu.CompilerParams(vmem_limit_bytes=24 * MIB),
        name="decode",
    )(grid_t, lat_t, dsum, w_out_t, *slots)


def local(
    grid_in, w_embed, enc_coef, enc_owner, slot_block, mesh_in, w_enc,
    proc_adj, proc_coef, proc_gain, w_proc, dec_coef, w_out,
):
    parts = lax.axis_size("nodes")
    block_mesh = enc_coef.shape[1]

    def swap(x, slot):
        pairs = [(i, partner(slot, i, parts)) for i in range(parts)]
        return lax.ppermute(x, "nodes", pairs)

    def swap_all(xs):
        return [xs[OWN]] + [swap(xs[s], s) for s in range(1, SLOTS)]

    lat_t, dsum, grid_t, *sums = encode(
        parts, slot_block, enc_owner.reshape(-1, 128), grid_in.T, w_embed, enc_coef,
        jnp.swapaxes(dec_coef, 1, 2),
    )
    received = swap_all(sums)
    near = prepare(parts, proc_adj, proc_coef, sums[OWN])
    mid, ids = update(received, mesh_in, w_enc)
    far_mid = swap(mid, FAR)
    near_mid = swap(mid, NEAR)
    mesh_out, *sends = process(
        block_mesh, ids, mid, near_mid, far_mid, near, proc_gain.reshape(1, -1), w_proc
    )
    returned = swap_all(sends)
    pred_t = decode(grid_t, lat_t, dsum, w_out.T, returned)
    return (pred_t.T, mesh_out)


def solution(mesh):
    return jax.shard_map(
        local,
        mesh=mesh,
        in_specs=(
            P(("groups", "nodes"), None),
            P(),
            P("nodes", None, None),
            P("nodes"),
            P("nodes"),
            P(("groups", "nodes"), None),
            P(),
            P("nodes", None),
            P("nodes", None, None, None),
            P(),
            P(),
            P("nodes", None, None),
            P(),
        ),
        out_specs=(P(("groups", "nodes"), None), P(("groups", "nodes"), None)),
        check_vma=False,
    )
```

```python
import functools

import jax
import jax.numpy as jnp
from jax import lax
from jax.experimental import pallas as pl
from jax.experimental.pallas import tpu as pltpu
from jax.sharding import PartitionSpec as P

F32 = jnp.float32
BF16 = jnp.bfloat16
MIB = 1 << 20
OWN, HALF, ODD, FAR, EVEN, NEAR = range(6)
SLOTS = 6
PAD = 128
AHEAD = 3


def partner(slot, me, parts):
    chip = me // 2 % 2
    core = me % 2
    step = {
        OWN: 0,
        HALF: parts // 2,
        ODD: 4 * chip - 2,
        EVEN: 2 - 4 * chip,
        FAR: 2 * core - 1,
        NEAR: 1 - 2 * core,
    }[slot]
    return (me + step + parts) % parts


def scalar_partner(slot, me, parts):
    chip = lax.rem(lax.div(me, 2), 2)
    core = lax.rem(me, 2)
    step = {
        OWN: 0,
        HALF: parts // 2,
        ODD: 4 * chip - 2,
        EVEN: 2 - 4 * chip,
        FAR: 2 * core - 1,
        NEAR: 1 - 2 * core,
    }[slot]
    return lax.rem(me + step + parts, parts)


def silu(x):
    half = 0.5 * x
    return half + half * jnp.tanh(half)


def hot_rows(ids, target):
    lanes = ids.shape[1]
    target = target.astype(BF16)
    one, zero = jnp.ones((), BF16), jnp.zeros((), BF16)
    return jnp.concatenate(
        [
            jnp.where(ids == target[:, at : at + lanes], one, zero)
            for at in range(0, target.shape[1], lanes)
        ],
        axis=1,
    )


def fill_targets(parts, per_block, block_mesh, owner_ref, tgt_ref):
    wide = tgt_ref.shape[1]
    me = lax.axis_index("nodes")
    chip = lax.rem(lax.div(me, 2), 2)
    core = lax.rem(me, 2)
    up2 = EVEN + (ODD - EVEN) * chip
    up1 = NEAR + (FAR - NEAR) * core
    off = owner_ref[...] - me
    off = jnp.where(off < 0, off + parts, off)
    slot = jnp.where(off == parts // 2, HALF, OWN)
    slot = jnp.where(off == 2, up2, slot)
    slot = jnp.where(off == parts - 2, ODD + EVEN - up2, slot)
    slot = jnp.where(off == 1, up1, slot)
    slot = jnp.where(off == parts - 1, NEAR + FAR - up1, slot)
    slot = slot.astype(F32)
    groups, lanes = owner_ref.shape
    all_blocks = tgt_ref.shape[0]
    total = jnp.zeros(tgt_ref.shape, F32)
    for r in range(groups):
        tile = lax.broadcasted_iota(jnp.int32, (all_blocks, lanes), 1) + r * lanes
        first = lax.broadcasted_iota(jnp.int32, (all_blocks, lanes), 0) * per_block
        mine = (tile >= first) & (tile < first + per_block)
        picked = jnp.where(mine, slot[r : r + 1, :], 0.0).astype(BF16)
        row = lax.broadcasted_iota(jnp.int32, (lanes, wide), 0) + r * lanes
        col = lax.broadcasted_iota(jnp.int32, (lanes, wide), 1)
        place = row - per_block * ((row * (2**19 // per_block + 1)) >> 19)
        spread = jnp.where(place == col // block_mesh, 1.0, 0.0).astype(BF16)
        total += jnp.dot(picked, spread, preferred_element_type=F32)
    col = lax.broadcasted_iota(jnp.int32, tgt_ref.shape, 1)
    tgt_ref[...] = total * block_mesh + (col % block_mesh).astype(F32)


def encode_kernel(
    parts, width, slot_hbm, owner_hbm, w_hbm, grid_hbm, enc_hbm, dec_hbm,
    lat_ref, dsum_ref, grid_ref, *rest,
):
    send_refs = rest[:SLOTS]
    (
        slot_ref, owner_ref, w_ref, enc_ref, dec_ref, wt_ref, tgt_ref, ids_ref, msum_ref,
        hold_ref, acc_ref, small_sems, sems,
    ) = rest[SLOTS:]
    tiles, block_mesh, block_grid = enc_ref.shape
    channels, points = grid_ref.shape
    latent = w_ref.shape[1]
    per_block = tiles * block_grid // points
    blocks = width // block_grid
    chunk = blocks * per_block
    steps = points // width
    wide = per_block * block_mesh
    rows = SLOTS * block_mesh

    def copies(step):
        cols = pl.ds(step * width, width)
        some = pl.ds(step * chunk, chunk)
        return (
            pltpu.make_async_copy(grid_hbm.at[:, cols], grid_ref.at[:, cols], sems.at[0, step]),
            pltpu.make_async_copy(enc_hbm.at[some], enc_ref.at[some], sems.at[1, step]),
            pltpu.make_async_copy(dec_hbm.at[some], dec_ref.at[some], sems.at[2, step]),
        )

    small = [
        pltpu.make_async_copy(source, target, small_sems.at[i])
        for i, (source, target) in enumerate(
            ((owner_hbm, owner_ref), (w_hbm, w_ref), (slot_hbm, slot_ref))
        )
    ]
    for copy in small:
        copy.start()
    def start(step):
        for copy in copies(step):
            copy.start()

    for step in range(AHEAD):
        start(step)
    ids_ref[...] = lax.broadcasted_iota(jnp.int32, ids_ref.shape, 0).astype(BF16)
    acc_ref[...] = jnp.zeros_like(acc_ref)
    for copy in small:
        copy.wait()
    wt_ref[:, :channels] = w_ref[...].astype(F32).T.astype(BF16)
    fill_targets(parts, per_block, block_mesh, owner_ref, tgt_ref)

    def collect(slot):
        acc_ref[...] += lax.dot_general(
            hold_ref[slot], msum_ref[slot], (((1,), (1,)), ((), ())), preferred_element_type=F32
        )

    for step in range(steps):
        slot = step % 2
        if step + AHEAD < steps:
            start(step + AHEAD)
        for copy in copies(step):
            copy.wait()
        if step > 0:
            collect(1 - slot)
        for b in range(blocks):
            hot = hot_rows(ids_ref[...], tgt_ref[pl.ds(step * blocks + b, 1), :])
            some = pl.ds(step * chunk + b * per_block, per_block)
            both = jnp.concatenate(
                [
                    enc_ref[some].reshape(wide, block_grid),
                    dec_ref[some].reshape(wide, block_grid),
                ],
                axis=1,
            )
            sums = jnp.dot(hot, both, preferred_element_type=F32).astype(BF16)
            msum_ref[slot, :, b * block_grid : (b + 1) * block_grid] = sums[:, :block_grid]
            first = (step * blocks + b) * block_grid
            dsum_ref[:, pl.ds(first, block_grid)] = sums[:, block_grid:]
        for half in range(0, width, 256):
            part = pl.ds(step * width + half, 256)
            lat = silu(
                jnp.dot(
                    wt_ref[:, :channels], grid_ref[:, part], preferred_element_type=F32
                )
            ).astype(BF16)
            lat_ref[:, part] = lat
            hold_ref[slot, :, half : half + 256] = lat

    collect(1)
    me = lax.axis_index("nodes")
    flipped = acc_ref[...].T.astype(BF16)
    for s in range(SLOTS):
        send_refs[s][:, :latent] = flipped[s * block_mesh : (s + 1) * block_mesh, :]
        block = slot_ref[scalar_partner(s, me, parts)].astype(F32)
        send_refs[s][:, latent:] = jnp.full((block_mesh, PAD), block, F32).astype(BF16)


def encode(parts, slot_block, owners, grid_t, w_embed, enc_coef, dec_t):
    channels, points = grid_t.shape
    latent = w_embed.shape[1]
    tiles, block_mesh, block_grid = enc_coef.shape
    grid_blocks = points // block_grid
    width = 512
    steps = points // width
    rows = SLOTS * block_mesh
    wide = tiles // grid_blocks * block_mesh
    vmem = pl.BlockSpec(memory_space=pltpu.VMEM)
    hbm = pl.BlockSpec(memory_space=pl.ANY)
    return pl.pallas_call(
        functools.partial(encode_kernel, parts, width),
        in_specs=[hbm] * 6,
        out_specs=[vmem] * (3 + SLOTS),
        out_shape=[
            pltpu.VMEM((latent, points), BF16),
            pltpu.VMEM((rows, points), BF16),
            pltpu.VMEM((channels, points), BF16),
        ]
        + [jax.ShapeDtypeStruct((block_mesh, latent + PAD), BF16)] * SLOTS,
        scratch_shapes=[
            pltpu.SMEM(slot_block.shape, jnp.int32),
            pltpu.VMEM(owners.shape, jnp.int32),
            pltpu.VMEM(w_embed.shape, BF16),
            pltpu.VMEM(enc_coef.shape, BF16),
            pltpu.VMEM(dec_t.shape, BF16),
            pltpu.VMEM((latent, 256), BF16),
            pltpu.VMEM((grid_blocks, wide), F32),
            pltpu.VMEM((rows, 128), BF16),
            pltpu.VMEM((2, rows, width), BF16),
            pltpu.VMEM((2, latent, width), BF16),
            pltpu.VMEM((latent, rows), F32),
            pltpu.SemaphoreType.DMA((3,)),
            pltpu.SemaphoreType.DMA((3, steps)),
        ],
        compiler_params=pltpu.CompilerParams(vmem_limit_bytes=24 * MIB),
        name="encode",
    )(
        *(
            pltpu.with_memory_space_constraint(x, pltpu.HBM)
            for x in (slot_block, owners, w_embed, grid_t, enc_coef, dec_t)
        )
    )


def prepare_kernel(parts, adj_ref, coef_ref, after_ref, near_ref):
    mesh_blocks, adj_width = adj_ref.shape
    block_mesh = coef_ref.shape[2]
    me = lax.axis_index("nodes")
    core = lax.rem(me, 2)
    columns = near_ref.shape[1]
    row = lax.broadcasted_iota(jnp.int32, (block_mesh, columns), 0)
    col = lax.broadcasted_iota(jnp.int32, (block_mesh, columns), 1)
    for b in range(mesh_blocks):
        total = jnp.zeros((block_mesh, columns), F32)
        for a in range(adj_width):
            which = adj_ref[b, a]
            listed = jnp.maximum(which, 0)
            side = lax.rem(lax.div(listed, mesh_blocks) - me + 1 + parts, parts)
            side = jnp.where(core == 0, 2 - side, side)
            place = side * mesh_blocks + lax.rem(listed, mesh_blocks)
            place = jnp.where(which >= 0, place, -columns)
            spot = jnp.where(col == place * block_mesh + row, 1.0, 0.0).astype(BF16)
            total += jnp.dot(coef_ref[b, a], spot, preferred_element_type=F32)
        near_ref[b * block_mesh : (b + 1) * block_mesh, :] = total.astype(BF16)


def prepare(parts, adj, coef, after):
    mesh_blocks, adj_width, block_mesh, _ = coef.shape
    count = mesh_blocks * block_mesh
    vmem = pl.BlockSpec(memory_space=pltpu.VMEM)
    return pl.pallas_call(
        functools.partial(prepare_kernel, parts),
        in_specs=[pl.BlockSpec(memory_space=pltpu.SMEM), vmem, vmem],
        out_specs=vmem,
        out_shape=jax.ShapeDtypeStruct((count, 3 * count), BF16),
        compiler_params=pltpu.CompilerParams(vmem_limit_bytes=8 * MIB),
        cost_estimate=pl.CostEstimate(
            flops=2 * adj_width * count * block_mesh * 3 * count,
            bytes_accessed=8 * count * 3 * count,
            transcendentals=0,
        ),
        name="prepare",
    )(adj, coef, after)


def update_kernel(*refs):
    slots = refs[:SLOTS]
    mesh_ref, w_ref, mid_ref, ids_ref = refs[SLOTS:]
    count, latent = mesh_ref.shape
    block_mesh = slots[0].shape[0]
    sums = [slot[:, :latent].astype(F32) for slot in slots]
    ids = [slot[:, latent:].astype(F32)[:1, :1] for slot in slots]
    for s in range(SLOTS):
        ids_ref[s : s + 1, :] = jnp.broadcast_to(ids[s], (1, latent))
    parts = []
    for b in range(count // block_mesh):
        total = jnp.zeros((block_mesh, latent), F32)
        for s in range(SLOTS):
            total += jnp.where(ids[s] == b, sums[s], 0.0)
        parts.append(total.astype(BF16))
    grown = jnp.dot(jnp.concatenate(parts, axis=0), w_ref[...], preferred_element_type=F32)
    mid_ref[...] = (mesh_ref[...].astype(F32) + silu(grown)).astype(BF16)


def update(slots, mesh_in, w_enc):
    vmem = pl.BlockSpec(memory_space=pltpu.VMEM)
    return pl.pallas_call(
        update_kernel,
        in_specs=[vmem] * (SLOTS + 2),
        out_specs=[vmem] * 2,
        out_shape=[
            jax.ShapeDtypeStruct(mesh_in.shape, BF16),
            jax.ShapeDtypeStruct((8, mesh_in.shape[1]), F32),
        ],
        compiler_params=pltpu.CompilerParams(vmem_limit_bytes=8 * MIB),
        name="mesh_update",
    )(*slots, mesh_in, w_enc)


def process_kernel(ids_ref, mid_ref, near_mid_ref, far_mid_ref, near_ref, gain_ref, w_ref, out_ref, *sends):
    count, latent = mid_ref.shape
    block_mesh = sends[0].shape[0]
    around = jnp.concatenate([near_mid_ref[...], mid_ref[...], far_mid_ref[...]], axis=0)
    message = jnp.dot(near_ref[...], around, preferred_element_type=F32)
    power = jnp.mean(message * message, axis=-1, keepdims=True)
    normed = (message * lax.rsqrt(power + 1e-05) * gain_ref[...]).astype(BF16)
    grown = jnp.dot(normed, w_ref[...], preferred_element_type=F32)
    grown = mid_ref[...].astype(F32) + silu(grown)
    out_ref[...] = grown.astype(BF16)
    for s in range(SLOTS):
        chosen = grown[:block_mesh, :]
        for b in range(1, count // block_mesh):
            block = grown[b * block_mesh : (b + 1) * block_mesh, :]
            chosen = jnp.where(ids_ref[s : s + 1, :] == b, block, chosen)
        sends[s][...] = chosen.astype(BF16)


def process(block_mesh, ids, mid, near_mid, far_mid, near, gain, w_proc):
    vmem = pl.BlockSpec(memory_space=pltpu.VMEM)
    latent = mid.shape[1]
    return pl.pallas_call(
        process_kernel,
        in_specs=[vmem] * 7,
        out_specs=[vmem] * (1 + SLOTS),
        out_shape=[jax.ShapeDtypeStruct(mid.shape, BF16)]
        + [jax.ShapeDtypeStruct((block_mesh, latent), BF16)] * SLOTS,
        compiler_params=pltpu.CompilerParams(vmem_limit_bytes=8 * MIB),
        name="mesh_process",
    )(ids, mid, near_mid, far_mid, near, gain, w_proc)


def decode_kernel(width, grid_ref, lat_ref, dsum_ref, w_ref, *rest):
    slots = rest[:SLOTS]
    out_hbm, back_ref, pred_ref, hold_ref, sems = rest[SLOTS:]
    steps = grid_ref.shape[1] // width

    def copy_out(step):
        cols = pl.ds(step * width, width)
        return pltpu.make_async_copy(pred_ref.at[:, cols], out_hbm.at[:, cols], sems.at[step])

    joined = jnp.concatenate([slot[...] for slot in slots], axis=0)
    back_ref[...] = joined.astype(F32).T.astype(BF16)

    def predict(step, slot):
        cols = pl.ds(step * width, width)
        pred_ref[:, cols] = (
            grid_ref[:, cols].astype(F32)
            + jnp.dot(w_ref[...], hold_ref[slot], preferred_element_type=F32)
        ).astype(BF16)

    for step in range(steps):
        slot = step % 2
        if step > 0:
            predict(step - 1, 1 - slot)
            copy_out(step - 1).start()
        for half in range(0, width, 256):
            part = pl.ds(step * width + half, 256)
            decoded = jnp.dot(back_ref[...], dsum_ref[:, part], preferred_element_type=F32)
            hidden = silu(lat_ref[:, part].astype(F32) + decoded)
            hold_ref[slot, :, half : half + 256] = hidden.astype(BF16)
    predict(steps - 1, (steps - 1) % 2)
    copy_out(steps - 1).start()
    for step in range(steps):
        copy_out(step).wait()


def decode(grid_t, lat_t, dsum, w_out_t, slots):
    channels, points = grid_t.shape
    latent = lat_t.shape[0]
    rows = dsum.shape[0]
    width = 512
    vmem = pl.BlockSpec(memory_space=pltpu.VMEM)
    return pl.pallas_call(
        functools.partial(decode_kernel, width),
        in_specs=[vmem] * (4 + SLOTS),
        out_specs=pl.BlockSpec(memory_space=pl.ANY),
        out_shape=jax.ShapeDtypeStruct((channels, points), BF16),
        scratch_shapes=[
            pltpu.VMEM((latent, rows), BF16),
            pltpu.VMEM((channels, points), BF16),
            pltpu.VMEM((2, latent, width), BF16),
            pltpu.SemaphoreType.DMA((points // width,)),
        ],
        compiler_params=pltpu.CompilerParams(vmem_limit_bytes=24 * MIB),
        name="decode",
    )(grid_t, lat_t, dsum, w_out_t, *slots)


def local(
    grid_in, w_embed, enc_coef, enc_owner, slot_block, mesh_in, w_enc,
    proc_adj, proc_coef, proc_gain, w_proc, dec_coef, w_out,
):
    parts = lax.axis_size("nodes")
    block_mesh = enc_coef.shape[1]

    def swap(x, slot):
        pairs = [(i, partner(slot, i, parts)) for i in range(parts)]
        return lax.ppermute(x, "nodes", pairs)

    def swap_all(xs):
        return [xs[OWN]] + [swap(xs[s], s) for s in range(1, SLOTS)]

    lat_t, dsum, grid_t, *sums = encode(
        parts, slot_block, enc_owner.reshape(-1, 128), grid_in.T, w_embed, enc_coef,
        jnp.swapaxes(dec_coef, 1, 2),
    )
    received = swap_all(sums)
    near = prepare(parts, proc_adj, proc_coef, sums[OWN])
    mid, ids = update(received, mesh_in, w_enc)
    far_mid = swap(mid, FAR)
    near_mid = swap(mid, NEAR)
    mesh_out, *sends = process(
        block_mesh, ids, mid, near_mid, far_mid, near, proc_gain.reshape(1, -1), w_proc
    )
    returned = swap_all(sends)
    pred_t = decode(grid_t, lat_t, dsum, w_out.T, returned)
    return (pred_t.T, mesh_out)


def solution(mesh):
    return jax.shard_map(
        local,
        mesh=mesh,
        in_specs=(
            P(("groups", "nodes"), None),
            P(),
            P("nodes", None, None),
            P("nodes"),
            P("nodes"),
            P(("groups", "nodes"), None),
            P(),
            P("nodes", None),
            P("nodes", None, None, None),
            P(),
            P(),
            P("nodes", None, None),
            P(),
        ),
        out_specs=(P(("groups", "nodes"), None), P(("groups", "nodes"), None)),
        check_vma=False,
    )
```

```python
import functools

import jax
import jax.numpy as jnp
from jax import lax
from jax.experimental import pallas as pl
from jax.experimental.pallas import tpu as pltpu
from jax.sharding import PartitionSpec as P

F32 = jnp.float32
BF16 = jnp.bfloat16
MIB = 1 << 20
OWN, HALF, ODD, FAR, EVEN, NEAR = range(6)
SLOTS = 6
PAD = 128
AHEAD = 3


def partner(slot, me, parts):
    chip = me // 2 % 2
    core = me % 2
    step = {
        OWN: 0,
        HALF: parts // 2,
        ODD: 4 * chip - 2,
        EVEN: 2 - 4 * chip,
        FAR: 2 * core - 1,
        NEAR: 1 - 2 * core,
    }[slot]
    return (me + step + parts) % parts


def scalar_partner(slot, me, parts):
    chip = lax.rem(lax.div(me, 2), 2)
    core = lax.rem(me, 2)
    step = {
        OWN: 0,
        HALF: parts // 2,
        ODD: 4 * chip - 2,
        EVEN: 2 - 4 * chip,
        FAR: 2 * core - 1,
        NEAR: 1 - 2 * core,
    }[slot]
    return lax.rem(me + step + parts, parts)


def silu(x):
    half = 0.5 * x
    return half + half * jnp.tanh(half)


def hot_rows(ids, target):
    lanes = ids.shape[1]
    target = target.astype(BF16)
    one, zero = jnp.ones((), BF16), jnp.zeros((), BF16)
    return jnp.concatenate(
        [
            jnp.where(ids == target[:, at : at + lanes], one, zero)
            for at in range(0, target.shape[1], lanes)
        ],
        axis=1,
    )


def fill_targets(parts, per_block, block_mesh, owner_ref, tgt_ref):
    wide = tgt_ref.shape[1]
    me = lax.axis_index("nodes")
    chip = lax.rem(lax.div(me, 2), 2)
    core = lax.rem(me, 2)
    up2 = EVEN + (ODD - EVEN) * chip
    up1 = NEAR + (FAR - NEAR) * core
    off = owner_ref[...] - me
    off = jnp.where(off < 0, off + parts, off)
    slot = jnp.where(off == parts // 2, HALF, OWN)
    slot = jnp.where(off == 2, up2, slot)
    slot = jnp.where(off == parts - 2, ODD + EVEN - up2, slot)
    slot = jnp.where(off == 1, up1, slot)
    slot = jnp.where(off == parts - 1, NEAR + FAR - up1, slot)
    slot = slot.astype(F32)
    groups, lanes = owner_ref.shape
    all_blocks = tgt_ref.shape[0]
    total = jnp.zeros(tgt_ref.shape, F32)
    for r in range(groups):
        tile = lax.broadcasted_iota(jnp.int32, (all_blocks, lanes), 1) + r * lanes
        first = lax.broadcasted_iota(jnp.int32, (all_blocks, lanes), 0) * per_block
        mine = (tile >= first) & (tile < first + per_block)
        picked = jnp.where(mine, slot[r : r + 1, :], 0.0).astype(BF16)
        row = lax.broadcasted_iota(jnp.int32, (lanes, wide), 0) + r * lanes
        col = lax.broadcasted_iota(jnp.int32, (lanes, wide), 1)
        place = row - per_block * ((row * (2**19 // per_block + 1)) >> 19)
        spread = jnp.where(place == col // block_mesh, 1.0, 0.0).astype(BF16)
        total += jnp.dot(picked, spread, preferred_element_type=F32)
    col = lax.broadcasted_iota(jnp.int32, tgt_ref.shape, 1)
    tgt_ref[...] = total * block_mesh + (col % block_mesh).astype(F32)


def encode_kernel(
    parts, width, slot_hbm, owner_hbm, w_hbm, grid_hbm, enc_hbm, dec_hbm,
    lat_ref, dsum_ref, grid_ref, *rest,
):
    send_refs = rest[:SLOTS]
    (
        slot_ref, owner_ref, w_ref, enc_ref, dec_ref, wt_ref, tgt_ref, ids_ref, msum_ref,
        hold_ref, acc_ref, small_sems, sems,
    ) = rest[SLOTS:]
    tiles, block_mesh, block_grid = enc_ref.shape
    channels, points = grid_ref.shape
    latent = w_ref.shape[1]
    per_block = tiles * block_grid // points
    blocks = width // block_grid
    chunk = blocks * per_block
    steps = points // width
    wide = per_block * block_mesh
    rows = SLOTS * block_mesh

    def copies(step):
        cols = pl.ds(step * width, width)
        some = pl.ds(step * chunk, chunk)
        return (
            pltpu.make_async_copy(grid_hbm.at[:, cols], grid_ref.at[:, cols], sems.at[0, step]),
            pltpu.make_async_copy(enc_hbm.at[some], enc_ref.at[some], sems.at[1, step]),
            pltpu.make_async_copy(dec_hbm.at[some], dec_ref.at[some], sems.at[2, step]),
        )

    small = [
        pltpu.make_async_copy(source, target, small_sems.at[i])
        for i, (source, target) in enumerate(
            ((owner_hbm, owner_ref), (w_hbm, w_ref), (slot_hbm, slot_ref))
        )
    ]
    for copy in small:
        copy.start()
    def start(step):
        for copy in copies(step):
            copy.start()

    for step in range(AHEAD):
        start(step)
    ids_ref[...] = lax.broadcasted_iota(jnp.int32, ids_ref.shape, 0).astype(BF16)
    acc_ref[...] = jnp.zeros_like(acc_ref)
    for copy in small:
        copy.wait()
    wt_ref[:, :channels] = w_ref[...].astype(F32).T.astype(BF16)
    fill_targets(parts, per_block, block_mesh, owner_ref, tgt_ref)

    def collect(slot):
        acc_ref[...] += lax.dot_general(
            hold_ref[slot], msum_ref[slot], (((1,), (1,)), ((), ())), preferred_element_type=F32
        )

    for step in range(steps):
        slot = step % 2
        if step + AHEAD < steps:
            start(step + AHEAD)
        for copy in copies(step):
            copy.wait()
        if step > 0:
            collect(1 - slot)
        for b in range(blocks):
            hot = hot_rows(ids_ref[...], tgt_ref[pl.ds(step * blocks + b, 1), :])
            some = pl.ds(step * chunk + b * per_block, per_block)
            both = jnp.concatenate(
                [
                    enc_ref[some].reshape(wide, block_grid),
                    dec_ref[some].reshape(wide, block_grid),
                ],
                axis=1,
            )
            sums = jnp.dot(hot, both, preferred_element_type=F32).astype(BF16)
            msum_ref[slot, :, b * block_grid : (b + 1) * block_grid] = sums[:, :block_grid]
            first = (step * blocks + b) * block_grid
            dsum_ref[:, pl.ds(first, block_grid)] = sums[:, block_grid:]
        for half in range(0, width, 256):
            part = pl.ds(step * width + half, 256)
            lat = silu(
                jnp.dot(
                    wt_ref[:, :channels], grid_ref[:, part], preferred_element_type=F32
                )
            ).astype(BF16)
            lat_ref[:, part] = lat
            hold_ref[slot, :, half : half + 256] = lat

    collect(1)
    me = lax.axis_index("nodes")
    flipped = acc_ref[...].T.astype(BF16)
    for s in range(SLOTS):
        send_refs[s][:, :latent] = flipped[s * block_mesh : (s + 1) * block_mesh, :]
        block = slot_ref[scalar_partner(s, me, parts)].astype(F32)
        send_refs[s][:, latent:] = jnp.full((block_mesh, PAD), block, F32).astype(BF16)


def encode(parts, slot_block, owners, grid_t, w_embed, enc_coef, dec_t):
    channels, points = grid_t.shape
    latent = w_embed.shape[1]
    tiles, block_mesh, block_grid = enc_coef.shape
    grid_blocks = points // block_grid
    width = 512
    steps = points // width
    rows = SLOTS * block_mesh
    wide = tiles // grid_blocks * block_mesh
    vmem = pl.BlockSpec(memory_space=pltpu.VMEM)
    hbm = pl.BlockSpec(memory_space=pl.ANY)
    return pl.pallas_call(
        functools.partial(encode_kernel, parts, width),
        in_specs=[hbm] * 6,
        out_specs=[vmem] * (3 + SLOTS),
        out_shape=[
            pltpu.VMEM((latent, points), BF16),
            pltpu.VMEM((rows, points), BF16),
            pltpu.VMEM((channels, points), BF16),
        ]
        + [jax.ShapeDtypeStruct((block_mesh, latent + PAD), BF16)] * SLOTS,
        scratch_shapes=[
            pltpu.SMEM(slot_block.shape, jnp.int32),
            pltpu.VMEM(owners.shape, jnp.int32),
            pltpu.VMEM(w_embed.shape, BF16),
            pltpu.VMEM(enc_coef.shape, BF16),
            pltpu.VMEM(dec_t.shape, BF16),
            pltpu.VMEM((latent, 256), BF16),
            pltpu.VMEM((grid_blocks, wide), F32),
            pltpu.VMEM((rows, 128), BF16),
            pltpu.VMEM((2, rows, width), BF16),
            pltpu.VMEM((2, latent, width), BF16),
            pltpu.VMEM((latent, rows), F32),
            pltpu.SemaphoreType.DMA((3,)),
            pltpu.SemaphoreType.DMA((3, steps)),
        ],
        compiler_params=pltpu.CompilerParams(vmem_limit_bytes=24 * MIB),
        name="encode",
    )(
        *(
            pltpu.with_memory_space_constraint(x, pltpu.HBM)
            for x in (slot_block, owners, w_embed, grid_t, enc_coef, dec_t)
        )
    )


def prepare_kernel(parts, adj_ref, coef_ref, after_ref, near_ref):
    mesh_blocks, adj_width = adj_ref.shape
    block_mesh = coef_ref.shape[2]
    me = lax.axis_index("nodes")
    core = lax.rem(me, 2)
    columns = near_ref.shape[1]
    row = lax.broadcasted_iota(jnp.int32, (block_mesh, columns), 0)
    col = lax.broadcasted_iota(jnp.int32, (block_mesh, columns), 1)
    for b in range(mesh_blocks):
        total = jnp.zeros((block_mesh, columns), F32)
        for a in range(adj_width):
            which = adj_ref[b, a]
            listed = jnp.maximum(which, 0)
            side = lax.rem(lax.div(listed, mesh_blocks) - me + 1 + parts, parts)
            side = jnp.where(core == 0, 2 - side, side)
            place = side * mesh_blocks + lax.rem(listed, mesh_blocks)
            place = jnp.where(which >= 0, place, -columns)
            spot = jnp.where(col == place * block_mesh + row, 1.0, 0.0).astype(BF16)
            total += jnp.dot(coef_ref[b, a], spot, preferred_element_type=F32)
        near_ref[b * block_mesh : (b + 1) * block_mesh, :] = total.astype(BF16)


def prepare(parts, adj, coef, after):
    mesh_blocks, adj_width, block_mesh, _ = coef.shape
    count = mesh_blocks * block_mesh
    vmem = pl.BlockSpec(memory_space=pltpu.VMEM)
    return pl.pallas_call(
        functools.partial(prepare_kernel, parts),
        in_specs=[pl.BlockSpec(memory_space=pltpu.SMEM), vmem, vmem],
        out_specs=vmem,
        out_shape=jax.ShapeDtypeStruct((count, 3 * count), BF16),
        compiler_params=pltpu.CompilerParams(vmem_limit_bytes=8 * MIB),
        cost_estimate=pl.CostEstimate(
            flops=2 * adj_width * count * block_mesh * 3 * count,
            bytes_accessed=8 * count * 3 * count,
            transcendentals=0,
        ),
        name="prepare",
    )(adj, coef, after)


def other_half(parts, ref):
    return ref[jnp.where(lax.axis_index("nodes") < parts // 2, 1, 0)]


def update_kernel(parts, *refs):
    slots = [other_half(parts, r) if s == HALF else r[...] for s, r in enumerate(refs[:SLOTS])]
    mesh_ref, w_ref, mid_ref, ids_ref = refs[SLOTS:]
    count, latent = mesh_ref.shape
    block_mesh = slots[0].shape[0]
    sums = [slot[:, :latent].astype(F32) for slot in slots]
    ids = [slot[:, latent:].astype(F32)[:1, :1] for slot in slots]
    for s in range(SLOTS):
        ids_ref[s : s + 1, :] = jnp.broadcast_to(ids[s], (1, latent))
    parts = []
    for b in range(count // block_mesh):
        total = jnp.zeros((block_mesh, latent), F32)
        for s in range(SLOTS):
            total += jnp.where(ids[s] == b, sums[s], 0.0)
        parts.append(total.astype(BF16))
    grown = jnp.dot(jnp.concatenate(parts, axis=0), w_ref[...], preferred_element_type=F32)
    mid_ref[...] = (mesh_ref[...].astype(F32) + silu(grown)).astype(BF16)


def update(parts, slots, mesh_in, w_enc):
    vmem = pl.BlockSpec(memory_space=pltpu.VMEM)
    return pl.pallas_call(
        functools.partial(update_kernel, parts),
        in_specs=[vmem] * (SLOTS + 2),
        out_specs=[vmem] * 2,
        out_shape=[
            jax.ShapeDtypeStruct(mesh_in.shape, BF16),
            jax.ShapeDtypeStruct((8, mesh_in.shape[1]), F32),
        ],
        compiler_params=pltpu.CompilerParams(vmem_limit_bytes=8 * MIB),
        name="mesh_update",
    )(*slots, mesh_in, w_enc)


def process_kernel(ids_ref, mid_ref, near_mid_ref, far_mid_ref, near_ref, gain_ref, w_ref, out_ref, *sends):
    count, latent = mid_ref.shape
    block_mesh = sends[0].shape[0]
    around = jnp.concatenate([near_mid_ref[...], mid_ref[...], far_mid_ref[...]], axis=0)
    message = jnp.dot(near_ref[...], around, preferred_element_type=F32)
    power = jnp.mean(message * message, axis=-1, keepdims=True)
    normed = (message * lax.rsqrt(power + 1e-05) * gain_ref[...]).astype(BF16)
    grown = jnp.dot(normed, w_ref[...], preferred_element_type=F32)
    grown = mid_ref[...].astype(F32) + silu(grown)
    out_ref[...] = grown.astype(BF16)
    for s in range(SLOTS):
        chosen = grown[:block_mesh, :]
        for b in range(1, count // block_mesh):
            block = grown[b * block_mesh : (b + 1) * block_mesh, :]
            chosen = jnp.where(ids_ref[s : s + 1, :] == b, block, chosen)
        sends[s][...] = chosen.astype(BF16)


def process(block_mesh, ids, mid, near_mid, far_mid, near, gain, w_proc):
    vmem = pl.BlockSpec(memory_space=pltpu.VMEM)
    latent = mid.shape[1]
    return pl.pallas_call(
        process_kernel,
        in_specs=[vmem] * 7,
        out_specs=[vmem] * (1 + SLOTS),
        out_shape=[jax.ShapeDtypeStruct(mid.shape, BF16)]
        + [jax.ShapeDtypeStruct((block_mesh, latent), BF16)] * SLOTS,
        compiler_params=pltpu.CompilerParams(vmem_limit_bytes=8 * MIB),
        name="mesh_process",
    )(ids, mid, near_mid, far_mid, near, gain, w_proc)


def decode_kernel(parts, width, grid_ref, lat_ref, dsum_ref, w_ref, *rest):
    slots = rest[:SLOTS]
    out_hbm, back_ref, pred_ref, hold_ref, sems = rest[SLOTS:]
    steps = grid_ref.shape[1] // width

    def copy_out(step):
        cols = pl.ds(step * width, width)
        return pltpu.make_async_copy(pred_ref.at[:, cols], out_hbm.at[:, cols], sems.at[step])

    joined = jnp.concatenate(
        [other_half(parts, r) if s == HALF else r[...] for s, r in enumerate(slots)], axis=0
    )
    back_ref[...] = joined.astype(F32).T.astype(BF16)

    def predict(step, slot):
        cols = pl.ds(step * width, width)
        pred_ref[:, cols] = (
            grid_ref[:, cols].astype(F32)
            + jnp.dot(w_ref[...], hold_ref[slot], preferred_element_type=F32)
        ).astype(BF16)

    for step in range(steps):
        slot = step % 2
        if step > 0:
            predict(step - 1, 1 - slot)
            copy_out(step - 1).start()
        for half in range(0, width, 256):
            part = pl.ds(step * width + half, 256)
            decoded = jnp.dot(back_ref[...], dsum_ref[:, part], preferred_element_type=F32)
            hidden = silu(lat_ref[:, part].astype(F32) + decoded)
            hold_ref[slot, :, half : half + 256] = hidden.astype(BF16)
    predict(steps - 1, (steps - 1) % 2)
    copy_out(steps - 1).start()
    for step in range(steps):
        copy_out(step).wait()


def decode(parts, grid_t, lat_t, dsum, w_out_t, slots):
    channels, points = grid_t.shape
    latent = lat_t.shape[0]
    rows = dsum.shape[0]
    width = 512
    vmem = pl.BlockSpec(memory_space=pltpu.VMEM)
    return pl.pallas_call(
        functools.partial(decode_kernel, parts, width),
        in_specs=[vmem] * (4 + SLOTS),
        out_specs=pl.BlockSpec(memory_space=pl.ANY),
        out_shape=jax.ShapeDtypeStruct((channels, points), BF16),
        scratch_shapes=[
            pltpu.VMEM((latent, rows), BF16),
            pltpu.VMEM((channels, points), BF16),
            pltpu.VMEM((2, latent, width), BF16),
            pltpu.SemaphoreType.DMA((points // width,)),
        ],
        compiler_params=pltpu.CompilerParams(vmem_limit_bytes=24 * MIB),
        name="decode",
    )(grid_t, lat_t, dsum, w_out_t, *slots)


def local(
    grid_in, w_embed, enc_coef, enc_owner, slot_block, mesh_in, w_enc,
    proc_adj, proc_coef, proc_gain, w_proc, dec_coef, w_out,
):
    parts = lax.axis_size("nodes")
    block_mesh = enc_coef.shape[1]

    def swap(x, slot):
        pairs = [(i, partner(slot, i, parts)) for i in range(parts)]
        return lax.ppermute(x, "nodes", pairs)

    def both_halves(x):
        pairs = [[i, i + parts // 2] for i in range(parts // 2)]
        return lax.all_gather(x, "nodes", axis=0, axis_index_groups=pairs)

    def swap_all(xs):
        far = both_halves(xs[HALF])
        return [xs[OWN], far] + [swap(xs[s], s) for s in range(2, SLOTS)]

    lat_t, dsum, grid_t, *sums = encode(
        parts, slot_block, enc_owner.reshape(-1, 128), grid_in.T, w_embed, enc_coef,
        jnp.swapaxes(dec_coef, 1, 2),
    )
    received = swap_all(sums)
    near = prepare(parts, proc_adj, proc_coef, sums[OWN])
    mid, ids = update(parts, received, mesh_in, w_enc)
    far_mid = swap(mid, FAR)
    near_mid = swap(mid, NEAR)
    mesh_out, *sends = process(
        block_mesh, ids, mid, near_mid, far_mid, near, proc_gain.reshape(1, -1), w_proc
    )
    returned = swap_all(sends)
    pred_t = decode(parts, grid_t, lat_t, dsum, w_out.T, returned)
    return (pred_t.T, mesh_out)


def solution(mesh):
    return jax.shard_map(
        local,
        mesh=mesh,
        in_specs=(
            P(("groups", "nodes"), None),
            P(),
            P("nodes", None, None),
            P("nodes"),
            P("nodes"),
            P(("groups", "nodes"), None),
            P(),
            P("nodes", None),
            P("nodes", None, None, None),
            P(),
            P(),
            P("nodes", None, None),
            P(),
        ),
        out_specs=(P(("groups", "nodes"), None), P(("groups", "nodes"), None)),
        check_vma=False,
    )
```

```python
import functools

import jax
import jax.numpy as jnp
from jax import lax
from jax.experimental import pallas as pl
from jax.experimental.pallas import tpu as pltpu
from jax.sharding import PartitionSpec as P

F32 = jnp.float32
BF16 = jnp.bfloat16
MIB = 1 << 20
OWN, HALF, ODD, FAR, EVEN, NEAR = range(6)
SLOTS = 6
PAD = 128
AHEAD = 3


def partner(slot, me, parts):
    chip = me // 2 % 2
    core = me % 2
    step = {
        OWN: 0,
        HALF: parts // 2,
        ODD: 4 * chip - 2,
        EVEN: 2 - 4 * chip,
        FAR: 2 * core - 1,
        NEAR: 1 - 2 * core,
    }[slot]
    return (me + step + parts) % parts


def scalar_partner(slot, me, parts):
    chip = lax.rem(lax.div(me, 2), 2)
    core = lax.rem(me, 2)
    step = {
        OWN: 0,
        HALF: parts // 2,
        ODD: 4 * chip - 2,
        EVEN: 2 - 4 * chip,
        FAR: 2 * core - 1,
        NEAR: 1 - 2 * core,
    }[slot]
    return lax.rem(me + step + parts, parts)


def silu_of_half(half):
    return half + half * jnp.tanh(half)


def silu(x):
    return silu_of_half(0.5 * x)


def hot_rows(ids, target):
    lanes = ids.shape[1]
    target = target.astype(BF16)
    one, zero = jnp.ones((), BF16), jnp.zeros((), BF16)
    return jnp.concatenate(
        [
            jnp.where(ids == target[:, at : at + lanes], one, zero)
            for at in range(0, target.shape[1], lanes)
        ],
        axis=1,
    )


def fill_targets(parts, per_block, block_mesh, owner_ref, tgt_ref):
    wide = tgt_ref.shape[1]
    me = lax.axis_index("nodes")
    chip = lax.rem(lax.div(me, 2), 2)
    core = lax.rem(me, 2)
    up2 = EVEN + (ODD - EVEN) * chip
    up1 = NEAR + (FAR - NEAR) * core
    off = owner_ref[...] - me
    off = jnp.where(off < 0, off + parts, off)
    slot = jnp.where(off == parts // 2, HALF, OWN)
    slot = jnp.where(off == 2, up2, slot)
    slot = jnp.where(off == parts - 2, ODD + EVEN - up2, slot)
    slot = jnp.where(off == 1, up1, slot)
    slot = jnp.where(off == parts - 1, NEAR + FAR - up1, slot)
    slot = slot.astype(F32)
    groups, lanes = owner_ref.shape
    all_blocks = tgt_ref.shape[0]
    total = jnp.zeros(tgt_ref.shape, F32)
    for r in range(groups):
        tile = lax.broadcasted_iota(jnp.int32, (all_blocks, lanes), 1) + r * lanes
        first = lax.broadcasted_iota(jnp.int32, (all_blocks, lanes), 0) * per_block
        mine = (tile >= first) & (tile < first + per_block)
        picked = jnp.where(mine, slot[r : r + 1, :], 0.0).astype(BF16)
        row = lax.broadcasted_iota(jnp.int32, (lanes, wide), 0) + r * lanes
        col = lax.broadcasted_iota(jnp.int32, (lanes, wide), 1)
        place = row - per_block * ((row * (2**19 // per_block + 1)) >> 19)
        spread = jnp.where(place == col // block_mesh, 1.0, 0.0).astype(BF16)
        total += jnp.dot(picked, spread, preferred_element_type=F32)
    col = lax.broadcasted_iota(jnp.int32, tgt_ref.shape, 1)
    tgt_ref[...] = total * block_mesh + (col % block_mesh).astype(F32)


def encode_kernel(
    parts, width, slot_hbm, owner_hbm, w_hbm, grid_hbm, enc_hbm, dec_hbm,
    lat_ref, dsum_ref, grid_ref, *rest,
):
    send_refs = rest[:SLOTS]
    (
        slot_ref, owner_ref, w_ref, enc_ref, dec_ref, wt_ref, tgt_ref, ids_ref, msum_ref,
        hold_ref, acc_ref, small_sems, sems,
    ) = rest[SLOTS:]
    tiles, block_mesh, block_grid = enc_ref.shape
    channels, points = grid_ref.shape
    latent = w_ref.shape[1]
    per_block = tiles * block_grid // points
    blocks = width // block_grid
    chunk = blocks * per_block
    steps = points // width
    wide = per_block * block_mesh
    rows = SLOTS * block_mesh

    def copies(step):
        cols = pl.ds(step * width, width)
        some = pl.ds(step * chunk, chunk)
        return (
            pltpu.make_async_copy(grid_hbm.at[:, cols], grid_ref.at[:, cols], sems.at[0, step]),
            pltpu.make_async_copy(enc_hbm.at[some], enc_ref.at[some], sems.at[1, step]),
            pltpu.make_async_copy(dec_hbm.at[some], dec_ref.at[some], sems.at[2, step]),
        )

    small = [
        pltpu.make_async_copy(source, target, small_sems.at[i])
        for i, (source, target) in enumerate(
            ((owner_hbm, owner_ref), (w_hbm, w_ref), (slot_hbm, slot_ref))
        )
    ]
    for copy in small:
        copy.start()
    def start(step):
        for copy in copies(step):
            copy.start()

    for step in range(AHEAD):
        start(step)
    ids_ref[...] = lax.broadcasted_iota(jnp.int32, ids_ref.shape, 0).astype(BF16)
    acc_ref[...] = jnp.zeros_like(acc_ref)
    for copy in small:
        copy.wait()
    wt_ref[:, :channels] = (0.5 * w_ref[...].astype(F32)).T.astype(BF16)
    fill_targets(parts, per_block, block_mesh, owner_ref, tgt_ref)

    def collect(slot):
        acc_ref[...] += lax.dot_general(
            hold_ref[slot], msum_ref[slot], (((1,), (1,)), ((), ())), preferred_element_type=F32
        )

    for step in range(steps):
        slot = step % 2
        if step + AHEAD < steps:
            start(step + AHEAD)
        for copy in copies(step):
            copy.wait()
        if step > 0:
            collect(1 - slot)
        for b in range(blocks):
            hot = hot_rows(ids_ref[...], tgt_ref[pl.ds(step * blocks + b, 1), :])
            some = pl.ds(step * chunk + b * per_block, per_block)
            both = jnp.concatenate(
                [
                    enc_ref[some].reshape(wide, block_grid),
                    dec_ref[some].reshape(wide, block_grid),
                ],
                axis=1,
            )
            sums = jnp.dot(hot, both, preferred_element_type=F32).astype(BF16)
            msum_ref[slot, :, b * block_grid : (b + 1) * block_grid] = sums[:, :block_grid]
            first = (step * blocks + b) * block_grid
            dsum_ref[:, pl.ds(first, block_grid)] = sums[:, block_grid:]
        for half in range(0, width, 256):
            part = pl.ds(step * width + half, 256)
            lat = silu_of_half(
                jnp.dot(
                    wt_ref[:, :channels], grid_ref[:, part], preferred_element_type=F32
                )
            ).astype(BF16)
            lat_ref[:, part] = lat
            hold_ref[slot, :, half : half + 256] = lat

    collect(1)
    me = lax.axis_index("nodes")
    flipped = acc_ref[...].T.astype(BF16)
    for s in range(SLOTS):
        send_refs[s][:, :latent] = flipped[s * block_mesh : (s + 1) * block_mesh, :]
        block = slot_ref[scalar_partner(s, me, parts)].astype(F32)
        send_refs[s][:, latent:] = jnp.full((block_mesh, PAD), block, F32).astype(BF16)


def encode(parts, slot_block, owners, grid_t, w_embed, enc_coef, dec_t):
    channels, points = grid_t.shape
    latent = w_embed.shape[1]
    tiles, block_mesh, block_grid = enc_coef.shape
    grid_blocks = points // block_grid
    width = 512
    steps = points // width
    rows = SLOTS * block_mesh
    wide = tiles // grid_blocks * block_mesh
    vmem = pl.BlockSpec(memory_space=pltpu.VMEM)
    hbm = pl.BlockSpec(memory_space=pl.ANY)
    return pl.pallas_call(
        functools.partial(encode_kernel, parts, width),
        in_specs=[hbm] * 6,
        out_specs=[vmem] * (3 + SLOTS),
        out_shape=[
            pltpu.VMEM((latent, points), BF16),
            pltpu.VMEM((rows, points), BF16),
            pltpu.VMEM((channels, points), BF16),
        ]
        + [jax.ShapeDtypeStruct((block_mesh, latent + PAD), BF16)] * SLOTS,
        scratch_shapes=[
            pltpu.SMEM(slot_block.shape, jnp.int32),
            pltpu.VMEM(owners.shape, jnp.int32),
            pltpu.VMEM(w_embed.shape, BF16),
            pltpu.VMEM(enc_coef.shape, BF16),
            pltpu.VMEM(dec_t.shape, BF16),
            pltpu.VMEM((latent, 256), BF16),
            pltpu.VMEM((grid_blocks, wide), F32),
            pltpu.VMEM((rows, 128), BF16),
            pltpu.VMEM((2, rows, width), BF16),
            pltpu.VMEM((2, latent, width), BF16),
            pltpu.VMEM((latent, rows), F32),
            pltpu.SemaphoreType.DMA((3,)),
            pltpu.SemaphoreType.DMA((3, steps)),
        ],
        compiler_params=pltpu.CompilerParams(vmem_limit_bytes=24 * MIB),
        name="encode",
    )(
        *(
            pltpu.with_memory_space_constraint(x, pltpu.HBM)
            for x in (slot_block, owners, w_embed, grid_t, enc_coef, dec_t)
        )
    )


def prepare_kernel(parts, adj_ref, coef_ref, after_ref, near_ref):
    mesh_blocks, adj_width = adj_ref.shape
    block_mesh = coef_ref.shape[2]
    me = lax.axis_index("nodes")
    core = lax.rem(me, 2)
    columns = near_ref.shape[1]
    row = lax.broadcasted_iota(jnp.int32, (block_mesh, columns), 0)
    col = lax.broadcasted_iota(jnp.int32, (block_mesh, columns), 1)
    for b in range(mesh_blocks):
        total = jnp.zeros((block_mesh, columns), F32)
        for a in range(adj_width):
            which = adj_ref[b, a]
            listed = jnp.maximum(which, 0)
            side = lax.rem(lax.div(listed, mesh_blocks) - me + 1 + parts, parts)
            side = jnp.where(core == 0, 2 - side, side)
            place = side * mesh_blocks + lax.rem(listed, mesh_blocks)
            place = jnp.where(which >= 0, place, -columns)
            spot = jnp.where(col == place * block_mesh + row, 1.0, 0.0).astype(BF16)
            total += jnp.dot(coef_ref[b, a], spot, preferred_element_type=F32)
        near_ref[b * block_mesh : (b + 1) * block_mesh, :] = total.astype(BF16)


def prepare(parts, adj, coef, after):
    mesh_blocks, adj_width, block_mesh, _ = coef.shape
    count = mesh_blocks * block_mesh
    vmem = pl.BlockSpec(memory_space=pltpu.VMEM)
    return pl.pallas_call(
        functools.partial(prepare_kernel, parts),
        in_specs=[pl.BlockSpec(memory_space=pltpu.SMEM), vmem, vmem],
        out_specs=vmem,
        out_shape=jax.ShapeDtypeStruct((count, 3 * count), BF16),
        compiler_params=pltpu.CompilerParams(vmem_limit_bytes=8 * MIB),
        cost_estimate=pl.CostEstimate(
            flops=2 * adj_width * count * block_mesh * 3 * count,
            bytes_accessed=8 * count * 3 * count,
            transcendentals=0,
        ),
        name="prepare",
    )(adj, coef, after)


def update_kernel(*refs):
    slots = refs[:SLOTS]
    mesh_ref, w_ref, mid_ref, ids_ref = refs[SLOTS:]
    count, latent = mesh_ref.shape
    block_mesh = slots[0].shape[0]
    sums = [slot[:, :latent].astype(F32) for slot in slots]
    ids = [slot[:, latent:].astype(F32)[:1, :1] for slot in slots]
    for s in range(SLOTS):
        ids_ref[s : s + 1, :] = jnp.broadcast_to(ids[s], (1, latent))
    parts = []
    for b in range(count // block_mesh):
        total = jnp.zeros((block_mesh, latent), F32)
        for s in range(SLOTS):
            total += jnp.where(ids[s] == b, sums[s], 0.0)
        parts.append(total.astype(BF16))
    grown = jnp.dot(jnp.concatenate(parts, axis=0), w_ref[...], preferred_element_type=F32)
    mid_ref[...] = (mesh_ref[...].astype(F32) + silu(grown)).astype(BF16)


def update(slots, mesh_in, w_enc):
    vmem = pl.BlockSpec(memory_space=pltpu.VMEM)
    return pl.pallas_call(
        update_kernel,
        in_specs=[vmem] * (SLOTS + 2),
        out_specs=[vmem] * 2,
        out_shape=[
            jax.ShapeDtypeStruct(mesh_in.shape, BF16),
            jax.ShapeDtypeStruct((8, mesh_in.shape[1]), F32),
        ],
        compiler_params=pltpu.CompilerParams(vmem_limit_bytes=8 * MIB),
        name="mesh_update",
    )(*slots, mesh_in, w_enc)


def process_kernel(ids_ref, mid_ref, near_mid_ref, far_mid_ref, near_ref, gain_ref, w_ref, out_ref, *sends):
    count, latent = mid_ref.shape
    block_mesh = sends[0].shape[0]
    around = jnp.concatenate([near_mid_ref[...], mid_ref[...], far_mid_ref[...]], axis=0)
    message = jnp.dot(near_ref[...], around, preferred_element_type=F32)
    power = jnp.mean(message * message, axis=-1, keepdims=True)
    normed = (message * lax.rsqrt(power + 1e-05) * gain_ref[...]).astype(BF16)
    grown = jnp.dot(normed, w_ref[...], preferred_element_type=F32)
    grown = mid_ref[...].astype(F32) + silu(grown)
    out_ref[...] = grown.astype(BF16)
    for s in range(SLOTS):
        chosen = grown[:block_mesh, :]
        for b in range(1, count // block_mesh):
            block = grown[b * block_mesh : (b + 1) * block_mesh, :]
            chosen = jnp.where(ids_ref[s : s + 1, :] == b, block, chosen)
        sends[s][...] = chosen.astype(BF16)


def process(block_mesh, ids, mid, near_mid, far_mid, near, gain, w_proc):
    vmem = pl.BlockSpec(memory_space=pltpu.VMEM)
    latent = mid.shape[1]
    return pl.pallas_call(
        process_kernel,
        in_specs=[vmem] * 7,
        out_specs=[vmem] * (1 + SLOTS),
        out_shape=[jax.ShapeDtypeStruct(mid.shape, BF16)]
        + [jax.ShapeDtypeStruct((block_mesh, latent), BF16)] * SLOTS,
        compiler_params=pltpu.CompilerParams(vmem_limit_bytes=8 * MIB),
        name="mesh_process",
    )(ids, mid, near_mid, far_mid, near, gain, w_proc)


def decode_kernel(width, grid_ref, lat_ref, dsum_ref, w_ref, *rest):
    slots = rest[:SLOTS]
    out_hbm, back_ref, pred_ref, hold_ref, sems = rest[SLOTS:]
    steps = grid_ref.shape[1] // width

    def copy_out(step):
        cols = pl.ds(step * width, width)
        return pltpu.make_async_copy(pred_ref.at[:, cols], out_hbm.at[:, cols], sems.at[step])

    joined = jnp.concatenate([slot[...] for slot in slots], axis=0)
    back_ref[...] = joined.T

    def predict(step, slot):
        cols = pl.ds(step * width, width)
        pred_ref[:, cols] = (
            grid_ref[:, cols].astype(F32)
            + jnp.dot(w_ref[...], hold_ref[slot], preferred_element_type=F32)
        ).astype(BF16)

    for step in range(steps):
        slot = step % 2
        if step > 0:
            predict(step - 1, 1 - slot)
            copy_out(step - 1).start()
        for half in range(0, width, 256):
            part = pl.ds(step * width + half, 256)
            decoded = jnp.dot(back_ref[...], dsum_ref[:, part], preferred_element_type=F32)
            hidden = silu(lat_ref[:, part].astype(F32) + decoded)
            hold_ref[slot, :, half : half + 256] = hidden.astype(BF16)
    predict(steps - 1, (steps - 1) % 2)
    copy_out(steps - 1).start()
    for step in range(steps):
        copy_out(step).wait()


def decode(grid_t, lat_t, dsum, w_out_t, slots):
    channels, points = grid_t.shape
    latent = lat_t.shape[0]
    rows = dsum.shape[0]
    width = 512
    vmem = pl.BlockSpec(memory_space=pltpu.VMEM)
    return pl.pallas_call(
        functools.partial(decode_kernel, width),
        in_specs=[vmem] * (4 + SLOTS),
        out_specs=pl.BlockSpec(memory_space=pl.ANY),
        out_shape=jax.ShapeDtypeStruct((channels, points), BF16),
        scratch_shapes=[
            pltpu.VMEM((latent, rows), BF16),
            pltpu.VMEM((channels, points), BF16),
            pltpu.VMEM((2, latent, width), BF16),
            pltpu.SemaphoreType.DMA((points // width,)),
        ],
        compiler_params=pltpu.CompilerParams(vmem_limit_bytes=24 * MIB),
        name="decode",
    )(grid_t, lat_t, dsum, w_out_t, *slots)


def local(
    grid_in, w_embed, enc_coef, enc_owner, slot_block, mesh_in, w_enc,
    proc_adj, proc_coef, proc_gain, w_proc, dec_coef, w_out,
):
    parts = lax.axis_size("nodes")
    block_mesh = enc_coef.shape[1]

    def swap(x, slot):
        pairs = [(i, partner(slot, i, parts)) for i in range(parts)]
        return lax.ppermute(x, "nodes", pairs)

    def swap_all(xs):
        out = {OWN: xs[OWN]}
        for s in (ODD, HALF, FAR, EVEN, NEAR):
            out[s] = swap(xs[s], s)
        return [out[s] for s in range(SLOTS)]

    lat_t, dsum, grid_t, *sums = encode(
        parts, slot_block, enc_owner.reshape(-1, 128), grid_in.T, w_embed, enc_coef,
        jnp.swapaxes(dec_coef, 1, 2),
    )
    received = swap_all(sums)
    near = prepare(parts, proc_adj, proc_coef, sums[OWN])
    mid, ids = update(received, mesh_in, w_enc)
    far_mid = swap(mid, FAR)
    near_mid = swap(mid, NEAR)
    mesh_out, *sends = process(
        block_mesh, ids, mid, near_mid, far_mid, near, proc_gain.reshape(1, -1), w_proc
    )
    returned = swap_all(sends)
    pred_t = decode(grid_t, lat_t, dsum, w_out.T, returned)
    return (pred_t.T, mesh_out)


def solution(mesh):
    return jax.shard_map(
        local,
        mesh=mesh,
        in_specs=(
            P(("groups", "nodes"), None),
            P(),
            P("nodes", None, None),
            P("nodes"),
            P("nodes"),
            P(("groups", "nodes"), None),
            P(),
            P("nodes", None),
            P("nodes", None, None, None),
            P(),
            P(),
            P("nodes", None, None),
            P(),
        ),
        out_specs=(P(("groups", "nodes"), None), P(("groups", "nodes"), None)),
        check_vma=False,
    )
```

```python
import functools

import jax
import jax.numpy as jnp
from jax import lax
from jax.experimental import pallas as pl
from jax.experimental.pallas import tpu as pltpu
from jax.sharding import PartitionSpec as P

F32 = jnp.float32
BF16 = jnp.bfloat16
MIB = 1 << 20
OWN, ODD, HALF, FAR, EVEN, NEAR = range(6)
SLOTS = 6
PAD = 128
AHEAD = 3


def partner(slot, me, parts):
    chip = me // 2 % 2
    core = me % 2
    step = {
        OWN: 0,
        HALF: parts // 2,
        ODD: 4 * chip - 2,
        EVEN: 2 - 4 * chip,
        FAR: 2 * core - 1,
        NEAR: 1 - 2 * core,
    }[slot]
    return (me + step + parts) % parts


def scalar_partner(slot, me, parts):
    chip = lax.rem(lax.div(me, 2), 2)
    core = lax.rem(me, 2)
    step = {
        OWN: 0,
        HALF: parts // 2,
        ODD: 4 * chip - 2,
        EVEN: 2 - 4 * chip,
        FAR: 2 * core - 1,
        NEAR: 1 - 2 * core,
    }[slot]
    return lax.rem(me + step + parts, parts)


def silu_of_half(half):
    return half + half * jnp.tanh(half)


def silu(x):
    return silu_of_half(0.5 * x)


def hot_rows(ids, target):
    lanes = ids.shape[1]
    target = target.astype(BF16)
    one, zero = jnp.ones((), BF16), jnp.zeros((), BF16)
    return jnp.concatenate(
        [
            jnp.where(ids == target[:, at : at + lanes], one, zero)
            for at in range(0, target.shape[1], lanes)
        ],
        axis=1,
    )


def spreads(per_block, block_mesh, groups, lanes, wide):
    out = []
    for r in range(groups):
        row = lax.broadcasted_iota(jnp.int32, (lanes, wide), 0) + r * lanes
        col = lax.broadcasted_iota(jnp.int32, (lanes, wide), 1)
        place = row - per_block * ((row * (2**19 // per_block + 1)) >> 19)
        out.append(jnp.where(place == col // block_mesh, 1.0, 0.0).astype(BF16))
    return out


def fill_targets(parts, per_block, block_mesh, spread_ref, owner_ref, tgt_ref):
    me = lax.axis_index("nodes")
    chip = lax.rem(lax.div(me, 2), 2)
    core = lax.rem(me, 2)
    up2 = EVEN + (ODD - EVEN) * chip
    up1 = NEAR + (FAR - NEAR) * core
    off = owner_ref[...] - me
    off = jnp.where(off < 0, off + parts, off)
    slot = jnp.where(off == parts // 2, HALF, OWN)
    slot = jnp.where(off == 2, up2, slot)
    slot = jnp.where(off == parts - 2, ODD + EVEN - up2, slot)
    slot = jnp.where(off == 1, up1, slot)
    slot = jnp.where(off == parts - 1, NEAR + FAR - up1, slot)
    slot = slot.astype(F32)
    groups, lanes = owner_ref.shape
    all_blocks = tgt_ref.shape[0]
    total = jnp.zeros(tgt_ref.shape, F32)
    for r in range(groups):
        tile = lax.broadcasted_iota(jnp.int32, (all_blocks, lanes), 1) + r * lanes
        first = lax.broadcasted_iota(jnp.int32, (all_blocks, lanes), 0) * per_block
        mine = (tile >= first) & (tile < first + per_block)
        picked = jnp.where(mine, slot[r : r + 1, :], 0.0).astype(BF16)
        total += jnp.dot(picked, spread_ref[r], preferred_element_type=F32)
    col = lax.broadcasted_iota(jnp.int32, tgt_ref.shape, 1)
    tgt_ref[...] = total * block_mesh + (col % block_mesh).astype(F32)


def encode_kernel(
    parts, width, slot_hbm, owner_hbm, w_hbm, grid_hbm, enc_hbm, dec_hbm,
    lat_ref, dsum_ref, grid_ref, *rest,
):
    send_refs = rest[:SLOTS]
    (
        slot_ref, owner_ref, w_ref, enc_ref, dec_ref, wt_ref, tgt_ref, ids_ref, msum_ref,
        hold_ref, acc_ref, spread_ref, small_sems, sems,
    ) = rest[SLOTS:]
    tiles, block_mesh, block_grid = enc_ref.shape
    channels, points = grid_ref.shape
    latent = w_ref.shape[1]
    per_block = tiles * block_grid // points
    blocks = width // block_grid
    chunk = blocks * per_block
    steps = points // width
    wide = per_block * block_mesh
    rows = SLOTS * block_mesh

    def copies(step):
        cols = pl.ds(step * width, width)
        some = pl.ds(step * chunk, chunk)
        return (
            pltpu.make_async_copy(grid_hbm.at[:, cols], grid_ref.at[:, cols], sems.at[0, step]),
            pltpu.make_async_copy(enc_hbm.at[some], enc_ref.at[some], sems.at[1, step]),
            pltpu.make_async_copy(dec_hbm.at[some], dec_ref.at[some], sems.at[2, step]),
        )

    small = [
        pltpu.make_async_copy(source, target, small_sems.at[i])
        for i, (source, target) in enumerate(
            ((owner_hbm, owner_ref), (w_hbm, w_ref), (slot_hbm, slot_ref))
        )
    ]
    for copy in small:
        copy.start()
    def start(step):
        for copy in copies(step):
            copy.start()

    start(0)
    ids_ref[...] = lax.broadcasted_iota(jnp.int32, ids_ref.shape, 0).astype(BF16)
    acc_ref[...] = jnp.zeros_like(acc_ref)
    for r, spread in enumerate(spreads(per_block, block_mesh, *owner_ref.shape, wide)):
        spread_ref[r] = spread
    for copy in small:
        copy.wait()
    for step in range(1, AHEAD):
        start(step)
    wt_ref[:, :channels] = (0.5 * w_ref[...].astype(F32)).T.astype(BF16)
    fill_targets(parts, per_block, block_mesh, spread_ref, owner_ref, tgt_ref)

    def collect(slot):
        acc_ref[...] += lax.dot_general(
            hold_ref[slot], msum_ref[slot], (((1,), (1,)), ((), ())), preferred_element_type=F32
        )

    for step in range(steps):
        slot = step % 2
        if step + AHEAD < steps:
            start(step + AHEAD)
        for copy in copies(step):
            copy.wait()
        if step > 0:
            collect(1 - slot)
        for b in range(blocks):
            hot = hot_rows(ids_ref[...], tgt_ref[pl.ds(step * blocks + b, 1), :])
            some = pl.ds(step * chunk + b * per_block, per_block)
            both = jnp.concatenate(
                [
                    enc_ref[some].reshape(wide, block_grid),
                    dec_ref[some].reshape(wide, block_grid),
                ],
                axis=1,
            )
            sums = jnp.dot(hot, both, preferred_element_type=F32).astype(BF16)
            msum_ref[slot, :, b * block_grid : (b + 1) * block_grid] = sums[:, :block_grid]
            first = (step * blocks + b) * block_grid
            dsum_ref[:, pl.ds(first, block_grid)] = sums[:, block_grid:]
        for half in range(0, width, 256):
            part = pl.ds(step * width + half, 256)
            lat = silu_of_half(
                jnp.dot(
                    wt_ref[:, :channels], grid_ref[:, part], preferred_element_type=F32
                )
            ).astype(BF16)
            lat_ref[:, part] = lat
            hold_ref[slot, :, half : half + 256] = lat

    collect(1)
    me = lax.axis_index("nodes")
    flipped = acc_ref[...].astype(BF16).T
    for s in range(SLOTS):
        send_refs[s][:, :latent] = flipped[s * block_mesh : (s + 1) * block_mesh, :]
        block = slot_ref[scalar_partner(s, me, parts)].astype(F32)
        send_refs[s][:, latent:] = jnp.full((block_mesh, PAD), block, F32).astype(BF16)


def encode(parts, slot_block, owners, grid_t, w_embed, enc_coef, dec_t):
    channels, points = grid_t.shape
    latent = w_embed.shape[1]
    tiles, block_mesh, block_grid = enc_coef.shape
    grid_blocks = points // block_grid
    width = 512
    steps = points // width
    rows = SLOTS * block_mesh
    wide = tiles // grid_blocks * block_mesh
    vmem = pl.BlockSpec(memory_space=pltpu.VMEM)
    hbm = pl.BlockSpec(memory_space=pl.ANY)
    return pl.pallas_call(
        functools.partial(encode_kernel, parts, width),
        in_specs=[hbm] * 6,
        out_specs=[vmem] * (3 + SLOTS),
        out_shape=[
            pltpu.VMEM((latent, points), BF16),
            pltpu.VMEM((rows, points), BF16),
            pltpu.VMEM((channels, points), BF16),
        ]
        + [jax.ShapeDtypeStruct((block_mesh, latent + PAD), BF16)] * SLOTS,
        scratch_shapes=[
            pltpu.SMEM(slot_block.shape, jnp.int32),
            pltpu.VMEM(owners.shape, jnp.int32),
            pltpu.VMEM(w_embed.shape, BF16),
            pltpu.VMEM(enc_coef.shape, BF16),
            pltpu.VMEM(dec_t.shape, BF16),
            pltpu.VMEM((latent, 256), BF16),
            pltpu.VMEM((grid_blocks, wide), F32),
            pltpu.VMEM((rows, 128), BF16),
            pltpu.VMEM((2, rows, width), BF16),
            pltpu.VMEM((2, latent, width), BF16),
            pltpu.VMEM((latent, rows), F32),
            pltpu.VMEM((*owners.shape, wide), BF16),
            pltpu.SemaphoreType.DMA((3,)),
            pltpu.SemaphoreType.DMA((3, steps)),
        ],
        compiler_params=pltpu.CompilerParams(vmem_limit_bytes=24 * MIB),
        name="encode",
    )(
        *(
            pltpu.with_memory_space_constraint(x, pltpu.HBM)
            for x in (slot_block, owners, w_embed, grid_t, enc_coef, dec_t)
        )
    )


def prepare_kernel(parts, adj_ref, coef_ref, mid_ref, near_ref, part_ref, all_ref):
    mesh_blocks, adj_width = adj_ref.shape
    block_mesh = coef_ref.shape[2]
    me = lax.axis_index("nodes")
    core = lax.rem(me, 2)
    count = mid_ref.shape[0]
    columns = all_ref.shape[1]
    row = lax.broadcasted_iota(jnp.int32, (block_mesh, columns), 0)
    col = lax.broadcasted_iota(jnp.int32, (block_mesh, columns), 1)
    for b in range(mesh_blocks):
        total = jnp.zeros((block_mesh, columns), F32)
        for a in range(adj_width):
            which = adj_ref[b, a]
            listed = jnp.maximum(which, 0)
            side = lax.rem(lax.div(listed, mesh_blocks) - me + 1 + parts, parts)
            side = jnp.where(side == 1, 2, jnp.where((side == 2) == (core == 0), 0, 1))
            place = side * mesh_blocks + lax.rem(listed, mesh_blocks)
            place = jnp.where(which >= 0, place, -columns)
            spot = jnp.where(col == place * block_mesh + row, 1.0, 0.0).astype(BF16)
            total += jnp.dot(coef_ref[b, a], spot, preferred_element_type=F32)
        all_ref[b * block_mesh : (b + 1) * block_mesh, :] = total.astype(BF16)
    near_ref[...] = all_ref[:, : 2 * count]
    part_ref[...] = jnp.dot(
        all_ref[:, 2 * count :], mid_ref[...], preferred_element_type=F32
    )


def prepare(parts, adj, coef, mid):
    mesh_blocks, adj_width, block_mesh, _ = coef.shape
    count = mesh_blocks * block_mesh
    vmem = pl.BlockSpec(memory_space=pltpu.VMEM)
    return pl.pallas_call(
        functools.partial(prepare_kernel, parts),
        in_specs=[pl.BlockSpec(memory_space=pltpu.SMEM), vmem, vmem],
        out_specs=[vmem] * 2,
        out_shape=[
            jax.ShapeDtypeStruct((count, 2 * count), BF16),
            jax.ShapeDtypeStruct(mid.shape, F32),
        ],
        scratch_shapes=[pltpu.VMEM((count, 3 * count), BF16)],
        compiler_params=pltpu.CompilerParams(vmem_limit_bytes=8 * MIB),
        cost_estimate=pl.CostEstimate(
            flops=2 * adj_width * count * block_mesh * 3 * count,
            bytes_accessed=8 * count * 3 * count,
            transcendentals=0,
        ),
        name="prepare",
    )(adj, coef, mid)


def update_kernel(*refs):
    slots = refs[:SLOTS]
    mesh_ref, w_ref, mid_ref, ids_ref = refs[SLOTS:]
    count, latent = mesh_ref.shape
    block_mesh = slots[0].shape[0]
    sums = [slot[:, :latent].astype(F32) for slot in slots]
    ids = [slot[:, latent:].astype(F32)[:1, :1] for slot in slots]
    for s in range(SLOTS):
        ids_ref[s : s + 1, :] = jnp.broadcast_to(ids[s], (1, latent))
    parts = []
    for b in range(count // block_mesh):
        total = jnp.zeros((block_mesh, latent), F32)
        for s in range(SLOTS):
            total += jnp.where(ids[s] == b, sums[s], 0.0)
        parts.append(total.astype(BF16))
    grown = jnp.dot(jnp.concatenate(parts, axis=0), w_ref[...], preferred_element_type=F32)
    mid_ref[...] = (mesh_ref[...].astype(F32) + silu(grown)).astype(BF16)


def update(slots, mesh_in, w_enc):
    vmem = pl.BlockSpec(memory_space=pltpu.VMEM)
    return pl.pallas_call(
        update_kernel,
        in_specs=[vmem] * (SLOTS + 2),
        out_specs=[vmem] * 2,
        out_shape=[
            jax.ShapeDtypeStruct(mesh_in.shape, BF16),
            jax.ShapeDtypeStruct((8, mesh_in.shape[1]), F32),
        ],
        compiler_params=pltpu.CompilerParams(vmem_limit_bytes=8 * MIB),
        name="mesh_update",
    )(*slots, mesh_in, w_enc)


def process_kernel(
    ids_ref, mid_ref, near_mid_ref, far_mid_ref, near_ref, part_ref, gain_ref, w_ref, out_ref, *sends
):
    count, latent = mid_ref.shape
    block_mesh = sends[0].shape[0]
    around = jnp.concatenate([near_mid_ref[...], far_mid_ref[...]], axis=0)
    message = part_ref[...] + jnp.dot(near_ref[...], around, preferred_element_type=F32)
    power = jnp.mean(message * message, axis=-1, keepdims=True)
    normed = (message * lax.rsqrt(power + 1e-05) * gain_ref[...]).astype(BF16)
    grown = jnp.dot(normed, w_ref[...], preferred_element_type=F32)
    grown = mid_ref[...].astype(F32) + silu(grown)
    out_ref[...] = grown.astype(BF16)
    for s in range(SLOTS):
        chosen = grown[:block_mesh, :]
        for b in range(1, count // block_mesh):
            block = grown[b * block_mesh : (b + 1) * block_mesh, :]
            chosen = jnp.where(ids_ref[s : s + 1, :] == b, block, chosen)
        sends[s][...] = chosen.astype(BF16)


def process(block_mesh, ids, mid, near_mid, far_mid, near, part, gain, w_proc):
    vmem = pl.BlockSpec(memory_space=pltpu.VMEM)
    latent = mid.shape[1]
    return pl.pallas_call(
        process_kernel,
        in_specs=[vmem] * 8,
        out_specs=[vmem] * (1 + SLOTS),
        out_shape=[jax.ShapeDtypeStruct(mid.shape, BF16)]
        + [jax.ShapeDtypeStruct((block_mesh, latent), BF16)] * SLOTS,
        compiler_params=pltpu.CompilerParams(vmem_limit_bytes=8 * MIB),
        name="mesh_process",
    )(ids, mid, near_mid, far_mid, near, part, gain, w_proc)


def decode_kernel(width, grid_ref, lat_ref, dsum_ref, w_ref, *rest):
    slots = rest[:SLOTS]
    out_hbm, back_ref, pred_ref, hold_ref, sems = rest[SLOTS:]
    steps = grid_ref.shape[1] // width

    def copy_out(step):
        cols = pl.ds(step * width, width)
        return pltpu.make_async_copy(pred_ref.at[:, cols], out_hbm.at[:, cols], sems.at[step])

    joined = jnp.concatenate([slot[...] for slot in slots], axis=0)
    back_ref[...] = joined.T

    def predict(step, slot):
        cols = pl.ds(step * width, width)
        pred_ref[:, cols] = (
            grid_ref[:, cols].astype(F32)
            + jnp.dot(w_ref[...], hold_ref[slot], preferred_element_type=F32)
        ).astype(BF16)

    for step in range(steps):
        slot = step % 2
        if step > 0:
            predict(step - 1, 1 - slot)
            copy_out(step - 1).start()
        for half in range(0, width, 256):
            part = pl.ds(step * width + half, 256)
            decoded = jnp.dot(back_ref[...], dsum_ref[:, part], preferred_element_type=F32)
            hidden = silu(lat_ref[:, part].astype(F32) + decoded)
            hold_ref[slot, :, half : half + 256] = hidden.astype(BF16)
    predict(steps - 1, (steps - 1) % 2)
    copy_out(steps - 1).start()
    for step in range(steps):
        copy_out(step).wait()


def decode(grid_t, lat_t, dsum, w_out_t, slots):
    channels, points = grid_t.shape
    latent = lat_t.shape[0]
    rows = dsum.shape[0]
    width = 512
    vmem = pl.BlockSpec(memory_space=pltpu.VMEM)
    return pl.pallas_call(
        functools.partial(decode_kernel, width),
        in_specs=[vmem] * (4 + SLOTS),
        out_specs=pl.BlockSpec(memory_space=pl.ANY),
        out_shape=jax.ShapeDtypeStruct((channels, points), BF16),
        scratch_shapes=[
            pltpu.VMEM((latent, rows), BF16),
            pltpu.VMEM((channels, points), BF16),
            pltpu.VMEM((2, latent, width), BF16),
            pltpu.SemaphoreType.DMA((points // width,)),
        ],
        compiler_params=pltpu.CompilerParams(vmem_limit_bytes=24 * MIB),
        name="decode",
    )(grid_t, lat_t, dsum, w_out_t, *slots)


def local(
    grid_in, w_embed, enc_coef, enc_owner, slot_block, mesh_in, w_enc,
    proc_adj, proc_coef, proc_gain, w_proc, dec_coef, w_out,
):
    parts = lax.axis_size("nodes")
    block_mesh = enc_coef.shape[1]

    def swap(x, slot):
        pairs = [(i, partner(slot, i, parts)) for i in range(parts)]
        return lax.ppermute(x, "nodes", pairs)

    def swap_all(xs):
        return [xs[OWN]] + [swap(xs[s], s) for s in range(1, SLOTS)]

    lat_t, dsum, grid_t, *sums = encode(
        parts, slot_block, enc_owner.reshape(-1, 128), grid_in.T, w_embed, enc_coef,
        jnp.swapaxes(dec_coef, 1, 2),
    )
    received = swap_all(sums)
    mid, ids = update(received, mesh_in, w_enc)
    far_mid = swap(mid, FAR)
    near_mid = swap(mid, NEAR)
    near, part = prepare(parts, proc_adj, proc_coef, mid)
    mesh_out, *sends = process(
        block_mesh, ids, mid, near_mid, far_mid, near, part, proc_gain.reshape(1, -1), w_proc
    )
    returned = swap_all(sends)
    pred_t = decode(grid_t, lat_t, dsum, w_out.T, returned)
    return (pred_t.T, mesh_out)


def solution(mesh):
    return jax.shard_map(
        local,
        mesh=mesh,
        in_specs=(
            P(("groups", "nodes"), None),
            P(),
            P("nodes", None, None),
            P("nodes"),
            P("nodes"),
            P(("groups", "nodes"), None),
            P(),
            P("nodes", None),
            P("nodes", None, None, None),
            P(),
            P(),
            P("nodes", None, None),
            P(),
        ),
        out_specs=(P(("groups", "nodes"), None), P(("groups", "nodes"), None)),
        check_vma=False,
    )
```

```python
import functools

import jax
import jax.numpy as jnp
from jax import lax
from jax.experimental import pallas as pl
from jax.experimental.pallas import tpu as pltpu
from jax.sharding import PartitionSpec as P

F32 = jnp.float32
BF16 = jnp.bfloat16
MIB = 1 << 20
OWN, FAR, HALF, ODD, EVEN, NEAR = range(6)
SLOTS = 6
PAD = 128
AHEAD = 3


def partner(slot, me, parts):
    chip = me // 2 % 2
    core = me % 2
    step = {
        OWN: 0,
        HALF: parts // 2,
        ODD: 4 * chip - 2,
        EVEN: 2 - 4 * chip,
        FAR: 2 * core - 1,
        NEAR: 1 - 2 * core,
    }[slot]
    return (me + step + parts) % parts


def scalar_partner(slot, me, parts):
    chip = lax.rem(lax.div(me, 2), 2)
    core = lax.rem(me, 2)
    step = {
        OWN: 0,
        HALF: parts // 2,
        ODD: 4 * chip - 2,
        EVEN: 2 - 4 * chip,
        FAR: 2 * core - 1,
        NEAR: 1 - 2 * core,
    }[slot]
    return lax.rem(me + step + parts, parts)


def silu_of_half(half):
    return half + half * jnp.tanh(half)


def silu(x):
    return silu_of_half(0.5 * x)


def hot_rows(ids, target):
    lanes = ids.shape[1]
    target = target.astype(BF16)
    one, zero = jnp.ones((), BF16), jnp.zeros((), BF16)
    return jnp.concatenate(
        [
            jnp.where(ids == target[:, at : at + lanes], one, zero)
            for at in range(0, target.shape[1], lanes)
        ],
        axis=1,
    )


def spreads(per_block, block_mesh, groups, lanes, wide):
    out = []
    for r in range(groups):
        row = lax.broadcasted_iota(jnp.int32, (lanes, wide), 0) + r * lanes
        col = lax.broadcasted_iota(jnp.int32, (lanes, wide), 1)
        place = row - per_block * ((row * (2**19 // per_block + 1)) >> 19)
        out.append(jnp.where(place == col // block_mesh, 1.0, 0.0).astype(BF16))
    return out


def fill_targets(parts, per_block, block_mesh, spread_ref, owner_ref, tgt_ref):
    me = lax.axis_index("nodes")
    chip = lax.rem(lax.div(me, 2), 2)
    core = lax.rem(me, 2)
    up2 = EVEN + (ODD - EVEN) * chip
    up1 = NEAR + (FAR - NEAR) * core
    off = owner_ref[...] - me
    off = jnp.where(off < 0, off + parts, off)
    slot = jnp.where(off == parts // 2, HALF, OWN)
    slot = jnp.where(off == 2, up2, slot)
    slot = jnp.where(off == parts - 2, ODD + EVEN - up2, slot)
    slot = jnp.where(off == 1, up1, slot)
    slot = jnp.where(off == parts - 1, NEAR + FAR - up1, slot)
    slot = slot.astype(F32)
    groups, lanes = owner_ref.shape
    all_blocks = tgt_ref.shape[0]
    total = jnp.zeros(tgt_ref.shape, F32)
    for r in range(groups):
        tile = lax.broadcasted_iota(jnp.int32, (all_blocks, lanes), 1) + r * lanes
        first = lax.broadcasted_iota(jnp.int32, (all_blocks, lanes), 0) * per_block
        mine = (tile >= first) & (tile < first + per_block)
        picked = jnp.where(mine, slot[r : r + 1, :], 0.0).astype(BF16)
        total += jnp.dot(picked, spread_ref[r], preferred_element_type=F32)
    col = lax.broadcasted_iota(jnp.int32, tgt_ref.shape, 1)
    tgt_ref[...] = total * block_mesh + (col % block_mesh).astype(F32)


def encode_kernel(
    parts, width, slot_hbm, owner_hbm, w_hbm, grid_hbm, enc_hbm, dec_hbm,
    lat_ref, dsum_ref, grid_ref, *rest,
):
    send_refs = rest[:SLOTS]
    (
        slot_ref, owner_ref, w_ref, enc_ref, dec_ref, wt_ref, tgt_ref, ids_ref, msum_ref,
        hold_ref, acc_ref, spread_ref, small_sems, sems,
    ) = rest[SLOTS:]
    tiles, block_mesh, block_grid = enc_ref.shape
    channels, points = grid_ref.shape
    latent = w_ref.shape[1]
    per_block = tiles * block_grid // points
    blocks = width // block_grid
    chunk = blocks * per_block
    steps = points // width
    wide = per_block * block_mesh
    rows = SLOTS * block_mesh

    def copies(step):
        cols = pl.ds(step * width, width)
        some = pl.ds(step * chunk, chunk)
        return (
            pltpu.make_async_copy(grid_hbm.at[:, cols], grid_ref.at[:, cols], sems.at[0, step]),
            pltpu.make_async_copy(enc_hbm.at[some], enc_ref.at[some], sems.at[1, step]),
            pltpu.make_async_copy(dec_hbm.at[some], dec_ref.at[some], sems.at[2, step]),
        )

    small = [
        pltpu.make_async_copy(source, target, small_sems.at[i])
        for i, (source, target) in enumerate(
            ((owner_hbm, owner_ref), (w_hbm, w_ref), (slot_hbm, slot_ref))
        )
    ]
    for copy in small:
        copy.start()
    def start(step):
        for copy in copies(step):
            copy.start()

    start(0)
    ids_ref[...] = lax.broadcasted_iota(jnp.int32, ids_ref.shape, 0).astype(BF16)
    acc_ref[...] = jnp.zeros_like(acc_ref)
    for r, spread in enumerate(spreads(per_block, block_mesh, *owner_ref.shape, wide)):
        spread_ref[r] = spread
    for copy in small:
        copy.wait()
    for step in range(1, AHEAD):
        start(step)
    wt_ref[:, :channels] = (0.5 * w_ref[...].astype(F32)).T.astype(BF16)
    fill_targets(parts, per_block, block_mesh, spread_ref, owner_ref, tgt_ref)

    def collect(slot):
        acc_ref[...] += lax.dot_general(
            hold_ref[slot], msum_ref[slot], (((1,), (1,)), ((), ())), preferred_element_type=F32
        )

    for step in range(steps):
        slot = step % 2
        if step + AHEAD < steps:
            start(step + AHEAD)
        for copy in copies(step):
            copy.wait()
        if step > 0:
            collect(1 - slot)
        for b in range(blocks):
            hot = hot_rows(ids_ref[...], tgt_ref[pl.ds(step * blocks + b, 1), :])
            some = pl.ds(step * chunk + b * per_block, per_block)
            both = jnp.concatenate(
                [
                    enc_ref[some].reshape(wide, block_grid),
                    dec_ref[some].reshape(wide, block_grid),
                ],
                axis=1,
            )
            sums = jnp.dot(hot, both, preferred_element_type=F32).astype(BF16)
            msum_ref[slot, :, b * block_grid : (b + 1) * block_grid] = sums[:, :block_grid]
            first = (step * blocks + b) * block_grid
            dsum_ref[:, pl.ds(first, block_grid)] = sums[:, block_grid:]
        for at in range(0, width, 256):
            part = pl.ds(step * width + at, 256)
            half = jnp.dot(
                wt_ref[:, :channels], grid_ref[:, part], preferred_element_type=F32
            )
            lat = silu_of_half(half.astype(BF16))
            lat_ref[:, part] = lat
            hold_ref[slot, :, at : at + 256] = lat

    collect(1)
    me = lax.axis_index("nodes")
    flipped = acc_ref[...].astype(BF16).T
    for s in range(SLOTS):
        send_refs[s][:, :latent] = flipped[s * block_mesh : (s + 1) * block_mesh, :]
        block = slot_ref[scalar_partner(s, me, parts)].astype(F32)
        send_refs[s][:, latent:] = jnp.full((block_mesh, PAD), block, F32).astype(BF16)


def encode(parts, slot_block, owners, grid_t, w_embed, enc_coef, dec_t):
    channels, points = grid_t.shape
    latent = w_embed.shape[1]
    tiles, block_mesh, block_grid = enc_coef.shape
    grid_blocks = points // block_grid
    width = 512
    steps = points // width
    rows = SLOTS * block_mesh
    wide = tiles // grid_blocks * block_mesh
    vmem = pl.BlockSpec(memory_space=pltpu.VMEM)
    hbm = pl.BlockSpec(memory_space=pl.ANY)
    return pl.pallas_call(
        functools.partial(encode_kernel, parts, width),
        in_specs=[hbm] * 6,
        out_specs=[vmem] * (3 + SLOTS),
        out_shape=[
            pltpu.VMEM((latent, points), BF16),
            pltpu.VMEM((rows, points), BF16),
            pltpu.VMEM((channels, points), BF16),
        ]
        + [jax.ShapeDtypeStruct((block_mesh, latent + PAD), BF16)] * SLOTS,
        scratch_shapes=[
            pltpu.SMEM(slot_block.shape, jnp.int32),
            pltpu.VMEM(owners.shape, jnp.int32),
            pltpu.VMEM(w_embed.shape, BF16),
            pltpu.VMEM(enc_coef.shape, BF16),
            pltpu.VMEM(dec_t.shape, BF16),
            pltpu.VMEM((latent, 256), BF16),
            pltpu.VMEM((grid_blocks, wide), F32),
            pltpu.VMEM((rows, 128), BF16),
            pltpu.VMEM((2, rows, width), BF16),
            pltpu.VMEM((2, latent, width), BF16),
            pltpu.VMEM((latent, rows), F32),
            pltpu.VMEM((*owners.shape, wide), BF16),
            pltpu.SemaphoreType.DMA((3,)),
            pltpu.SemaphoreType.DMA((3, steps)),
        ],
        compiler_params=pltpu.CompilerParams(vmem_limit_bytes=24 * MIB),
        name="encode",
    )(
        *(
            pltpu.with_memory_space_constraint(x, pltpu.HBM)
            for x in (slot_block, owners, w_embed, grid_t, enc_coef, dec_t)
        )
    )


def prepare_kernel(parts, adj_ref, coef_ref, mid_ref, near_ref, part_ref, all_ref):
    mesh_blocks, adj_width = adj_ref.shape
    block_mesh = coef_ref.shape[2]
    me = lax.axis_index("nodes")
    core = lax.rem(me, 2)
    count = mid_ref.shape[0]
    columns = all_ref.shape[1]
    row = lax.broadcasted_iota(jnp.int32, (block_mesh, columns), 0)
    col = lax.broadcasted_iota(jnp.int32, (block_mesh, columns), 1)
    for b in range(mesh_blocks):
        total = jnp.zeros((block_mesh, columns), F32)
        for a in range(adj_width):
            which = adj_ref[b, a]
            listed = jnp.maximum(which, 0)
            side = lax.rem(lax.div(listed, mesh_blocks) - me + 1 + parts, parts)
            side = jnp.where(side == 1, 2, jnp.where((side == 2) == (core == 0), 0, 1))
            place = side * mesh_blocks + lax.rem(listed, mesh_blocks)
            place = jnp.where(which >= 0, place, -columns)
            spot = jnp.where(col == place * block_mesh + row, 1.0, 0.0).astype(BF16)
            total += jnp.dot(coef_ref[b, a], spot, preferred_element_type=F32)
        all_ref[b * block_mesh : (b + 1) * block_mesh, :] = total.astype(BF16)
    near_ref[...] = all_ref[:, : 2 * count]
    part_ref[...] = jnp.dot(
        all_ref[:, 2 * count :], mid_ref[...], preferred_element_type=F32
    )


def prepare(parts, adj, coef, mid):
    mesh_blocks, adj_width, block_mesh, _ = coef.shape
    count = mesh_blocks * block_mesh
    vmem = pl.BlockSpec(memory_space=pltpu.VMEM)
    return pl.pallas_call(
        functools.partial(prepare_kernel, parts),
        in_specs=[pl.BlockSpec(memory_space=pltpu.SMEM), vmem, vmem],
        out_specs=[vmem] * 2,
        out_shape=[
            jax.ShapeDtypeStruct((count, 2 * count), BF16),
            jax.ShapeDtypeStruct(mid.shape, F32),
        ],
        scratch_shapes=[pltpu.VMEM((count, 3 * count), BF16)],
        compiler_params=pltpu.CompilerParams(vmem_limit_bytes=8 * MIB),
        cost_estimate=pl.CostEstimate(
            flops=2 * adj_width * count * block_mesh * 3 * count,
            bytes_accessed=8 * count * 3 * count,
            transcendentals=0,
        ),
        name="prepare",
    )(adj, coef, mid)


def update_kernel(*refs):
    slots = refs[:SLOTS]
    mesh_ref, w_ref, mid_ref, ids_ref = refs[SLOTS:]
    count, latent = mesh_ref.shape
    block_mesh = slots[0].shape[0]
    sums = [slot[:, :latent].astype(F32) for slot in slots]
    ids = [slot[:, latent:].astype(F32)[:1, :1] for slot in slots]
    for s in range(SLOTS):
        ids_ref[s : s + 1, :] = jnp.broadcast_to(ids[s], (1, latent))
    parts = []
    for b in range(count // block_mesh):
        total = jnp.zeros((block_mesh, latent), F32)
        for s in range(SLOTS):
            total += jnp.where(ids[s] == b, sums[s], 0.0)
        parts.append(total.astype(BF16))
    grown = jnp.dot(jnp.concatenate(parts, axis=0), w_ref[...], preferred_element_type=F32)
    mid_ref[...] = (mesh_ref[...].astype(F32) + silu(grown)).astype(BF16)


def update(slots, mesh_in, w_enc):
    vmem = pl.BlockSpec(memory_space=pltpu.VMEM)
    return pl.pallas_call(
        update_kernel,
        in_specs=[vmem] * (SLOTS + 2),
        out_specs=[vmem] * 2,
        out_shape=[
            jax.ShapeDtypeStruct(mesh_in.shape, BF16),
            jax.ShapeDtypeStruct((8, mesh_in.shape[1]), F32),
        ],
        compiler_params=pltpu.CompilerParams(vmem_limit_bytes=8 * MIB),
        name="mesh_update",
    )(*slots, mesh_in, w_enc)


def process_kernel(
    ids_ref, mid_ref, near_mid_ref, far_mid_ref, near_ref, part_ref, gain_ref, w_ref, out_ref, *sends
):
    count, latent = mid_ref.shape
    block_mesh = sends[0].shape[0]
    around = jnp.concatenate([near_mid_ref[...], far_mid_ref[...]], axis=0)
    message = part_ref[...] + jnp.dot(near_ref[...], around, preferred_element_type=F32)
    power = jnp.mean(message * message, axis=-1, keepdims=True)
    normed = (message * lax.rsqrt(power + 1e-05) * gain_ref[...]).astype(BF16)
    grown = jnp.dot(normed, w_ref[...], preferred_element_type=F32)
    grown = mid_ref[...].astype(F32) + silu(grown)
    out_ref[...] = grown.astype(BF16)
    for s in range(SLOTS):
        chosen = grown[:block_mesh, :]
        for b in range(1, count // block_mesh):
            block = grown[b * block_mesh : (b + 1) * block_mesh, :]
            chosen = jnp.where(ids_ref[s : s + 1, :] == b, block, chosen)
        sends[s][...] = chosen.astype(BF16)


def process(block_mesh, ids, mid, near_mid, far_mid, near, part, gain, w_proc):
    vmem = pl.BlockSpec(memory_space=pltpu.VMEM)
    latent = mid.shape[1]
    return pl.pallas_call(
        process_kernel,
        in_specs=[vmem] * 8,
        out_specs=[vmem] * (1 + SLOTS),
        out_shape=[jax.ShapeDtypeStruct(mid.shape, BF16)]
        + [jax.ShapeDtypeStruct((block_mesh, latent), BF16)] * SLOTS,
        compiler_params=pltpu.CompilerParams(vmem_limit_bytes=8 * MIB),
        name="mesh_process",
    )(ids, mid, near_mid, far_mid, near, part, gain, w_proc)


def decode_kernel(width, grid_ref, lat_ref, dsum_ref, w_ref, *rest):
    slots = rest[:SLOTS]
    out_hbm, back_ref, pred_ref, hold_ref, sems = rest[SLOTS:]
    steps = grid_ref.shape[1] // width

    def copy_out(step):
        cols = pl.ds(step * width, width)
        return pltpu.make_async_copy(pred_ref.at[:, cols], out_hbm.at[:, cols], sems.at[step])

    joined = jnp.concatenate([slot[...] for slot in slots], axis=0)
    back_ref[...] = joined.T

    def predict(step, slot):
        cols = pl.ds(step * width, width)
        pred_ref[:, cols] = (
            grid_ref[:, cols].astype(F32)
            + jnp.dot(w_ref[...], hold_ref[slot], preferred_element_type=F32)
        ).astype(BF16)

    for step in range(steps):
        slot = step % 2
        if step > 0:
            predict(step - 1, 1 - slot)
            copy_out(step - 1).start()
        for half in range(0, width, 256):
            part = pl.ds(step * width + half, 256)
            decoded = jnp.dot(back_ref[...], dsum_ref[:, part], preferred_element_type=F32)
            halved = 0.5 * (lat_ref[:, part].astype(F32) + decoded)
            hold_ref[slot, :, half : half + 256] = silu_of_half(halved.astype(BF16))
    predict(steps - 1, (steps - 1) % 2)
    copy_out(steps - 1).start()
    for step in range(steps):
        copy_out(step).wait()


def decode(grid_t, lat_t, dsum, w_out_t, slots):
    channels, points = grid_t.shape
    latent = lat_t.shape[0]
    rows = dsum.shape[0]
    width = 512
    vmem = pl.BlockSpec(memory_space=pltpu.VMEM)
    return pl.pallas_call(
        functools.partial(decode_kernel, width),
        in_specs=[vmem] * (4 + SLOTS),
        out_specs=pl.BlockSpec(memory_space=pl.ANY),
        out_shape=jax.ShapeDtypeStruct((channels, points), BF16),
        scratch_shapes=[
            pltpu.VMEM((latent, rows), BF16),
            pltpu.VMEM((channels, points), BF16),
            pltpu.VMEM((2, latent, width), BF16),
            pltpu.SemaphoreType.DMA((points // width,)),
        ],
        compiler_params=pltpu.CompilerParams(vmem_limit_bytes=24 * MIB),
        name="decode",
    )(grid_t, lat_t, dsum, w_out_t, *slots)


def local(
    grid_in, w_embed, enc_coef, enc_owner, slot_block, mesh_in, w_enc,
    proc_adj, proc_coef, proc_gain, w_proc, dec_coef, w_out,
):
    parts = lax.axis_size("nodes")
    block_mesh = enc_coef.shape[1]

    def swap(x, slot):
        pairs = [(i, partner(slot, i, parts)) for i in range(parts)]
        return lax.ppermute(x, "nodes", pairs)

    def swap_all(xs):
        return [xs[OWN]] + [swap(xs[s], s) for s in range(1, SLOTS)]

    lat_t, dsum, grid_t, *sums = encode(
        parts, slot_block, enc_owner.reshape(-1, 128), grid_in.T, w_embed, enc_coef,
        jnp.swapaxes(dec_coef, 1, 2),
    )
    received = swap_all(sums)
    mid, ids = update(received, mesh_in, w_enc)
    far_mid = swap(mid, FAR)
    near_mid = swap(mid, NEAR)
    near, part = prepare(parts, proc_adj, proc_coef, mid)
    mesh_out, *sends = process(
        block_mesh, ids, mid, near_mid, far_mid, near, part, proc_gain.reshape(1, -1), w_proc
    )
    returned = swap_all(sends)
    pred_t = decode(grid_t, lat_t, dsum, w_out.T, returned)
    return (pred_t.T, mesh_out)


def solution(mesh):
    return jax.shard_map(
        local,
        mesh=mesh,
        in_specs=(
            P(("groups", "nodes"), None),
            P(),
            P("nodes", None, None),
            P("nodes"),
            P("nodes"),
            P(("groups", "nodes"), None),
            P(),
            P("nodes", None),
            P("nodes", None, None, None),
            P(),
            P(),
            P("nodes", None, None),
            P(),
        ),
        out_specs=(P(("groups", "nodes"), None), P(("groups", "nodes"), None)),
        check_vma=False,
    )
```

```python
import functools

import jax
import jax.numpy as jnp
from jax import lax
from jax.experimental import pallas as pl
from jax.experimental.pallas import tpu as pltpu
from jax.sharding import PartitionSpec as P

F32 = jnp.float32
BF16 = jnp.bfloat16
MIB = 1 << 20
OWN, ODD, HALF, FAR, EVEN, NEAR = range(6)
SLOTS = 6
PAD = 128
AHEAD = 3


def partner(slot, me, parts):
    chip = me // 2 % 2
    core = me % 2
    step = {
        OWN: 0,
        HALF: parts // 2,
        ODD: 4 * chip - 2,
        EVEN: 2 - 4 * chip,
        FAR: 2 * core - 1,
        NEAR: 1 - 2 * core,
    }[slot]
    return (me + step + parts) % parts


def scalar_partner(slot, me, parts):
    chip = lax.rem(lax.div(me, 2), 2)
    core = lax.rem(me, 2)
    step = {
        OWN: 0,
        HALF: parts // 2,
        ODD: 4 * chip - 2,
        EVEN: 2 - 4 * chip,
        FAR: 2 * core - 1,
        NEAR: 1 - 2 * core,
    }[slot]
    return lax.rem(me + step + parts, parts)


def silu_of_half(half):
    return half + half * jnp.tanh(half)


def silu(x):
    return silu_of_half(0.5 * x)


def hot_rows(ids, target):
    lanes = ids.shape[1]
    target = target.astype(BF16)
    one, zero = jnp.ones((), BF16), jnp.zeros((), BF16)
    return jnp.concatenate(
        [
            jnp.where(ids == target[:, at : at + lanes], one, zero)
            for at in range(0, target.shape[1], lanes)
        ],
        axis=1,
    )


def spreads(per_block, block_mesh, groups, lanes, wide):
    out = []
    for r in range(groups):
        row = lax.broadcasted_iota(jnp.int32, (lanes, wide), 0) + r * lanes
        col = lax.broadcasted_iota(jnp.int32, (lanes, wide), 1)
        place = row - per_block * ((row * (2**19 // per_block + 1)) >> 19)
        out.append(jnp.where(place == col // block_mesh, 1.0, 0.0).astype(BF16))
    return out


def fill_targets(parts, per_block, block_mesh, spread_ref, owner_ref, tgt_ref):
    me = lax.axis_index("nodes")
    chip = lax.rem(lax.div(me, 2), 2)
    core = lax.rem(me, 2)
    up2 = EVEN + (ODD - EVEN) * chip
    up1 = NEAR + (FAR - NEAR) * core
    off = owner_ref[...] - me
    off = jnp.where(off < 0, off + parts, off)
    slot = jnp.where(off == parts // 2, HALF, OWN)
    slot = jnp.where(off == 2, up2, slot)
    slot = jnp.where(off == parts - 2, ODD + EVEN - up2, slot)
    slot = jnp.where(off == 1, up1, slot)
    slot = jnp.where(off == parts - 1, NEAR + FAR - up1, slot)
    slot = slot.astype(F32)
    groups, lanes = owner_ref.shape
    all_blocks = tgt_ref.shape[0]
    total = jnp.zeros(tgt_ref.shape, F32)
    for r in range(groups):
        tile = lax.broadcasted_iota(jnp.int32, (all_blocks, lanes), 1) + r * lanes
        first = lax.broadcasted_iota(jnp.int32, (all_blocks, lanes), 0) * per_block
        mine = (tile >= first) & (tile < first + per_block)
        picked = jnp.where(mine, slot[r : r + 1, :], 0.0).astype(BF16)
        total += jnp.dot(picked, spread_ref[r], preferred_element_type=F32)
    col = lax.broadcasted_iota(jnp.int32, tgt_ref.shape, 1)
    tgt_ref[...] = total * block_mesh + (col % block_mesh).astype(F32)


def encode_kernel(
    parts, width, slot_hbm, owner_hbm, w_hbm, grid_hbm, enc_hbm, dec_hbm,
    lat_ref, dsum_ref, grid_ref, *rest,
):
    send_refs = rest[:SLOTS]
    (
        slot_ref, owner_ref, w_ref, enc_ref, dec_ref, wt_ref, tgt_ref, ids_ref, msum_ref,
        hold_ref, acc_ref, spread_ref, small_sems, sems,
    ) = rest[SLOTS:]
    tiles, block_mesh, block_grid = enc_ref.shape
    channels, points = grid_ref.shape
    latent = w_ref.shape[1]
    per_block = tiles * block_grid // points
    blocks = width // block_grid
    chunk = blocks * per_block
    steps = points // width
    wide = per_block * block_mesh
    rows = SLOTS * block_mesh

    def copies(step):
        cols = pl.ds(step * width, width)
        some = pl.ds(step * chunk, chunk)
        return (
            pltpu.make_async_copy(grid_hbm.at[:, cols], grid_ref.at[:, cols], sems.at[0, step]),
            pltpu.make_async_copy(enc_hbm.at[some], enc_ref.at[some], sems.at[1, step]),
            pltpu.make_async_copy(dec_hbm.at[some], dec_ref.at[some], sems.at[2, step]),
        )

    small = [
        pltpu.make_async_copy(source, target, small_sems.at[i])
        for i, (source, target) in enumerate(
            ((owner_hbm, owner_ref), (w_hbm, w_ref), (slot_hbm, slot_ref))
        )
    ]
    for copy in small:
        copy.start()
    def start(step):
        for copy in copies(step):
            copy.start()

    start(0)
    ids_ref[...] = lax.broadcasted_iota(jnp.int32, ids_ref.shape, 0).astype(BF16)
    acc_ref[...] = jnp.zeros_like(acc_ref)
    for r, spread in enumerate(spreads(per_block, block_mesh, *owner_ref.shape, wide)):
        spread_ref[r] = spread
    for copy in small:
        copy.wait()
    for step in range(1, AHEAD):
        start(step)
    wt_ref[:, :channels] = (0.5 * w_ref[...].astype(F32)).T.astype(BF16)
    fill_targets(parts, per_block, block_mesh, spread_ref, owner_ref, tgt_ref)

    def collect(slot):
        acc_ref[...] += lax.dot_general(
            hold_ref[slot], msum_ref[slot], (((1,), (1,)), ((), ())), preferred_element_type=F32
        )

    for step in range(steps):
        slot = step % 2
        if step + AHEAD < steps:
            start(step + AHEAD)
        for copy in copies(step):
            copy.wait()
        if step > 0:
            collect(1 - slot)
        for b in range(blocks):
            hot = hot_rows(ids_ref[...], tgt_ref[pl.ds(step * blocks + b, 1), :])
            some = pl.ds(step * chunk + b * per_block, per_block)
            both = jnp.concatenate(
                [
                    enc_ref[some].reshape(wide, block_grid),
                    dec_ref[some].reshape(wide, block_grid),
                ],
                axis=1,
            )
            sums = jnp.dot(hot, both, preferred_element_type=F32).astype(BF16)
            msum_ref[slot, :, b * block_grid : (b + 1) * block_grid] = sums[:, :block_grid]
            first = (step * blocks + b) * block_grid
            dsum_ref[:, pl.ds(first, block_grid)] = sums[:, block_grid:]
        for half in range(0, width, 256):
            part = pl.ds(step * width + half, 256)
            lat = silu_of_half(
                jnp.dot(
                    wt_ref[:, :channels], grid_ref[:, part], preferred_element_type=F32
                )
            ).astype(BF16)
            lat_ref[:, part] = lat
            hold_ref[slot, :, half : half + 256] = lat

    collect(1)
    me = lax.axis_index("nodes")
    flipped = acc_ref[...].astype(BF16).T
    for s in range(SLOTS):
        send_refs[s][:, :latent] = flipped[s * block_mesh : (s + 1) * block_mesh, :]
        block = slot_ref[scalar_partner(s, me, parts)].astype(F32)
        send_refs[s][:, latent:] = jnp.full((block_mesh, PAD), block, F32).astype(BF16)


def encode(parts, slot_block, owners, grid_t, w_embed, enc_coef, dec_t):
    channels, points = grid_t.shape
    latent = w_embed.shape[1]
    tiles, block_mesh, block_grid = enc_coef.shape
    grid_blocks = points // block_grid
    width = 512
    steps = points // width
    rows = SLOTS * block_mesh
    wide = tiles // grid_blocks * block_mesh
    vmem = pl.BlockSpec(memory_space=pltpu.VMEM)
    hbm = pl.BlockSpec(memory_space=pl.ANY)
    return pl.pallas_call(
        functools.partial(encode_kernel, parts, width),
        in_specs=[hbm] * 6,
        out_specs=[vmem] * (3 + SLOTS),
        out_shape=[
            pltpu.VMEM((latent, points), BF16),
            pltpu.VMEM((rows, points), BF16),
            pltpu.VMEM((channels, points), BF16),
        ]
        + [jax.ShapeDtypeStruct((block_mesh, latent + PAD), BF16)] * SLOTS,
        scratch_shapes=[
            pltpu.SMEM(slot_block.shape, jnp.int32),
            pltpu.VMEM(owners.shape, jnp.int32),
            pltpu.VMEM(w_embed.shape, BF16),
            pltpu.VMEM(enc_coef.shape, BF16),
            pltpu.VMEM(dec_t.shape, BF16),
            pltpu.VMEM((latent, 256), BF16),
            pltpu.VMEM((grid_blocks, wide), F32),
            pltpu.VMEM((rows, 128), BF16),
            pltpu.VMEM((2, rows, width), BF16),
            pltpu.VMEM((2, latent, width), BF16),
            pltpu.VMEM((latent, rows), F32),
            pltpu.VMEM((*owners.shape, wide), BF16),
            pltpu.SemaphoreType.DMA((3,)),
            pltpu.SemaphoreType.DMA((3, steps)),
        ],
        compiler_params=pltpu.CompilerParams(vmem_limit_bytes=24 * MIB),
        name="encode",
    )(
        *(
            pltpu.with_memory_space_constraint(x, pltpu.HBM)
            for x in (slot_block, owners, w_embed, grid_t, enc_coef, dec_t)
        )
    )


def prepare_kernel(parts, adj_ref, coef_ref, mid_ref, near_ref, part_ref, all_ref):
    mesh_blocks, adj_width = adj_ref.shape
    block_mesh = coef_ref.shape[2]
    me = lax.axis_index("nodes")
    core = lax.rem(me, 2)
    count = mid_ref.shape[0]
    columns = all_ref.shape[1]
    row = lax.broadcasted_iota(jnp.int32, (block_mesh, columns), 0)
    col = lax.broadcasted_iota(jnp.int32, (block_mesh, columns), 1)
    for b in range(mesh_blocks):
        total = jnp.zeros((block_mesh, columns), F32)
        for a in range(adj_width):
            which = adj_ref[b, a]
            listed = jnp.maximum(which, 0)
            side = lax.rem(lax.div(listed, mesh_blocks) - me + 1 + parts, parts)
            side = jnp.where(side == 1, 2, jnp.where((side == 2) == (core == 0), 0, 1))
            place = side * mesh_blocks + lax.rem(listed, mesh_blocks)
            place = jnp.where(which >= 0, place, -columns)
            spot = jnp.where(col == place * block_mesh + row, 1.0, 0.0).astype(BF16)
            total += jnp.dot(coef_ref[b, a], spot, preferred_element_type=F32)
        all_ref[b * block_mesh : (b + 1) * block_mesh, :] = total.astype(BF16)
    near_ref[...] = all_ref[:, : 2 * count]
    part_ref[...] = jnp.dot(
        all_ref[:, 2 * count :], mid_ref[...], preferred_element_type=F32
    )


def prepare(parts, adj, coef, mid):
    mesh_blocks, adj_width, block_mesh, _ = coef.shape
    count = mesh_blocks * block_mesh
    vmem = pl.BlockSpec(memory_space=pltpu.VMEM)
    return pl.pallas_call(
        functools.partial(prepare_kernel, parts),
        in_specs=[pl.BlockSpec(memory_space=pltpu.SMEM), vmem, vmem],
        out_specs=[vmem] * 2,
        out_shape=[
            jax.ShapeDtypeStruct((count, 2 * count), BF16),
            jax.ShapeDtypeStruct(mid.shape, F32),
        ],
        scratch_shapes=[pltpu.VMEM((count, 3 * count), BF16)],
        compiler_params=pltpu.CompilerParams(vmem_limit_bytes=8 * MIB),
        cost_estimate=pl.CostEstimate(
            flops=2 * adj_width * count * block_mesh * 3 * count,
            bytes_accessed=8 * count * 3 * count,
            transcendentals=0,
        ),
        name="prepare",
    )(adj, coef, mid)


def update_kernel(*refs):
    slots = refs[:SLOTS]
    mesh_ref, w_ref, mid_ref, ids_ref = refs[SLOTS:]
    count, latent = mesh_ref.shape
    block_mesh = slots[0].shape[0]
    sums = [slot[:, :latent].astype(F32) for slot in slots]
    ids = [slot[:, latent:].astype(F32)[:1, :1] for slot in slots]
    for s in range(SLOTS):
        ids_ref[s : s + 1, :] = jnp.broadcast_to(ids[s], (1, latent))
    parts = []
    for b in range(count // block_mesh):
        total = jnp.zeros((block_mesh, latent), F32)
        for s in range(SLOTS):
            total += jnp.where(ids[s] == b, sums[s], 0.0)
        parts.append(total.astype(BF16))
    grown = jnp.dot(jnp.concatenate(parts, axis=0), w_ref[...], preferred_element_type=F32)
    mid_ref[...] = (mesh_ref[...].astype(F32) + silu(grown)).astype(BF16)


def update(slots, mesh_in, w_enc):
    vmem = pl.BlockSpec(memory_space=pltpu.VMEM)
    return pl.pallas_call(
        update_kernel,
        in_specs=[vmem] * (SLOTS + 2),
        out_specs=[vmem] * 2,
        out_shape=[
            jax.ShapeDtypeStruct(mesh_in.shape, BF16),
            jax.ShapeDtypeStruct((8, mesh_in.shape[1]), F32),
        ],
        compiler_params=pltpu.CompilerParams(vmem_limit_bytes=8 * MIB),
        name="mesh_update",
    )(*slots, mesh_in, w_enc)


def process_kernel(
    ids_ref, mid_ref, near_mid_ref, far_mid_ref, near_ref, part_ref, gain_ref, w_ref, out_ref, *sends
):
    count, latent = mid_ref.shape
    block_mesh = sends[0].shape[0]
    around = jnp.concatenate([near_mid_ref[...], far_mid_ref[...]], axis=0)
    message = part_ref[...] + jnp.dot(near_ref[...], around, preferred_element_type=F32)
    power = jnp.mean(message * message, axis=-1, keepdims=True)
    normed = (message * lax.rsqrt(power + 1e-05) * gain_ref[...]).astype(BF16)
    grown = jnp.dot(normed, w_ref[...], preferred_element_type=F32)
    grown = mid_ref[...].astype(F32) + silu(grown)
    out_ref[...] = grown.astype(BF16)
    for s in range(SLOTS):
        chosen = grown[:block_mesh, :]
        for b in range(1, count // block_mesh):
            block = grown[b * block_mesh : (b + 1) * block_mesh, :]
            chosen = jnp.where(ids_ref[s : s + 1, :] == b, block, chosen)
        sends[s][...] = chosen.astype(BF16)


def process(block_mesh, ids, mid, near_mid, far_mid, near, part, gain, w_proc):
    vmem = pl.BlockSpec(memory_space=pltpu.VMEM)
    latent = mid.shape[1]
    return pl.pallas_call(
        process_kernel,
        in_specs=[vmem] * 8,
        out_specs=[vmem] * (1 + SLOTS),
        out_shape=[jax.ShapeDtypeStruct(mid.shape, BF16)]
        + [jax.ShapeDtypeStruct((block_mesh, latent), BF16)] * SLOTS,
        compiler_params=pltpu.CompilerParams(vmem_limit_bytes=8 * MIB),
        name="mesh_process",
    )(ids, mid, near_mid, far_mid, near, part, gain, w_proc)


def decode_kernel(width, grid_ref, lat_ref, dsum_ref, w_ref, *rest):
    slots = rest[:SLOTS]
    out_hbm, back_ref, pred_ref, hold_ref, sems = rest[SLOTS:]
    steps = grid_ref.shape[1] // width

    def copy_out(step):
        cols = pl.ds(step * width, width)
        return pltpu.make_async_copy(pred_ref.at[:, cols], out_hbm.at[:, cols], sems.at[step])

    joined = jnp.concatenate([slot[...] for slot in slots], axis=0)
    back_ref[...] = (BF16(0.5) * joined).T

    def predict(step, slot):
        cols = pl.ds(step * width, width)
        pred_ref[:, cols] = (
            grid_ref[:, cols].astype(F32)
            + jnp.dot(w_ref[...], hold_ref[slot], preferred_element_type=F32)
        ).astype(BF16)

    for step in range(steps):
        slot = step % 2
        if step > 0:
            predict(step - 1, 1 - slot)
            copy_out(step - 1).start()
        for half in range(0, width, 256):
            part = pl.ds(step * width + half, 256)
            decoded = jnp.dot(back_ref[...], dsum_ref[:, part], preferred_element_type=F32)
            halved = BF16(0.5) * lat_ref[:, part] + decoded.astype(BF16)
            hold_ref[slot, :, half : half + 256] = silu_of_half(halved)
    predict(steps - 1, (steps - 1) % 2)
    copy_out(steps - 1).start()
    for step in range(steps):
        copy_out(step).wait()


def decode(grid_t, lat_t, dsum, w_out_t, slots):
    channels, points = grid_t.shape
    latent = lat_t.shape[0]
    rows = dsum.shape[0]
    width = 512
    vmem = pl.BlockSpec(memory_space=pltpu.VMEM)
    return pl.pallas_call(
        functools.partial(decode_kernel, width),
        in_specs=[vmem] * (4 + SLOTS),
        out_specs=pl.BlockSpec(memory_space=pl.ANY),
        out_shape=jax.ShapeDtypeStruct((channels, points), BF16),
        scratch_shapes=[
            pltpu.VMEM((latent, rows), BF16),
            pltpu.VMEM((channels, points), BF16),
            pltpu.VMEM((2, latent, width), BF16),
            pltpu.SemaphoreType.DMA((points // width,)),
        ],
        compiler_params=pltpu.CompilerParams(vmem_limit_bytes=24 * MIB),
        name="decode",
    )(grid_t, lat_t, dsum, w_out_t, *slots)


def local(
    grid_in, w_embed, enc_coef, enc_owner, slot_block, mesh_in, w_enc,
    proc_adj, proc_coef, proc_gain, w_proc, dec_coef, w_out,
):
    parts = lax.axis_size("nodes")
    block_mesh = enc_coef.shape[1]

    def swap(x, slot):
        pairs = [(i, partner(slot, i, parts)) for i in range(parts)]
        return lax.ppermute(x, "nodes", pairs)

    def swap_all(xs):
        return [xs[OWN]] + [swap(xs[s], s) for s in range(1, SLOTS)]

    lat_t, dsum, grid_t, *sums = encode(
        parts, slot_block, enc_owner.reshape(-1, 128), grid_in.T, w_embed, enc_coef,
        jnp.swapaxes(dec_coef, 1, 2),
    )
    received = swap_all(sums)
    mid, ids = update(received, mesh_in, w_enc)
    far_mid = swap(mid, FAR)
    near_mid = swap(mid, NEAR)
    near, part = prepare(parts, proc_adj, proc_coef, mid)
    mesh_out, *sends = process(
        block_mesh, ids, mid, near_mid, far_mid, near, part, proc_gain.reshape(1, -1), w_proc
    )
    returned = swap_all(sends)
    pred_t = decode(grid_t, lat_t, dsum, w_out.T, returned)
    return (pred_t.T, mesh_out)


def solution(mesh):
    return jax.shard_map(
        local,
        mesh=mesh,
        in_specs=(
            P(("groups", "nodes"), None),
            P(),
            P("nodes", None, None),
            P("nodes"),
            P("nodes"),
            P(("groups", "nodes"), None),
            P(),
            P("nodes", None),
            P("nodes", None, None, None),
            P(),
            P(),
            P("nodes", None, None),
            P(),
        ),
        out_specs=(P(("groups", "nodes"), None), P(("groups", "nodes"), None)),
        check_vma=False,
    )
```

```python
import functools

import jax
import jax.numpy as jnp
from jax import lax
from jax.experimental import pallas as pl
from jax.experimental.pallas import tpu as pltpu
from jax.sharding import PartitionSpec as P

F32 = jnp.float32
BF16 = jnp.bfloat16
MIB = 1 << 20
OWN, ODD, HALF, FAR, EVEN, NEAR = range(6)
SLOTS = 6
PAD = 128
AHEAD = 3


def partner(slot, me, parts):
    chip = me // 2 % 2
    core = me % 2
    step = {
        OWN: 0,
        HALF: parts // 2,
        ODD: 4 * chip - 2,
        EVEN: 2 - 4 * chip,
        FAR: 2 * core - 1,
        NEAR: 1 - 2 * core,
    }[slot]
    return (me + step + parts) % parts


def scalar_partner(slot, me, parts):
    chip = lax.rem(lax.div(me, 2), 2)
    core = lax.rem(me, 2)
    step = {
        OWN: 0,
        HALF: parts // 2,
        ODD: 4 * chip - 2,
        EVEN: 2 - 4 * chip,
        FAR: 2 * core - 1,
        NEAR: 1 - 2 * core,
    }[slot]
    return lax.rem(me + step + parts, parts)


def silu_of_half(half):
    return half + half * jnp.tanh(half)


def silu(x):
    return silu_of_half(0.5 * x)


def hot_rows(ids, target):
    lanes = ids.shape[1]
    target = target.astype(BF16)
    one, zero = jnp.ones((), BF16), jnp.zeros((), BF16)
    return jnp.concatenate(
        [
            jnp.where(ids == target[:, at : at + lanes], one, zero)
            for at in range(0, target.shape[1], lanes)
        ],
        axis=1,
    )


def spreads(per_block, block_mesh, groups, lanes, wide):
    out = []
    for r in range(groups):
        row = lax.broadcasted_iota(jnp.int32, (lanes, wide), 0) + r * lanes
        col = lax.broadcasted_iota(jnp.int32, (lanes, wide), 1)
        place = row - per_block * ((row * (2**19 // per_block + 1)) >> 19)
        out.append(jnp.where(place == col // block_mesh, 1.0, 0.0).astype(BF16))
    return out


def fill_targets(parts, per_block, block_mesh, spread_ref, owner_ref, tgt_ref):
    me = lax.axis_index("nodes")
    chip = lax.rem(lax.div(me, 2), 2)
    core = lax.rem(me, 2)
    up2 = EVEN + (ODD - EVEN) * chip
    up1 = NEAR + (FAR - NEAR) * core
    off = owner_ref[...] - me
    off = jnp.where(off < 0, off + parts, off)
    slot = jnp.where(off == parts // 2, HALF, OWN)
    slot = jnp.where(off == 2, up2, slot)
    slot = jnp.where(off == parts - 2, ODD + EVEN - up2, slot)
    slot = jnp.where(off == 1, up1, slot)
    slot = jnp.where(off == parts - 1, NEAR + FAR - up1, slot)
    slot = slot.astype(F32)
    groups, lanes = owner_ref.shape
    all_blocks = tgt_ref.shape[0]
    total = jnp.zeros(tgt_ref.shape, F32)
    for r in range(groups):
        tile = lax.broadcasted_iota(jnp.int32, (all_blocks, lanes), 1) + r * lanes
        first = lax.broadcasted_iota(jnp.int32, (all_blocks, lanes), 0) * per_block
        mine = (tile >= first) & (tile < first + per_block)
        picked = jnp.where(mine, slot[r : r + 1, :], 0.0).astype(BF16)
        total += jnp.dot(picked, spread_ref[r], preferred_element_type=F32)
    col = lax.broadcasted_iota(jnp.int32, tgt_ref.shape, 1)
    tgt_ref[...] = total * block_mesh + (col % block_mesh).astype(F32)


def encode_kernel(
    parts, width, slot_hbm, owner_hbm, w_hbm, grid_hbm, enc_hbm, dec_hbm,
    lat_ref, dsum_ref, grid_ref, *rest,
):
    send_refs = rest[:SLOTS]
    (
        slot_ref, owner_ref, w_ref, enc_ref, dec_ref, wt_ref, tgt_ref, ids_ref, msum_ref,
        acc_ref, spread_ref, small_sems, sems,
    ) = rest[SLOTS:]
    tiles, block_mesh, block_grid = enc_ref.shape
    channels, points = grid_ref.shape
    latent = w_ref.shape[1]
    per_block = tiles * block_grid // points
    blocks = width // block_grid
    chunk = blocks * per_block
    steps = points // width
    wide = per_block * block_mesh
    rows = SLOTS * block_mesh

    def copies(step):
        cols = pl.ds(step * width, width)
        some = pl.ds(step * chunk, chunk)
        return (
            pltpu.make_async_copy(grid_hbm.at[:, cols], grid_ref.at[:, cols], sems.at[0, step]),
            pltpu.make_async_copy(enc_hbm.at[some], enc_ref.at[some], sems.at[1, step]),
            pltpu.make_async_copy(dec_hbm.at[some], dec_ref.at[some], sems.at[2, step]),
        )

    small = [
        pltpu.make_async_copy(source, target, small_sems.at[i])
        for i, (source, target) in enumerate(
            ((owner_hbm, owner_ref), (w_hbm, w_ref), (slot_hbm, slot_ref))
        )
    ]
    for copy in small:
        copy.start()
    def start(step):
        for copy in copies(step):
            copy.start()

    start(0)
    ids_ref[...] = lax.broadcasted_iota(jnp.int32, ids_ref.shape, 0).astype(BF16)
    acc_ref[...] = jnp.zeros_like(acc_ref)
    for r, spread in enumerate(spreads(per_block, block_mesh, *owner_ref.shape, wide)):
        spread_ref[r] = spread
    for copy in small:
        copy.wait()
    for step in range(1, AHEAD):
        start(step)
    wt_ref[:, :channels] = (0.5 * w_ref[...].astype(F32)).T.astype(BF16)
    fill_targets(parts, per_block, block_mesh, spread_ref, owner_ref, tgt_ref)

    def collect(step):
        lat = lat_ref[:, step * width : (step + 1) * width]
        acc_ref[...] += lax.dot_general(
            msum_ref[step % 2], lat, (((1,), (1,)), ((), ())), preferred_element_type=F32
        )

    for step in range(steps):
        slot = step % 2
        if step + AHEAD < steps:
            start(step + AHEAD)
        for copy in copies(step):
            copy.wait()
        if step > 0:
            collect(step - 1)
        for b in range(blocks):
            hot = hot_rows(ids_ref[...], tgt_ref[pl.ds(step * blocks + b, 1), :])
            some = pl.ds(step * chunk + b * per_block, per_block)
            both = jnp.concatenate(
                [
                    enc_ref[some].reshape(wide, block_grid),
                    dec_ref[some].reshape(wide, block_grid),
                ],
                axis=1,
            )
            sums = jnp.dot(hot, both, preferred_element_type=F32).astype(BF16)
            msum_ref[slot, :, b * block_grid : (b + 1) * block_grid] = sums[:, :block_grid]
            first = (step * blocks + b) * block_grid
            dsum_ref[:, pl.ds(first, block_grid)] = sums[:, block_grid:]
        for half in range(0, width, 256):
            part = pl.ds(step * width + half, 256)
            lat = silu_of_half(
                jnp.dot(
                    wt_ref[:, :channels], grid_ref[:, part], preferred_element_type=F32
                )
            ).astype(BF16)
            lat_ref[:, part] = lat

    collect(steps - 1)
    me = lax.axis_index("nodes")
    summed = acc_ref[...].astype(BF16)
    for s in range(SLOTS):
        send_refs[s][:, :latent] = summed[s * block_mesh : (s + 1) * block_mesh, :]
        block = slot_ref[scalar_partner(s, me, parts)].astype(F32)
        send_refs[s][:, latent:] = jnp.full((block_mesh, PAD), block, F32).astype(BF16)


def encode(parts, slot_block, owners, grid_t, w_embed, enc_coef, dec_t):
    channels, points = grid_t.shape
    latent = w_embed.shape[1]
    tiles, block_mesh, block_grid = enc_coef.shape
    grid_blocks = points // block_grid
    width = 512
    steps = points // width
    rows = SLOTS * block_mesh
    wide = tiles // grid_blocks * block_mesh
    vmem = pl.BlockSpec(memory_space=pltpu.VMEM)
    hbm = pl.BlockSpec(memory_space=pl.ANY)
    return pl.pallas_call(
        functools.partial(encode_kernel, parts, width),
        in_specs=[hbm] * 6,
        out_specs=[vmem] * (3 + SLOTS),
        out_shape=[
            pltpu.VMEM((latent, points), BF16),
            pltpu.VMEM((rows, points), BF16),
            pltpu.VMEM((channels, points), BF16),
        ]
        + [jax.ShapeDtypeStruct((block_mesh, latent + PAD), BF16)] * SLOTS,
        scratch_shapes=[
            pltpu.SMEM(slot_block.shape, jnp.int32),
            pltpu.VMEM(owners.shape, jnp.int32),
            pltpu.VMEM(w_embed.shape, BF16),
            pltpu.VMEM(enc_coef.shape, BF16),
            pltpu.VMEM(dec_t.shape, BF16),
            pltpu.VMEM((latent, 256), BF16),
            pltpu.VMEM((grid_blocks, wide), F32),
            pltpu.VMEM((rows, 128), BF16),
            pltpu.VMEM((2, rows, width), BF16),
            pltpu.VMEM((rows, latent), F32),
            pltpu.VMEM((*owners.shape, wide), BF16),
            pltpu.SemaphoreType.DMA((3,)),
            pltpu.SemaphoreType.DMA((3, steps)),
        ],
        compiler_params=pltpu.CompilerParams(vmem_limit_bytes=24 * MIB),
        name="encode",
    )(
        *(
            pltpu.with_memory_space_constraint(x, pltpu.HBM)
            for x in (slot_block, owners, w_embed, grid_t, enc_coef, dec_t)
        )
    )


def prepare_kernel(parts, adj_ref, coef_ref, mid_ref, near_ref, part_ref, all_ref):
    mesh_blocks, adj_width = adj_ref.shape
    block_mesh = coef_ref.shape[2]
    me = lax.axis_index("nodes")
    core = lax.rem(me, 2)
    count = mid_ref.shape[0]
    columns = all_ref.shape[1]
    row = lax.broadcasted_iota(jnp.int32, (block_mesh, columns), 0)
    col = lax.broadcasted_iota(jnp.int32, (block_mesh, columns), 1)
    for b in range(mesh_blocks):
        total = jnp.zeros((block_mesh, columns), F32)
        for a in range(adj_width):
            which = adj_ref[b, a]
            listed = jnp.maximum(which, 0)
            side = lax.rem(lax.div(listed, mesh_blocks) - me + 1 + parts, parts)
            side = jnp.where(side == 1, 2, jnp.where((side == 2) == (core == 0), 0, 1))
            place = side * mesh_blocks + lax.rem(listed, mesh_blocks)
            place = jnp.where(which >= 0, place, -columns)
            spot = jnp.where(col == place * block_mesh + row, 1.0, 0.0).astype(BF16)
            total += jnp.dot(coef_ref[b, a], spot, preferred_element_type=F32)
        all_ref[b * block_mesh : (b + 1) * block_mesh, :] = total.astype(BF16)
    near_ref[...] = all_ref[:, : 2 * count]
    part_ref[...] = jnp.dot(
        all_ref[:, 2 * count :], mid_ref[...], preferred_element_type=F32
    )


def prepare(parts, adj, coef, mid):
    mesh_blocks, adj_width, block_mesh, _ = coef.shape
    count = mesh_blocks * block_mesh
    vmem = pl.BlockSpec(memory_space=pltpu.VMEM)
    return pl.pallas_call(
        functools.partial(prepare_kernel, parts),
        in_specs=[pl.BlockSpec(memory_space=pltpu.SMEM), vmem, vmem],
        out_specs=[vmem] * 2,
        out_shape=[
            jax.ShapeDtypeStruct((count, 2 * count), BF16),
            jax.ShapeDtypeStruct(mid.shape, F32),
        ],
        scratch_shapes=[pltpu.VMEM((count, 3 * count), BF16)],
        compiler_params=pltpu.CompilerParams(vmem_limit_bytes=8 * MIB),
        cost_estimate=pl.CostEstimate(
            flops=2 * adj_width * count * block_mesh * 3 * count,
            bytes_accessed=8 * count * 3 * count,
            transcendentals=0,
        ),
        name="prepare",
    )(adj, coef, mid)


def update_kernel(*refs):
    slots = refs[:SLOTS]
    mesh_ref, w_ref, mid_ref, ids_ref = refs[SLOTS:]
    count, latent = mesh_ref.shape
    block_mesh = slots[0].shape[0]
    sums = [slot[:, :latent].astype(F32) for slot in slots]
    ids = [slot[:, latent:].astype(F32)[:1, :1] for slot in slots]
    for s in range(SLOTS):
        ids_ref[s : s + 1, :] = jnp.broadcast_to(ids[s], (1, latent))
    parts = []
    for b in range(count // block_mesh):
        total = jnp.zeros((block_mesh, latent), F32)
        for s in range(SLOTS):
            total += jnp.where(ids[s] == b, sums[s], 0.0)
        parts.append(total.astype(BF16))
    grown = jnp.dot(jnp.concatenate(parts, axis=0), w_ref[...], preferred_element_type=F32)
    mid_ref[...] = (mesh_ref[...].astype(F32) + silu(grown)).astype(BF16)


def update(slots, mesh_in, w_enc):
    vmem = pl.BlockSpec(memory_space=pltpu.VMEM)
    return pl.pallas_call(
        update_kernel,
        in_specs=[vmem] * (SLOTS + 2),
        out_specs=[vmem] * 2,
        out_shape=[
            jax.ShapeDtypeStruct(mesh_in.shape, BF16),
            jax.ShapeDtypeStruct((8, mesh_in.shape[1]), F32),
        ],
        compiler_params=pltpu.CompilerParams(vmem_limit_bytes=8 * MIB),
        name="mesh_update",
    )(*slots, mesh_in, w_enc)


def process_kernel(
    ids_ref, mid_ref, near_mid_ref, far_mid_ref, near_ref, part_ref, gain_ref, w_ref, out_ref, *sends
):
    count, latent = mid_ref.shape
    block_mesh = sends[0].shape[0]
    around = jnp.concatenate([near_mid_ref[...], far_mid_ref[...]], axis=0)
    message = part_ref[...] + jnp.dot(near_ref[...], around, preferred_element_type=F32)
    power = jnp.mean(message * message, axis=-1, keepdims=True)
    normed = (message * lax.rsqrt(power + 1e-05) * gain_ref[...]).astype(BF16)
    grown = jnp.dot(normed, w_ref[...], preferred_element_type=F32)
    grown = mid_ref[...].astype(F32) + silu(grown)
    out_ref[...] = grown.astype(BF16)
    for s in range(SLOTS):
        chosen = grown[:block_mesh, :]
        for b in range(1, count // block_mesh):
            block = grown[b * block_mesh : (b + 1) * block_mesh, :]
            chosen = jnp.where(ids_ref[s : s + 1, :] == b, block, chosen)
        sends[s][...] = chosen.astype(BF16)


def process(block_mesh, ids, mid, near_mid, far_mid, near, part, gain, w_proc):
    vmem = pl.BlockSpec(memory_space=pltpu.VMEM)
    latent = mid.shape[1]
    return pl.pallas_call(
        process_kernel,
        in_specs=[vmem] * 8,
        out_specs=[vmem] * (1 + SLOTS),
        out_shape=[jax.ShapeDtypeStruct(mid.shape, BF16)]
        + [jax.ShapeDtypeStruct((block_mesh, latent), BF16)] * SLOTS,
        compiler_params=pltpu.CompilerParams(vmem_limit_bytes=8 * MIB),
        name="mesh_process",
    )(ids, mid, near_mid, far_mid, near, part, gain, w_proc)


def decode_kernel(width, grid_ref, lat_ref, dsum_ref, w_ref, *rest):
    slots = rest[:SLOTS]
    out_hbm, back_ref, pred_ref, hold_ref, sems = rest[SLOTS:]
    steps = grid_ref.shape[1] // width

    def copy_out(step):
        cols = pl.ds(step * width, width)
        return pltpu.make_async_copy(pred_ref.at[:, cols], out_hbm.at[:, cols], sems.at[step])

    joined = jnp.concatenate([slot[...] for slot in slots], axis=0)
    back_ref[...] = (BF16(0.5) * joined).T

    def predict(step, slot):
        cols = pl.ds(step * width, width)
        pred_ref[:, cols] = (
            grid_ref[:, cols].astype(F32)
            + jnp.dot(w_ref[...], hold_ref[slot], preferred_element_type=F32)
        ).astype(BF16)

    for step in range(steps):
        slot = step % 2
        if step > 0:
            predict(step - 1, 1 - slot)
            copy_out(step - 1).start()
        for half in range(0, width, 256):
            part = pl.ds(step * width + half, 256)
            decoded = jnp.dot(back_ref[...], dsum_ref[:, part], preferred_element_type=F32)
            halved = BF16(0.5) * lat_ref[:, part] + decoded.astype(BF16)
            hold_ref[slot, :, half : half + 256] = silu_of_half(halved)
    predict(steps - 1, (steps - 1) % 2)
    copy_out(steps - 1).start()
    for step in range(steps):
        copy_out(step).wait()


def decode(grid_t, lat_t, dsum, w_out_t, slots):
    channels, points = grid_t.shape
    latent = lat_t.shape[0]
    rows = dsum.shape[0]
    width = 512
    vmem = pl.BlockSpec(memory_space=pltpu.VMEM)
    return pl.pallas_call(
        functools.partial(decode_kernel, width),
        in_specs=[vmem] * (4 + SLOTS),
        out_specs=pl.BlockSpec(memory_space=pl.ANY),
        out_shape=jax.ShapeDtypeStruct((channels, points), BF16),
        scratch_shapes=[
            pltpu.VMEM((latent, rows), BF16),
            pltpu.VMEM((channels, points), BF16),
            pltpu.VMEM((2, latent, width), BF16),
            pltpu.SemaphoreType.DMA((points // width,)),
        ],
        compiler_params=pltpu.CompilerParams(vmem_limit_bytes=24 * MIB),
        name="decode",
    )(grid_t, lat_t, dsum, w_out_t, *slots)


def local(
    grid_in, w_embed, enc_coef, enc_owner, slot_block, mesh_in, w_enc,
    proc_adj, proc_coef, proc_gain, w_proc, dec_coef, w_out,
):
    parts = lax.axis_size("nodes")
    block_mesh = enc_coef.shape[1]

    def swap(x, slot):
        pairs = [(i, partner(slot, i, parts)) for i in range(parts)]
        return lax.ppermute(x, "nodes", pairs)

    def swap_all(xs):
        return [xs[OWN]] + [swap(xs[s], s) for s in range(1, SLOTS)]

    lat_t, dsum, grid_t, *sums = encode(
        parts, slot_block, enc_owner.reshape(-1, 128), grid_in.T, w_embed, enc_coef,
        jnp.swapaxes(dec_coef, 1, 2),
    )
    received = swap_all(sums)
    mid, ids = update(received, mesh_in, w_enc)
    far_mid = swap(mid, FAR)
    near_mid = swap(mid, NEAR)
    near, part = prepare(parts, proc_adj, proc_coef, mid)
    mesh_out, *sends = process(
        block_mesh, ids, mid, near_mid, far_mid, near, part, proc_gain.reshape(1, -1), w_proc
    )
    returned = swap_all(sends)
    pred_t = decode(grid_t, lat_t, dsum, w_out.T, returned)
    return (pred_t.T, mesh_out)


def solution(mesh):
    return jax.shard_map(
        local,
        mesh=mesh,
        in_specs=(
            P(("groups", "nodes"), None),
            P(),
            P("nodes", None, None),
            P("nodes"),
            P("nodes"),
            P(("groups", "nodes"), None),
            P(),
            P("nodes", None),
            P("nodes", None, None, None),
            P(),
            P(),
            P("nodes", None, None),
            P(),
        ),
        out_specs=(P(("groups", "nodes"), None), P(("groups", "nodes"), None)),
        check_vma=False,
    )
```

```python
import functools

import jax
import jax.numpy as jnp
from jax import lax
from jax.experimental import pallas as pl
from jax.experimental.pallas import tpu as pltpu
from jax.sharding import PartitionSpec as P

F32 = jnp.float32
BF16 = jnp.bfloat16
MIB = 1 << 20
OWN, ODD, HALF, FAR, EVEN, NEAR = range(6)
SLOTS = 6
PAD = 128
AHEAD = 3


def partner(slot, me, parts):
    chip = me // 2 % 2
    core = me % 2
    step = {
        OWN: 0,
        HALF: parts // 2,
        ODD: 4 * chip - 2,
        EVEN: 2 - 4 * chip,
        FAR: 2 * core - 1,
        NEAR: 1 - 2 * core,
    }[slot]
    return (me + step + parts) % parts


def scalar_partner(slot, me, parts):
    chip = lax.rem(lax.div(me, 2), 2)
    core = lax.rem(me, 2)
    step = {
        OWN: 0,
        HALF: parts // 2,
        ODD: 4 * chip - 2,
        EVEN: 2 - 4 * chip,
        FAR: 2 * core - 1,
        NEAR: 1 - 2 * core,
    }[slot]
    return lax.rem(me + step + parts, parts)


def silu_of_half(half):
    return half + half * jnp.tanh(half)


def silu(x):
    return silu_of_half(0.5 * x)


def hot_rows(ids, target):
    lanes = ids.shape[1]
    target = target.astype(BF16)
    one, zero = jnp.ones((), BF16), jnp.zeros((), BF16)
    return jnp.concatenate(
        [
            jnp.where(ids == target[:, at : at + lanes], one, zero)
            for at in range(0, target.shape[1], lanes)
        ],
        axis=1,
    )


def spreads(per_block, block_mesh, groups, lanes, wide):
    out = []
    for r in range(groups):
        row = lax.broadcasted_iota(jnp.int32, (lanes, wide), 0) + r * lanes
        col = lax.broadcasted_iota(jnp.int32, (lanes, wide), 1)
        place = row - per_block * ((row * (2**19 // per_block + 1)) >> 19)
        out.append(jnp.where(place == col // block_mesh, 1.0, 0.0).astype(BF16))
    return out


def fill_targets(parts, per_block, block_mesh, spread_ref, owner_ref, tgt_ref):
    me = lax.axis_index("nodes")
    chip = lax.rem(lax.div(me, 2), 2)
    core = lax.rem(me, 2)
    up2 = EVEN + (ODD - EVEN) * chip
    up1 = NEAR + (FAR - NEAR) * core
    off = owner_ref[...] - me
    off = jnp.where(off < 0, off + parts, off)
    slot = jnp.where(off == parts // 2, HALF, OWN)
    slot = jnp.where(off == 2, up2, slot)
    slot = jnp.where(off == parts - 2, ODD + EVEN - up2, slot)
    slot = jnp.where(off == 1, up1, slot)
    slot = jnp.where(off == parts - 1, NEAR + FAR - up1, slot)
    slot = slot.astype(F32)
    groups, lanes = owner_ref.shape
    all_blocks = tgt_ref.shape[0]
    total = jnp.zeros(tgt_ref.shape, F32)
    for r in range(groups):
        tile = lax.broadcasted_iota(jnp.int32, (all_blocks, lanes), 1) + r * lanes
        first = lax.broadcasted_iota(jnp.int32, (all_blocks, lanes), 0) * per_block
        mine = (tile >= first) & (tile < first + per_block)
        picked = jnp.where(mine, slot[r : r + 1, :], 0.0).astype(BF16)
        total += jnp.dot(picked, spread_ref[r], preferred_element_type=F32)
    col = lax.broadcasted_iota(jnp.int32, tgt_ref.shape, 1)
    tgt_ref[...] = total * block_mesh + (col % block_mesh).astype(F32)


def encode_kernel(
    parts, width, slot_hbm, owner_hbm, w_hbm, grid_hbm, enc_hbm,
    lat_ref, tgt_ref, grid_ref, *rest,
):
    send_refs = rest[:SLOTS]
    (
        slot_ref, owner_ref, w_ref, enc_ref, wt_ref, ids_ref, msum_ref,
        acc_ref, spread_ref, small_sems, sems,
    ) = rest[SLOTS:]
    tiles, block_mesh, block_grid = enc_ref.shape
    channels, points = grid_ref.shape
    latent = w_ref.shape[1]
    per_block = tiles * block_grid // points
    blocks = width // block_grid
    chunk = blocks * per_block
    steps = points // width
    wide = per_block * block_mesh
    rows = SLOTS * block_mesh

    def copies(step):
        cols = pl.ds(step * width, width)
        some = pl.ds(step * chunk, chunk)
        return (
            pltpu.make_async_copy(grid_hbm.at[:, cols], grid_ref.at[:, cols], sems.at[0, step]),
            pltpu.make_async_copy(enc_hbm.at[some], enc_ref.at[some], sems.at[1, step]),
        )

    small = [
        pltpu.make_async_copy(source, target, small_sems.at[i])
        for i, (source, target) in enumerate(
            ((owner_hbm, owner_ref), (w_hbm, w_ref), (slot_hbm, slot_ref))
        )
    ]
    for copy in small:
        copy.start()
    def start(step):
        for copy in copies(step):
            copy.start()

    start(0)
    ids_ref[...] = lax.broadcasted_iota(jnp.int32, ids_ref.shape, 0).astype(BF16)
    acc_ref[...] = jnp.zeros_like(acc_ref)
    for r, spread in enumerate(spreads(per_block, block_mesh, *owner_ref.shape, wide)):
        spread_ref[r] = spread
    for copy in small:
        copy.wait()
    for step in range(1, AHEAD):
        start(step)
    wt_ref[:, :channels] = (0.5 * w_ref[...].astype(F32)).T.astype(BF16)
    fill_targets(parts, per_block, block_mesh, spread_ref, owner_ref, tgt_ref)

    def collect(step):
        lat = lat_ref[:, step * width : (step + 1) * width]
        acc_ref[...] += lax.dot_general(
            msum_ref[step % 2], lat, (((1,), (1,)), ((), ())), preferred_element_type=F32
        )

    for step in range(steps):
        slot = step % 2
        if step + AHEAD < steps:
            start(step + AHEAD)
        for copy in copies(step):
            copy.wait()
        if step > 0:
            collect(step - 1)
        for b in range(blocks):
            hot = hot_rows(ids_ref[...], tgt_ref[pl.ds(step * blocks + b, 1), :])
            some = pl.ds(step * chunk + b * per_block, per_block)
            tiles_of = enc_ref[some].reshape(wide, block_grid)
            sums = jnp.dot(hot, tiles_of, preferred_element_type=F32).astype(BF16)
            msum_ref[slot, :, b * block_grid : (b + 1) * block_grid] = sums
        for half in range(0, width, 256):
            part = pl.ds(step * width + half, 256)
            lat = silu_of_half(
                jnp.dot(
                    wt_ref[:, :channels], grid_ref[:, part], preferred_element_type=F32
                )
            ).astype(BF16)
            lat_ref[:, part] = lat

    collect(steps - 1)
    me = lax.axis_index("nodes")
    summed = acc_ref[...].astype(BF16)
    for s in range(SLOTS):
        send_refs[s][:, :latent] = summed[s * block_mesh : (s + 1) * block_mesh, :]
        block = slot_ref[scalar_partner(s, me, parts)].astype(F32)
        send_refs[s][:, latent:] = jnp.full((block_mesh, PAD), block, F32).astype(BF16)


def encode(parts, slot_block, owners, grid_t, w_embed, enc_coef):
    channels, points = grid_t.shape
    latent = w_embed.shape[1]
    tiles, block_mesh, block_grid = enc_coef.shape
    grid_blocks = points // block_grid
    width = 512
    steps = points // width
    rows = SLOTS * block_mesh
    wide = tiles // grid_blocks * block_mesh
    vmem = pl.BlockSpec(memory_space=pltpu.VMEM)
    hbm = pl.BlockSpec(memory_space=pl.ANY)
    return pl.pallas_call(
        functools.partial(encode_kernel, parts, width),
        in_specs=[hbm] * 5,
        out_specs=[vmem] * (3 + SLOTS),
        out_shape=[
            pltpu.VMEM((latent, points), BF16),
            pltpu.VMEM((grid_blocks, wide), F32),
            pltpu.VMEM((channels, points), BF16),
        ]
        + [jax.ShapeDtypeStruct((block_mesh, latent + PAD), BF16)] * SLOTS,
        scratch_shapes=[
            pltpu.SMEM(slot_block.shape, jnp.int32),
            pltpu.VMEM(owners.shape, jnp.int32),
            pltpu.VMEM(w_embed.shape, BF16),
            pltpu.VMEM(enc_coef.shape, BF16),
            pltpu.VMEM((latent, 256), BF16),
            pltpu.VMEM((rows, 128), BF16),
            pltpu.VMEM((2, rows, width), BF16),
            pltpu.VMEM((rows, latent), F32),
            pltpu.VMEM((*owners.shape, wide), BF16),
            pltpu.SemaphoreType.DMA((3,)),
            pltpu.SemaphoreType.DMA((2, steps)),
        ],
        compiler_params=pltpu.CompilerParams(vmem_limit_bytes=24 * MIB),
        name="encode",
    )(
        *(
            pltpu.with_memory_space_constraint(x, pltpu.HBM)
            for x in (slot_block, owners, w_embed, grid_t, enc_coef)
        )
    )


def decoder_sums_kernel(tgt_ref, dec_hbm, dsum_ref, done_ref, dec_ref, ids_ref, sems):
    tiles, block_mesh, block_grid = dec_ref.shape
    grid_blocks, wide = tgt_ref.shape
    per_block = tiles // grid_blocks
    steps = sems.shape[0]
    chunk = tiles // steps
    blocks = grid_blocks // steps

    def copy(step):
        some = pl.ds(step * chunk, chunk)
        return pltpu.make_async_copy(dec_hbm.at[some], dec_ref.at[some], sems.at[step])

    for step in range(steps):
        copy(step).start()
    ids_ref[...] = lax.broadcasted_iota(jnp.int32, ids_ref.shape, 0).astype(BF16)
    for step in range(steps):
        copy(step).wait()
        for g in range(step * blocks, (step + 1) * blocks):
            hot = hot_rows(ids_ref[...], tgt_ref[g : g + 1, :])
            some = pl.ds(g * per_block, per_block)
            sums = jnp.dot(
                hot, dec_ref[some].reshape(wide, block_grid), preferred_element_type=F32
            )
            dsum_ref[:, g * block_grid : (g + 1) * block_grid] = sums.astype(BF16)
    done_ref[...] = jnp.zeros_like(done_ref)


def decoder_sums(tgt, dec_t):
    tiles, block_mesh, block_grid = dec_t.shape
    grid_blocks, wide = tgt.shape
    rows = SLOTS * block_mesh
    steps = 8
    vmem = pl.BlockSpec(memory_space=pltpu.VMEM)
    return pl.pallas_call(
        decoder_sums_kernel,
        in_specs=[vmem, pl.BlockSpec(memory_space=pl.ANY)],
        out_specs=[vmem] * 2,
        out_shape=[
            pltpu.VMEM((rows, grid_blocks * block_grid), BF16),
            jax.ShapeDtypeStruct((8, 128), F32),
        ],
        scratch_shapes=[
            pltpu.VMEM(dec_t.shape, BF16),
            pltpu.VMEM((rows, 128), BF16),
            pltpu.SemaphoreType.DMA((steps,)),
        ],
        compiler_params=pltpu.CompilerParams(vmem_limit_bytes=16 * MIB),
        cost_estimate=pl.CostEstimate(
            flops=2 * rows * wide * block_grid * grid_blocks,
            bytes_accessed=2 * (dec_t.size + rows * grid_blocks * block_grid),
            transcendentals=0,
        ),
        name="decoder_sums",
    )(tgt, pltpu.with_memory_space_constraint(dec_t, pltpu.HBM))


def prepare_kernel(parts, adj_ref, coef_ref, mid_ref, near_ref, part_ref, all_ref):
    mesh_blocks, adj_width = adj_ref.shape
    block_mesh = coef_ref.shape[2]
    me = lax.axis_index("nodes")
    core = lax.rem(me, 2)
    count = mid_ref.shape[0]
    columns = all_ref.shape[1]
    row = lax.broadcasted_iota(jnp.int32, (block_mesh, columns), 0)
    col = lax.broadcasted_iota(jnp.int32, (block_mesh, columns), 1)
    for b in range(mesh_blocks):
        total = jnp.zeros((block_mesh, columns), F32)
        for a in range(adj_width):
            which = adj_ref[b, a]
            listed = jnp.maximum(which, 0)
            side = lax.rem(lax.div(listed, mesh_blocks) - me + 1 + parts, parts)
            side = jnp.where(side == 1, 2, jnp.where((side == 2) == (core == 0), 0, 1))
            place = side * mesh_blocks + lax.rem(listed, mesh_blocks)
            place = jnp.where(which >= 0, place, -columns)
            spot = jnp.where(col == place * block_mesh + row, 1.0, 0.0).astype(BF16)
            total += jnp.dot(coef_ref[b, a], spot, preferred_element_type=F32)
        all_ref[b * block_mesh : (b + 1) * block_mesh, :] = total.astype(BF16)
    near_ref[...] = all_ref[:, : 2 * count]
    part_ref[...] = jnp.dot(
        all_ref[:, 2 * count :], mid_ref[...], preferred_element_type=F32
    )


def prepare(parts, adj, coef, mid):
    mesh_blocks, adj_width, block_mesh, _ = coef.shape
    count = mesh_blocks * block_mesh
    vmem = pl.BlockSpec(memory_space=pltpu.VMEM)
    return pl.pallas_call(
        functools.partial(prepare_kernel, parts),
        in_specs=[pl.BlockSpec(memory_space=pltpu.SMEM), vmem, vmem],
        out_specs=[vmem] * 2,
        out_shape=[
            jax.ShapeDtypeStruct((count, 2 * count), BF16),
            jax.ShapeDtypeStruct(mid.shape, F32),
        ],
        scratch_shapes=[pltpu.VMEM((count, 3 * count), BF16)],
        compiler_params=pltpu.CompilerParams(vmem_limit_bytes=8 * MIB),
        cost_estimate=pl.CostEstimate(
            flops=2 * adj_width * count * block_mesh * 3 * count,
            bytes_accessed=8 * count * 3 * count,
            transcendentals=0,
        ),
        name="prepare",
    )(adj, coef, mid)


def update_kernel(*refs):
    slots = refs[:SLOTS]
    mesh_ref, w_ref, after_ref, mid_ref, ids_ref = refs[SLOTS:]
    count, latent = mesh_ref.shape
    block_mesh = slots[0].shape[0]
    sums = [slot[:, :latent].astype(F32) for slot in slots]
    ids = [slot[:, latent:].astype(F32)[:1, :1] for slot in slots]
    for s in range(SLOTS):
        ids_ref[s : s + 1, :] = jnp.broadcast_to(ids[s], (1, latent))
    parts = []
    for b in range(count // block_mesh):
        total = jnp.zeros((block_mesh, latent), F32)
        for s in range(SLOTS):
            total += jnp.where(ids[s] == b, sums[s], 0.0)
        parts.append(total.astype(BF16))
    grown = jnp.dot(jnp.concatenate(parts, axis=0), w_ref[...], preferred_element_type=F32)
    mid_ref[...] = (mesh_ref[...].astype(F32) + silu(grown)).astype(BF16)


def update(slots, mesh_in, w_enc, after):
    vmem = pl.BlockSpec(memory_space=pltpu.VMEM)
    return pl.pallas_call(
        update_kernel,
        in_specs=[vmem] * (SLOTS + 3),
        out_specs=[vmem] * 2,
        out_shape=[
            jax.ShapeDtypeStruct(mesh_in.shape, BF16),
            jax.ShapeDtypeStruct((8, mesh_in.shape[1]), F32),
        ],
        compiler_params=pltpu.CompilerParams(vmem_limit_bytes=8 * MIB),
        name="mesh_update",
    )(*slots, mesh_in, w_enc, after)


def process_kernel(
    ids_ref, mid_ref, near_mid_ref, far_mid_ref, near_ref, part_ref, gain_ref, w_ref, out_ref, *sends
):
    count, latent = mid_ref.shape
    block_mesh = sends[0].shape[0]
    around = jnp.concatenate([near_mid_ref[...], far_mid_ref[...]], axis=0)
    message = part_ref[...] + jnp.dot(near_ref[...], around, preferred_element_type=F32)
    power = jnp.mean(message * message, axis=-1, keepdims=True)
    normed = (message * lax.rsqrt(power + 1e-05) * gain_ref[...]).astype(BF16)
    grown = jnp.dot(normed, w_ref[...], preferred_element_type=F32)
    grown = mid_ref[...].astype(F32) + silu(grown)
    out_ref[...] = grown.astype(BF16)
    for s in range(SLOTS):
        chosen = grown[:block_mesh, :]
        for b in range(1, count // block_mesh):
            block = grown[b * block_mesh : (b + 1) * block_mesh, :]
            chosen = jnp.where(ids_ref[s : s + 1, :] == b, block, chosen)
        sends[s][...] = chosen.astype(BF16)


def process(block_mesh, ids, mid, near_mid, far_mid, near, part, gain, w_proc):
    vmem = pl.BlockSpec(memory_space=pltpu.VMEM)
    latent = mid.shape[1]
    return pl.pallas_call(
        process_kernel,
        in_specs=[vmem] * 8,
        out_specs=[vmem] * (1 + SLOTS),
        out_shape=[jax.ShapeDtypeStruct(mid.shape, BF16)]
        + [jax.ShapeDtypeStruct((block_mesh, latent), BF16)] * SLOTS,
        compiler_params=pltpu.CompilerParams(vmem_limit_bytes=8 * MIB),
        name="mesh_process",
    )(ids, mid, near_mid, far_mid, near, part, gain, w_proc)


def decode_kernel(width, grid_ref, lat_ref, dsum_ref, w_ref, *rest):
    slots = rest[:SLOTS]
    out_hbm, back_ref, pred_ref, hold_ref, sems = rest[SLOTS:]
    steps = grid_ref.shape[1] // width

    def copy_out(step):
        cols = pl.ds(step * width, width)
        return pltpu.make_async_copy(pred_ref.at[:, cols], out_hbm.at[:, cols], sems.at[step])

    joined = jnp.concatenate([slot[...] for slot in slots], axis=0)
    back_ref[...] = (BF16(0.5) * joined).T

    def predict(step, slot):
        cols = pl.ds(step * width, width)
        pred_ref[:, cols] = (
            grid_ref[:, cols].astype(F32)
            + jnp.dot(w_ref[...], hold_ref[slot], preferred_element_type=F32)
        ).astype(BF16)

    for step in range(steps):
        slot = step % 2
        if step > 0:
            predict(step - 1, 1 - slot)
            copy_out(step - 1).start()
        for half in range(0, width, 256):
            part = pl.ds(step * width + half, 256)
            decoded = jnp.dot(back_ref[...], dsum_ref[:, part], preferred_element_type=F32)
            halved = BF16(0.5) * lat_ref[:, part] + decoded.astype(BF16)
            hold_ref[slot, :, half : half + 256] = silu_of_half(halved)
    predict(steps - 1, (steps - 1) % 2)
    copy_out(steps - 1).start()
    for step in range(steps):
        copy_out(step).wait()


def decode(grid_t, lat_t, dsum, w_out_t, slots):
    channels, points = grid_t.shape
    latent = lat_t.shape[0]
    rows = dsum.shape[0]
    width = 512
    vmem = pl.BlockSpec(memory_space=pltpu.VMEM)
    return pl.pallas_call(
        functools.partial(decode_kernel, width),
        in_specs=[vmem] * (4 + SLOTS),
        out_specs=pl.BlockSpec(memory_space=pl.ANY),
        out_shape=jax.ShapeDtypeStruct((channels, points), BF16),
        scratch_shapes=[
            pltpu.VMEM((latent, rows), BF16),
            pltpu.VMEM((channels, points), BF16),
            pltpu.VMEM((2, latent, width), BF16),
            pltpu.SemaphoreType.DMA((points // width,)),
        ],
        compiler_params=pltpu.CompilerParams(vmem_limit_bytes=24 * MIB),
        name="decode",
    )(grid_t, lat_t, dsum, w_out_t, *slots)


def local(
    grid_in, w_embed, enc_coef, enc_owner, slot_block, mesh_in, w_enc,
    proc_adj, proc_coef, proc_gain, w_proc, dec_coef, w_out,
):
    parts = lax.axis_size("nodes")
    block_mesh = enc_coef.shape[1]

    def swap(x, slot):
        pairs = [(i, partner(slot, i, parts)) for i in range(parts)]
        return lax.ppermute(x, "nodes", pairs)

    def swap_all(xs):
        return [xs[OWN]] + [swap(xs[s], s) for s in range(1, SLOTS)]

    lat_t, tgt, grid_t, *sums = encode(
        parts, slot_block, enc_owner.reshape(-1, 128), grid_in.T, w_embed, enc_coef
    )
    received = swap_all(sums)
    dsum, after = decoder_sums(tgt, jnp.swapaxes(dec_coef, 1, 2))
    mid, ids = update(received, mesh_in, w_enc, after)
    far_mid = swap(mid, FAR)
    near_mid = swap(mid, NEAR)
    near, part = prepare(parts, proc_adj, proc_coef, mid)
    mesh_out, *sends = process(
        block_mesh, ids, mid, near_mid, far_mid, near, part, proc_gain.reshape(1, -1), w_proc
    )
    returned = swap_all(sends)
    pred_t = decode(grid_t, lat_t, dsum, w_out.T, returned)
    return (pred_t.T, mesh_out)


def solution(mesh):
    return jax.shard_map(
        local,
        mesh=mesh,
        in_specs=(
            P(("groups", "nodes"), None),
            P(),
            P("nodes", None, None),
            P("nodes"),
            P("nodes"),
            P(("groups", "nodes"), None),
            P(),
            P("nodes", None),
            P("nodes", None, None, None),
            P(),
            P(),
            P("nodes", None, None),
            P(),
        ),
        out_specs=(P(("groups", "nodes"), None), P(("groups", "nodes"), None)),
        check_vma=False,
    )
```

```python
import functools

import jax
import jax.numpy as jnp
from jax import lax
from jax.experimental import pallas as pl
from jax.experimental.pallas import tpu as pltpu
from jax.sharding import PartitionSpec as P

F32 = jnp.float32
BF16 = jnp.bfloat16
MIB = 1 << 20
OWN, ODD, HALF, FAR, EVEN, NEAR = range(6)
SLOTS = 6
PAD = 128
AHEAD = 3


def partner(slot, me, parts):
    chip = me // 2 % 2
    core = me % 2
    step = {
        OWN: 0,
        HALF: parts // 2,
        ODD: 4 * chip - 2,
        EVEN: 2 - 4 * chip,
        FAR: 2 * core - 1,
        NEAR: 1 - 2 * core,
    }[slot]
    return (me + step + parts) % parts


def scalar_partner(slot, me, parts):
    chip = lax.rem(lax.div(me, 2), 2)
    core = lax.rem(me, 2)
    step = {
        OWN: 0,
        HALF: parts // 2,
        ODD: 4 * chip - 2,
        EVEN: 2 - 4 * chip,
        FAR: 2 * core - 1,
        NEAR: 1 - 2 * core,
    }[slot]
    return lax.rem(me + step + parts, parts)


def silu_of_half(half):
    return half + half * jnp.tanh(half)


def silu(x):
    return silu_of_half(0.5 * x)


def hot_rows(ids, target):
    lanes = ids.shape[1]
    target = target.astype(BF16)
    one, zero = jnp.ones((), BF16), jnp.zeros((), BF16)
    return jnp.concatenate(
        [
            jnp.where(ids == target[:, at : at + lanes], one, zero)
            for at in range(0, target.shape[1], lanes)
        ],
        axis=1,
    )


def spreads(per_block, block_mesh, groups, lanes, wide):
    out = []
    for r in range(groups):
        row = lax.broadcasted_iota(jnp.int32, (lanes, wide), 0) + r * lanes
        col = lax.broadcasted_iota(jnp.int32, (lanes, wide), 1)
        place = row - per_block * ((row * (2**19 // per_block + 1)) >> 19)
        out.append(jnp.where(place == col // block_mesh, 1.0, 0.0).astype(BF16))
    return out


def fill_targets(parts, per_block, block_mesh, spread_ref, owner_ref, tgt_ref):
    me = lax.axis_index("nodes")
    chip = lax.rem(lax.div(me, 2), 2)
    core = lax.rem(me, 2)
    up2 = EVEN + (ODD - EVEN) * chip
    up1 = NEAR + (FAR - NEAR) * core
    off = owner_ref[...] - me
    off = jnp.where(off < 0, off + parts, off)
    slot = jnp.where(off == parts // 2, HALF, OWN)
    slot = jnp.where(off == 2, up2, slot)
    slot = jnp.where(off == parts - 2, ODD + EVEN - up2, slot)
    slot = jnp.where(off == 1, up1, slot)
    slot = jnp.where(off == parts - 1, NEAR + FAR - up1, slot)
    slot = slot.astype(F32)
    groups, lanes = owner_ref.shape
    all_blocks = tgt_ref.shape[0]
    total = jnp.zeros(tgt_ref.shape, F32)
    for r in range(groups):
        tile = lax.broadcasted_iota(jnp.int32, (all_blocks, lanes), 1) + r * lanes
        first = lax.broadcasted_iota(jnp.int32, (all_blocks, lanes), 0) * per_block
        mine = (tile >= first) & (tile < first + per_block)
        picked = jnp.where(mine, slot[r : r + 1, :], 0.0).astype(BF16)
        total += jnp.dot(picked, spread_ref[r], preferred_element_type=F32)
    col = lax.broadcasted_iota(jnp.int32, tgt_ref.shape, 1)
    tgt_ref[...] = total * block_mesh + (col % block_mesh).astype(F32)


def encode_kernel(
    parts, width, slot_hbm, owner_hbm, w_hbm, grid_hbm, enc_hbm, dec_hbm,
    lat_ref, dsum_ref, grid_ref, *rest,
):
    send_refs = rest[:SLOTS]
    (
        slot_ref, owner_ref, w_ref, enc_ref, dec_ref, wt_ref, tgt_ref, ids_ref, msum_ref,
        acc_ref, spread_ref, small_sems, sems,
    ) = rest[SLOTS:]
    tiles, block_mesh, block_grid = enc_ref.shape
    channels, points = grid_ref.shape
    latent = w_ref.shape[1]
    per_block = tiles * block_grid // points
    blocks = width // block_grid
    chunk = blocks * per_block
    steps = points // width
    wide = per_block * block_mesh
    rows = SLOTS * block_mesh

    def copies(step):
        cols = pl.ds(step * width, width)
        some = pl.ds(step * chunk, chunk)
        return (
            pltpu.make_async_copy(grid_hbm.at[:, cols], grid_ref.at[:, cols], sems.at[0, step]),
            pltpu.make_async_copy(enc_hbm.at[some], enc_ref.at[some], sems.at[1, step]),
            pltpu.make_async_copy(dec_hbm.at[some], dec_ref.at[some], sems.at[2, step]),
        )

    small = [
        pltpu.make_async_copy(source, target, small_sems.at[i])
        for i, (source, target) in enumerate(
            ((owner_hbm, owner_ref), (w_hbm, w_ref), (slot_hbm, slot_ref))
        )
    ]
    for copy in small:
        copy.start()
    def start(step):
        for copy in copies(step):
            copy.start()

    start(0)
    ids_ref[...] = lax.broadcasted_iota(jnp.int32, ids_ref.shape, 0).astype(BF16)
    acc_ref[...] = jnp.zeros_like(acc_ref)
    for r, spread in enumerate(spreads(per_block, block_mesh, *owner_ref.shape, wide)):
        spread_ref[r] = spread
    for copy in small:
        copy.wait()
    for step in range(1, AHEAD):
        start(step)
    wt_ref[:, :channels] = (0.5 * w_ref[...].astype(F32)).T.astype(BF16)
    fill_targets(parts, per_block, block_mesh, spread_ref, owner_ref, tgt_ref)

    def collect(step):
        lat = lat_ref[:, step * width : (step + 1) * width]
        acc_ref[...] += lax.dot_general(
            msum_ref[step % 2], lat, (((1,), (1,)), ((), ())), preferred_element_type=F32
        )

    for step in range(steps):
        slot = step % 2
        if step + AHEAD < steps:
            start(step + AHEAD)
        for copy in copies(step):
            copy.wait()
        if step > 0:
            collect(step - 1)
        for b in range(blocks):
            hot = hot_rows(ids_ref[...], tgt_ref[pl.ds(step * blocks + b, 1), :])
            some = pl.ds(step * chunk + b * per_block, per_block)
            both = jnp.concatenate(
                [
                    enc_ref[some].reshape(wide, block_grid),
                    dec_ref[some].reshape(wide, block_grid),
                ],
                axis=1,
            )
            sums = jnp.dot(hot, both, preferred_element_type=F32).astype(BF16)
            msum_ref[slot, :, b * block_grid : (b + 1) * block_grid] = sums[:, :block_grid]
            first = (step * blocks + b) * block_grid
            dsum_ref[:, pl.ds(first, block_grid)] = sums[:, block_grid:]
        for half in range(0, width, 256):
            part = pl.ds(step * width + half, 256)
            lat = silu_of_half(
                jnp.dot(
                    wt_ref[:, :channels], grid_ref[:, part], preferred_element_type=F32
                )
            ).astype(BF16)
            lat_ref[:, part] = lat

    collect(steps - 1)
    me = lax.axis_index("nodes")
    summed = acc_ref[...].astype(BF16)
    for s in range(SLOTS):
        send_refs[s][:, :latent] = summed[s * block_mesh : (s + 1) * block_mesh, :]
        block = slot_ref[scalar_partner(s, me, parts)].astype(F32)
        send_refs[s][:, latent:] = jnp.full((block_mesh, PAD), block, F32).astype(BF16)


def encode(parts, slot_block, owners, grid_t, w_embed, enc_coef, dec_t):
    channels, points = grid_t.shape
    latent = w_embed.shape[1]
    tiles, block_mesh, block_grid = enc_coef.shape
    grid_blocks = points // block_grid
    width = 1024
    steps = points // width
    rows = SLOTS * block_mesh
    wide = tiles // grid_blocks * block_mesh
    vmem = pl.BlockSpec(memory_space=pltpu.VMEM)
    hbm = pl.BlockSpec(memory_space=pl.ANY)
    return pl.pallas_call(
        functools.partial(encode_kernel, parts, width),
        in_specs=[hbm] * 6,
        out_specs=[vmem] * (3 + SLOTS),
        out_shape=[
            pltpu.VMEM((latent, points), BF16),
            pltpu.VMEM((rows, points), BF16),
            pltpu.VMEM((channels, points), BF16),
        ]
        + [jax.ShapeDtypeStruct((block_mesh, latent + PAD), BF16)] * SLOTS,
        scratch_shapes=[
            pltpu.SMEM(slot_block.shape, jnp.int32),
            pltpu.VMEM(owners.shape, jnp.int32),
            pltpu.VMEM(w_embed.shape, BF16),
            pltpu.VMEM(enc_coef.shape, BF16),
            pltpu.VMEM(dec_t.shape, BF16),
            pltpu.VMEM((latent, 256), BF16),
            pltpu.VMEM((grid_blocks, wide), F32),
            pltpu.VMEM((rows, 128), BF16),
            pltpu.VMEM((2, rows, width), BF16),
            pltpu.VMEM((rows, latent), F32),
            pltpu.VMEM((*owners.shape, wide), BF16),
            pltpu.SemaphoreType.DMA((3,)),
            pltpu.SemaphoreType.DMA((3, steps)),
        ],
        compiler_params=pltpu.CompilerParams(vmem_limit_bytes=24 * MIB),
        name="encode",
    )(
        *(
            pltpu.with_memory_space_constraint(x, pltpu.HBM)
            for x in (slot_block, owners, w_embed, grid_t, enc_coef, dec_t)
        )
    )


def prepare_kernel(parts, adj_ref, coef_ref, mid_ref, near_ref, part_ref, all_ref):
    mesh_blocks, adj_width = adj_ref.shape
    block_mesh = coef_ref.shape[2]
    me = lax.axis_index("nodes")
    core = lax.rem(me, 2)
    count = mid_ref.shape[0]
    columns = all_ref.shape[1]
    row = lax.broadcasted_iota(jnp.int32, (block_mesh, columns), 0)
    col = lax.broadcasted_iota(jnp.int32, (block_mesh, columns), 1)
    for b in range(mesh_blocks):
        total = jnp.zeros((block_mesh, columns), F32)
        for a in range(adj_width):
            which = adj_ref[b, a]
            listed = jnp.maximum(which, 0)
            side = lax.rem(lax.div(listed, mesh_blocks) - me + 1 + parts, parts)
            side = jnp.where(side == 1, 2, jnp.where((side == 2) == (core == 0), 0, 1))
            place = side * mesh_blocks + lax.rem(listed, mesh_blocks)
            place = jnp.where(which >= 0, place, -columns)
            spot = jnp.where(col == place * block_mesh + row, 1.0, 0.0).astype(BF16)
            total += jnp.dot(coef_ref[b, a], spot, preferred_element_type=F32)
        all_ref[b * block_mesh : (b + 1) * block_mesh, :] = total.astype(BF16)
    near_ref[...] = all_ref[:, : 2 * count]
    part_ref[...] = jnp.dot(
        all_ref[:, 2 * count :], mid_ref[...], preferred_element_type=F32
    )


def prepare(parts, adj, coef, mid):
    mesh_blocks, adj_width, block_mesh, _ = coef.shape
    count = mesh_blocks * block_mesh
    vmem = pl.BlockSpec(memory_space=pltpu.VMEM)
    return pl.pallas_call(
        functools.partial(prepare_kernel, parts),
        in_specs=[pl.BlockSpec(memory_space=pltpu.SMEM), vmem, vmem],
        out_specs=[vmem] * 2,
        out_shape=[
            jax.ShapeDtypeStruct((count, 2 * count), BF16),
            jax.ShapeDtypeStruct(mid.shape, F32),
        ],
        scratch_shapes=[pltpu.VMEM((count, 3 * count), BF16)],
        compiler_params=pltpu.CompilerParams(vmem_limit_bytes=8 * MIB),
        cost_estimate=pl.CostEstimate(
            flops=2 * adj_width * count * block_mesh * 3 * count,
            bytes_accessed=8 * count * 3 * count,
            transcendentals=0,
        ),
        name="prepare",
    )(adj, coef, mid)


def update_kernel(*refs):
    slots = refs[:SLOTS]
    mesh_ref, w_ref, mid_ref, ids_ref = refs[SLOTS:]
    count, latent = mesh_ref.shape
    block_mesh = slots[0].shape[0]
    sums = [slot[:, :latent].astype(F32) for slot in slots]
    ids = [slot[:, latent:].astype(F32)[:1, :1] for slot in slots]
    for s in range(SLOTS):
        ids_ref[s : s + 1, :] = jnp.broadcast_to(ids[s], (1, latent))
    parts = []
    for b in range(count // block_mesh):
        total = jnp.zeros((block_mesh, latent), F32)
        for s in range(SLOTS):
            total += jnp.where(ids[s] == b, sums[s], 0.0)
        parts.append(total.astype(BF16))
    grown = jnp.dot(jnp.concatenate(parts, axis=0), w_ref[...], preferred_element_type=F32)
    mid_ref[...] = (mesh_ref[...].astype(F32) + silu(grown)).astype(BF16)


def update(slots, mesh_in, w_enc):
    vmem = pl.BlockSpec(memory_space=pltpu.VMEM)
    return pl.pallas_call(
        update_kernel,
        in_specs=[vmem] * (SLOTS + 2),
        out_specs=[vmem] * 2,
        out_shape=[
            jax.ShapeDtypeStruct(mesh_in.shape, BF16),
            jax.ShapeDtypeStruct((8, mesh_in.shape[1]), F32),
        ],
        compiler_params=pltpu.CompilerParams(vmem_limit_bytes=8 * MIB),
        name="mesh_update",
    )(*slots, mesh_in, w_enc)


def process_kernel(
    ids_ref, mid_ref, near_mid_ref, far_mid_ref, near_ref, part_ref, gain_ref, w_ref, out_ref, *sends
):
    count, latent = mid_ref.shape
    block_mesh = sends[0].shape[0]
    around = jnp.concatenate([near_mid_ref[...], far_mid_ref[...]], axis=0)
    message = part_ref[...] + jnp.dot(near_ref[...], around, preferred_element_type=F32)
    power = jnp.mean(message * message, axis=-1, keepdims=True)
    normed = (message * lax.rsqrt(power + 1e-05) * gain_ref[...]).astype(BF16)
    grown = jnp.dot(normed, w_ref[...], preferred_element_type=F32)
    grown = mid_ref[...].astype(F32) + silu(grown)
    out_ref[...] = grown.astype(BF16)
    for s in range(SLOTS):
        chosen = grown[:block_mesh, :]
        for b in range(1, count // block_mesh):
            block = grown[b * block_mesh : (b + 1) * block_mesh, :]
            chosen = jnp.where(ids_ref[s : s + 1, :] == b, block, chosen)
        sends[s][...] = chosen.astype(BF16)


def process(block_mesh, ids, mid, near_mid, far_mid, near, part, gain, w_proc):
    vmem = pl.BlockSpec(memory_space=pltpu.VMEM)
    latent = mid.shape[1]
    return pl.pallas_call(
        process_kernel,
        in_specs=[vmem] * 8,
        out_specs=[vmem] * (1 + SLOTS),
        out_shape=[jax.ShapeDtypeStruct(mid.shape, BF16)]
        + [jax.ShapeDtypeStruct((block_mesh, latent), BF16)] * SLOTS,
        compiler_params=pltpu.CompilerParams(vmem_limit_bytes=8 * MIB),
        name="mesh_process",
    )(ids, mid, near_mid, far_mid, near, part, gain, w_proc)


def decode_kernel(width, grid_ref, lat_ref, dsum_ref, w_ref, *rest):
    slots = rest[:SLOTS]
    out_hbm, back_ref, pred_ref, hold_ref, sems = rest[SLOTS:]
    steps = grid_ref.shape[1] // width

    def copy_out(step):
        cols = pl.ds(step * width, width)
        return pltpu.make_async_copy(pred_ref.at[:, cols], out_hbm.at[:, cols], sems.at[step])

    joined = jnp.concatenate([slot[...] for slot in slots], axis=0)
    back_ref[...] = (BF16(0.5) * joined).T

    def predict(step, slot):
        cols = pl.ds(step * width, width)
        pred_ref[:, cols] = (
            grid_ref[:, cols].astype(F32)
            + jnp.dot(w_ref[...], hold_ref[slot], preferred_element_type=F32)
        ).astype(BF16)

    for step in range(steps):
        slot = step % 2
        if step > 0:
            predict(step - 1, 1 - slot)
            copy_out(step - 1).start()
        for half in range(0, width, 256):
            part = pl.ds(step * width + half, 256)
            decoded = jnp.dot(back_ref[...], dsum_ref[:, part], preferred_element_type=F32)
            halved = BF16(0.5) * lat_ref[:, part] + decoded.astype(BF16)
            hold_ref[slot, :, half : half + 256] = silu_of_half(halved)
    predict(steps - 1, (steps - 1) % 2)
    copy_out(steps - 1).start()
    for step in range(steps):
        copy_out(step).wait()


def decode(grid_t, lat_t, dsum, w_out_t, slots):
    channels, points = grid_t.shape
    latent = lat_t.shape[0]
    rows = dsum.shape[0]
    width = 512
    vmem = pl.BlockSpec(memory_space=pltpu.VMEM)
    return pl.pallas_call(
        functools.partial(decode_kernel, width),
        in_specs=[vmem] * (4 + SLOTS),
        out_specs=pl.BlockSpec(memory_space=pl.ANY),
        out_shape=jax.ShapeDtypeStruct((channels, points), BF16),
        scratch_shapes=[
            pltpu.VMEM((latent, rows), BF16),
            pltpu.VMEM((channels, points), BF16),
            pltpu.VMEM((2, latent, width), BF16),
            pltpu.SemaphoreType.DMA((points // width,)),
        ],
        compiler_params=pltpu.CompilerParams(vmem_limit_bytes=24 * MIB),
        name="decode",
    )(grid_t, lat_t, dsum, w_out_t, *slots)


def local(
    grid_in, w_embed, enc_coef, enc_owner, slot_block, mesh_in, w_enc,
    proc_adj, proc_coef, proc_gain, w_proc, dec_coef, w_out,
):
    parts = lax.axis_size("nodes")
    block_mesh = enc_coef.shape[1]

    def swap(x, slot):
        pairs = [(i, partner(slot, i, parts)) for i in range(parts)]
        return lax.ppermute(x, "nodes", pairs)

    def swap_all(xs):
        return [xs[OWN]] + [swap(xs[s], s) for s in range(1, SLOTS)]

    lat_t, dsum, grid_t, *sums = encode(
        parts, slot_block, enc_owner.reshape(-1, 128), grid_in.T, w_embed, enc_coef,
        jnp.swapaxes(dec_coef, 1, 2),
    )
    received = swap_all(sums)
    mid, ids = update(received, mesh_in, w_enc)
    far_mid = swap(mid, FAR)
    near_mid = swap(mid, NEAR)
    near, part = prepare(parts, proc_adj, proc_coef, mid)
    mesh_out, *sends = process(
        block_mesh, ids, mid, near_mid, far_mid, near, part, proc_gain.reshape(1, -1), w_proc
    )
    returned = swap_all(sends)
    pred_t = decode(grid_t, lat_t, dsum, w_out.T, returned)
    return (pred_t.T, mesh_out)


def solution(mesh):
    return jax.shard_map(
        local,
        mesh=mesh,
        in_specs=(
            P(("groups", "nodes"), None),
            P(),
            P("nodes", None, None),
            P("nodes"),
            P("nodes"),
            P(("groups", "nodes"), None),
            P(),
            P("nodes", None),
            P("nodes", None, None, None),
            P(),
            P(),
            P("nodes", None, None),
            P(),
        ),
        out_specs=(P(("groups", "nodes"), None), P(("groups", "nodes"), None)),
        check_vma=False,
    )
```
